32 devices in a mesh: seg: 16 (over z, y, core), blk: 2 (over x).
Axes of the slice: x: 2, y: 2, z: 4, core: 2. Of those that a mesh axis runs over, the one named last changes fastest.
Arguments:
- state: bfloat16 [16, 4, 128, 2048], P('seg', 'blk'), may hold values from -6 to 6
- left_env: bfloat16 [16, 14, 4, 128, 128], P('seg', None, 'blk'), may hold values from -5 to 5
- right_env: bfloat16 [16, 14, 4, 128, 128], P('seg', None, 'blk'), may hold values from -3 to 3
- site_ops: bfloat16 [16, 14, 16, 16], P('seg'), may hold values from -4 to 4
- sector_map: int32 [16, 14, 4], P('seg'), may hold values from 0 to 3, as said below
- ranks: int32 [16, 4], P('seg', 'blk'), may hold values from 1 to 128
Outputs:
- new_state: bfloat16 [16, 4, 128, 2048], P('seg', 'blk')
- from_left: float32 [16, 14, 4, 128, 128], P('seg', None, 'blk')
- from_right: float32 [16, 14, 4, 128, 128], P('seg', None, 'blk')
The draws below stay inside these ranges and needn't reach their ends.
Inputs may be any that keep to these rules, and one draw needn't show every extreme that they name: `sector_map`: channel 0 carries every block into itself; the other channels' source blocks are arbitrary.
All inputs are finite; a program needn't handle non-finite values.
Results may differ from the reference program's by a relative error of at most 0.012.
Values may be sent and summed in bfloat16 or wider, within the bound.
No kernel may reach another device: no remote copies, remote signals or barrier semaphores. Data moves between devices by JAX's collectives and lax.ppermute only.
A program may use at most 192 MiB of HBM per device.

```python
import math
import jax
import jax.numpy as jnp
from jax import lax

BLK = 128
PHYS2 = 16
CHAN = 14
NB = 4
SEGS = 16


def draw_left_env(key, part):
    key = jax.random.fold_in(key, 11)
    jitter_key, scale_key = jax.random.split(key)
    array_shape = (SEGS, CHAN, NB, BLK, BLK)
    jitter = jnp.clip(jax.random.normal(jitter_key, array_shape, jnp.float32), -4.0, 4.0)
    factor = jnp.exp(jax.random.uniform(scale_key, (SEGS, NB), jnp.float32, math.log(0.6), 0.0))
    jitter = jitter / math.sqrt(BLK)
    position = jnp.arange(NB, dtype=jnp.float32) / max(NB - 1, 1)
    gain_rows = jnp.exp(math.log(3.0) * position)[None, :] * factor
    identity = jnp.eye(BLK, dtype=jnp.float32)
    channel_zero = gain_rows[:, :, None, None] * (identity[None, None] + 0.5 * jitter[:, 0])
    return jnp.concatenate([channel_zero[:, None], jitter[:, 1:]], axis=1).astype(jnp.bfloat16)


def draw_right_env(key, part):
    key = jax.random.fold_in(key, 12)
    jitter_key, scale_key = jax.random.split(key)
    array_shape = (SEGS, CHAN, NB, BLK, BLK)
    jitter = jnp.clip(jax.random.normal(jitter_key, array_shape, jnp.float32), -4.0, 4.0)
    factor = jnp.exp(jax.random.uniform(scale_key, (SEGS, NB), jnp.float32, math.log(0.7), math.log(1.4)))
    jitter = jitter / math.sqrt(BLK)
    identity = jnp.eye(BLK, dtype=jnp.float32)
    channel_zero = factor[:, :, None, None] * (identity[None, None] + 0.5 * jitter[:, 0])
    return jnp.concatenate([channel_zero[:, None], jitter[:, 1:]], axis=1).astype(jnp.bfloat16)


def draw_site_ops(key, part):
    key = jax.random.fold_in(key, 13)
    jitter_key, level_key, spread_key = jax.random.split(key, 3)
    array_shape = (SEGS, CHAN, PHYS2, PHYS2)
    jitter = jnp.clip(jax.random.normal(jitter_key, array_shape, jnp.float32), -4.0, 4.0)
    jitter = jitter / math.sqrt(PHYS2)
    level = jax.random.uniform(level_key, (SEGS,), jnp.float32, 1.0, 2.0)
    spread = jax.random.uniform(spread_key, (SEGS, PHYS2), jnp.float32, 0.0, 1.0)
    identity = jnp.eye(PHYS2, dtype=jnp.float32)
    diagonal = (level[:, None] + spread)[:, :, None] * identity[None]
    channel_zero = diagonal + 0.5 * jitter[:, 0]
    return jnp.concatenate([channel_zero[:, None], jitter[:, 1:]], axis=1).astype(jnp.bfloat16)


def draw_sector_map(key, part):
    key = jax.random.fold_in(key, 14)
    sources = jax.random.randint(key, (SEGS, CHAN, NB), 0, NB, dtype=jnp.int32)
    own_blocks = jnp.broadcast_to(jnp.arange(NB, dtype=jnp.int32)[None, None, :], (SEGS, 1, NB))
    return jnp.concatenate([own_blocks, sources[:, 1:]], axis=1)


def place_ends(entries, key, least, top_value):
    spot = [jax.random.randint(jax.random.fold_in(key, axis), (), 0, length) for axis, length in enumerate(entries.shape)]
    widest = entries.shape.index(max(entries.shape))
    next_to = spot[:widest] + [(spot[widest] + 1) % entries.shape[widest]] + spot[widest + 1:]
    return entries.at[tuple(spot)].set(least).at[tuple(next_to)].set(top_value)


def level_of(key, extent, shards, low, high):
    def one(dim, parts):
        heights = jax.random.uniform(jax.random.fold_in(jax.random.fold_in(key, 6), dim), (parts,), jnp.float32, low / len(shards), high / len(shards))
        return jnp.repeat(jnp.exp(heights), extent[dim] // parts).reshape((-1,) + (1,) * (len(extent) - dim - 1))

    factor_of = one(*shards[0])
    for cut in shards[1:]:
        factor_of = factor_of * one(*cut)
    return factor_of


def noise(stream_key, shape, width, limit, cuts=(), kind=jnp.bfloat16):
    gain = level_of(stream_key, shape, cuts, -0.22, 0.18) if cuts else 1.0
    array = jax.random.normal(stream_key, shape, jnp.float32) * width * gain
    return jnp.minimum(jnp.maximum(array, -limit), limit).astype(kind)


def setup_inputs(seed: int = 0) -> dict:
    arg_keys = jax.random.split(jax.random.key(seed), 7)
    return {
        "state": noise(arg_keys[0], (SEGS, NB, BLK, PHYS2 * BLK), 1.0, 6.0, ((0, 16), (1, 2))),
        "left_env": draw_left_env(jax.random.fold_in(arg_keys[6], 71), 0),
        "right_env": draw_right_env(jax.random.fold_in(arg_keys[6], 71), 0),
        "site_ops": draw_site_ops(jax.random.fold_in(arg_keys[6], 71), 0),
        "sector_map": draw_sector_map(jax.random.fold_in(arg_keys[6], 71), 0),
        "ranks": place_ends(jax.random.randint(arg_keys[5], (SEGS, NB), 1, BLK + 1), jax.random.fold_in(arg_keys[5], 1), 1, BLK).astype(jnp.int32),
    }


STEP_SIZE = 0.25
EPSILON = 1e-06

def apply_hamiltonian(vector, left_env, right_env, site_ops, sector_map):
    blocks = vector.reshape(NB, BLK, PHYS2, BLK)
    sources = blocks[sector_map.astype(jnp.int32)]
    mixed_ops = jnp.einsum('kpq,kbaqc->kbapc', site_ops.astype(jnp.float32), sources.astype(jnp.float32)).astype(jnp.bfloat16)
    left_part = jnp.einsum('kbxa,kbapc->kbxpc', left_env.astype(jnp.float32), mixed_ops.astype(jnp.float32)).astype(jnp.bfloat16)
    result = jnp.einsum('kbcd,kbapd->bapc', right_env.astype(jnp.float32), left_part.astype(jnp.float32))
    return result.reshape(NB, BLK, PHYS2 * BLK)

def segment_update(packed):
    state, left_env, right_env, site_ops, sector_map, ranks = packed
    image_rows = apply_hamiltonian(state, left_env, right_env, site_ops, sector_map)
    state_float = state.astype(jnp.float32)
    energy_one = jnp.sum(state_float * image_rows) / jnp.sum(state_float * state_float)
    first_step = (state_float - STEP_SIZE * (image_rows - energy_one * state_float)).astype(jnp.bfloat16)
    image_next = apply_hamiltonian(first_step, left_env, right_env, site_ops, sector_map)
    first_float = first_step.astype(jnp.float32)
    energy_two = jnp.sum(first_float * image_next) / jnp.sum(first_float * first_float)
    keep_mask = (jnp.arange(BLK, dtype=jnp.int32)[None, :] < ranks.astype(jnp.int32)[:, None]).astype(jnp.float32)[:, :, None]
    kept_part = keep_mask * (first_float - STEP_SIZE * (image_next - energy_two * first_float))
    norm_square = jnp.sum(kept_part * kept_part)
    total_cells = jnp.float32(NB * BLK * PHYS2 * BLK)
    new_state = (kept_part * jnp.sqrt(total_cells / (norm_square + EPSILON))).astype(jnp.bfloat16)
    state_four = new_state.reshape(NB, BLK, PHYS2, BLK).astype(jnp.float32)
    env_scale = 1.0 / math.sqrt(PHYS2 * BLK)
    left_mixed = jnp.einsum('kbxa,bapc->kbxpc', left_env.astype(jnp.float32), state_four).astype(jnp.bfloat16)
    left_new = jnp.einsum('bxpc,kbxpd->kbcd', state_four, left_mixed.astype(jnp.float32)) * env_scale
    right_mixed = jnp.einsum('kbcd,bapd->kbapc', right_env.astype(jnp.float32), state_four).astype(jnp.bfloat16)
    right_new = jnp.einsum('bapc,kbxpc->kbax', state_four, right_mixed.astype(jnp.float32)) * env_scale
    return (new_state, left_new, right_new)

def reference(state, left_env, right_env, site_ops, sector_map, ranks):
    new_state, left_new, right_new = lax.map(segment_update, (state, left_env, right_env, site_ops, sector_map, ranks))
    from_left = jnp.concatenate([jnp.zeros_like(left_new[:1]), left_new[:-1]], axis=0)
    from_right = jnp.concatenate([right_new[1:], jnp.zeros_like(right_new[:1])], axis=0)
    return (new_state, from_left, from_right)
```

```python
import functools
import math

import jax
import jax.numpy as jnp
from jax import lax
from jax.experimental import pallas as pl
from jax.experimental.pallas import tpu as pltpu
from jax.sharding import PartitionSpec as P

STEP_SIZE = 0.25
EPSILON = 1e-06
LANES = 128
ROWS = 16
F32 = jnp.float32
BF16 = jnp.bfloat16
VMEM = pl.BlockSpec(memory_space=pltpu.VMEM)
SMEM = pl.BlockSpec(memory_space=pltpu.SMEM)
PARAMS = pltpu.CompilerParams(vmem_limit_bytes=32 * 1024 * 1024)


def dot(left, right):
    return lax.dot_general(
        left, right, (((1,), (0,)), ((), ())), preferred_element_type=F32
    )


def make_kron(ops_ref, kron_ref):
    chan, phys, _ = ops_ref.shape
    wide = phys * ROWS
    spread_rows = (
        lax.broadcasted_iota(jnp.int32, (wide, phys), 0) // ROWS
        == lax.broadcasted_iota(jnp.int32, (wide, phys), 1)
    ).astype(F32).astype(BF16)
    spread_cols = (
        lax.broadcasted_iota(jnp.int32, (phys, wide), 1) // ROWS
        == lax.broadcasted_iota(jnp.int32, (phys, wide), 0)
    ).astype(F32).astype(BF16)
    diagonal = (
        lax.broadcasted_iota(jnp.int32, (wide, wide), 0) % ROWS
        == lax.broadcasted_iota(jnp.int32, (wide, wide), 1) % ROWS
    )

    def one(k, carry):
        tall = dot(spread_rows, ops_ref[k]).astype(BF16)
        full = dot(tall, spread_cols)
        kron_ref[k] = jnp.where(diagonal, full, 0.0).astype(BF16)
        return carry

    lax.fori_loop(0, chan, one, 0)


def list_pairs(rel_ref, low, high, chan_list, src_list, live_list, dest_list):
    chan, dests = rel_ref.shape
    place = jnp.int32(0)
    for b in range(dests):
        for k in range(chan):
            source = rel_ref[k, b]
            chan_list[place] = k
            src_list[place] = source - low
            live_list[place] = 1
            dest_list[place] = b
            place = place + jnp.where((source >= low) & (source < high), 1, 0)
        chan_list[place] = 0
        src_list[place] = 0
        live_list[place] = 0
        dest_list[place] = b
        place = place + lax.rem(place, 2)
    return place // 2


def add_pairs(steps, lists, kron_ref, x_ref, left_ref, right_t_ref, acc_ref, mixed_ref, part_ref):
    chan_list, src_list, live_list, dest_list = lists
    rows = x_ref.shape[1]
    phys = x_ref.shape[2] // LANES

    def step(s, carry):
        dest = dest_list[2 * s]
        weights = []
        for i in range(2):
            k = chan_list[2 * s + i]
            source = src_list[2 * s + i]
            kron = kron_ref[k]
            for g in range(rows // (2 * ROWS)):
                halves = []
                for j in range(2):
                    r0 = (2 * g + j) * ROWS
                    halves.append(
                        jnp.concatenate(
                            [
                                x_ref[source, r0 : r0 + ROWS, q * LANES : (q + 1) * LANES]
                                for q in range(phys)
                            ],
                            axis=0,
                        )
                    )
                out = dot(kron, jnp.concatenate(halves, axis=1)).astype(BF16)
                for j in range(2):
                    r0 = (2 * g + j) * ROWS
                    for p in range(phys):
                        mixed_ref[i, r0 : r0 + ROWS, p * LANES : (p + 1) * LANES] = out[
                            p * ROWS : (p + 1) * ROWS, j * LANES : (j + 1) * LANES
                        ]
            left = left_ref[k, dest]
            for c in range(phys // 2):
                cols = slice(c * 2 * LANES, (c + 1) * 2 * LANES)
                part_ref[i, :, cols] = dot(left, mixed_ref[i, :, cols]).astype(BF16)
            right = right_t_ref[k, dest]
            if i == 1:
                right = jnp.where(live_list[2 * s + 1] > 0, right, jnp.zeros_like(right))
            weights.append(right)
        both = jnp.concatenate(weights, axis=0)
        for p in range(phys):
            cols = slice(p * LANES, (p + 1) * LANES)
            pair = jnp.concatenate([part_ref[0, :, cols], part_ref[1, :, cols]], axis=1)
            acc_ref[dest, :, cols] += dot(pair, both)
        return carry

    lax.fori_loop(0, steps, step, 0)


def fold(values):
    total = values[:, :LANES]
    for p in range(1, values.shape[1] // LANES):
        total = total + values[:, p * LANES : (p + 1) * LANES]
    return total


def row_loop(blocks, rows, body, count):
    zeros = tuple(jnp.zeros((ROWS, LANES), F32) for _ in range(count))
    per = rows // ROWS

    def step(n, carry):
        return body(n // per, pl.ds(pl.multiple_of(lax.rem(n, per) * ROWS, ROWS), ROWS), carry)

    return lax.fori_loop(0, blocks * per, step, zeros)


def put_sums(out_ref, values):
    for n, value in enumerate(values):
        out_ref[n : n + 1, :] = jnp.full((1, LANES), 1.0, F32) * value


def quotient(num, den):
    return jnp.where(den > 0, num / jnp.where(den > 0, den, 1.0), 0.0)


def first_local(
    rel_ref, ops_ref, x_ref, left_ref, right_ref,
    kron_ref, right_t_ref, image_ref, sums_ref,
    mixed_ref, part_ref, chan_list, src_list, live_list, dest_list,
):
    lists = (chan_list, src_list, live_list, dest_list)
    make_kron(ops_ref, kron_ref)
    chan, dests = left_ref.shape[:2]

    def turn(n, carry):
        k, b = n // dests, lax.rem(n, dests)
        right_t_ref[k, b] = right_ref[k, b].astype(F32).T.astype(BF16)
        return carry

    lax.fori_loop(0, chan * dests, turn, 0)
    image_ref[...] = jnp.zeros_like(image_ref)
    steps = list_pairs(rel_ref, 0, dests, *lists)
    add_pairs(steps, lists, kron_ref, x_ref, left_ref, right_t_ref, image_ref, mixed_ref, part_ref)

    def sums(b, r, carry):
        x = x_ref[b, r, :].astype(F32)
        return carry[0] + fold(x * image_ref[b, r, :]), carry[1] + fold(x * x)

    num, den = row_loop(dests, x_ref.shape[1], sums, 2)
    put_sums(sums_ref, (jnp.sum(num), jnp.sum(den)))


def first_remote(
    rel_ref, kron_ref, other_ref, left_ref, right_t_ref,
    acc_ref,
    mixed_ref, part_ref, chan_list, src_list, live_list, dest_list,
):
    lists = (chan_list, src_list, live_list, dest_list)
    dests = left_ref.shape[1]
    acc_ref[...] = jnp.zeros_like(acc_ref)
    steps = list_pairs(rel_ref, dests, dests + 1, *lists)
    add_pairs(steps, lists, kron_ref, other_ref, left_ref, right_t_ref, acc_ref, mixed_ref, part_ref)


def first_finish(
    rel_ref, kron_ref, other_ref, left_ref, right_t_ref, before_ref, x_ref, image_ref, sums_ref,
    acc_ref, guess_ref, out_sums_ref,
    mixed_ref, part_ref, chan_list, src_list, live_list, dest_list,
):
    lists = (chan_list, src_list, live_list, dest_list)
    dests = left_ref.shape[1]
    acc_ref[...] = before_ref[...]
    steps = list_pairs(rel_ref, dests + 1, 2 * dests, *lists)
    add_pairs(steps, lists, kron_ref, other_ref, left_ref, right_t_ref, acc_ref, mixed_ref, part_ref)
    num_local, den = sums_ref[0:1, :], sums_ref[1:2, :]
    shift = quotient(num_local, den)
    keep_state = jnp.tile(1.0 + STEP_SIZE * shift, (1, x_ref.shape[2] // LANES))

    def sums(b, r, carry):
        x = x_ref[b, r, :].astype(F32)
        remote = acc_ref[b, r, :]
        guess_ref[b, r, :] = (keep_state * x - STEP_SIZE * (image_ref[b, r, :] + remote)).astype(BF16)
        return (carry[0] + fold(x * remote),)

    (num,) = row_loop(dests, x_ref.shape[1], sums, 1)
    out_sums_ref[0:1, :] = num_local + jnp.sum(num)
    out_sums_ref[1:2, :] = den
    out_sums_ref[2:3, :] = shift
    out_sums_ref[3:8, :] = jnp.zeros((5, LANES), F32)


def second_local(
    rel_ref, kron_ref, guess_ref, left_ref, right_t_ref,
    acc_ref,
    mixed_ref, part_ref, chan_list, src_list, live_list, dest_list,
):
    lists = (chan_list, src_list, live_list, dest_list)
    dests = left_ref.shape[1]
    acc_ref[...] = jnp.zeros_like(acc_ref)
    steps = list_pairs(rel_ref, 0, dests, *lists)
    add_pairs(steps, lists, kron_ref, guess_ref, left_ref, right_t_ref, acc_ref, mixed_ref, part_ref)


def second_remote(
    rel_ref, kron_ref, other_ref, left_ref, right_t_ref, before_ref, x_ref, image_ref, remote_ref,
    mine_ref, theirs_ref,
    acc_ref, first_ref,
    mixed_ref, part_ref, chan_list, src_list, live_list, dest_list,
):
    lists = (chan_list, src_list, live_list, dest_list)
    dests = left_ref.shape[1]
    energy = (mine_ref[0:1, :] + theirs_ref[0:1, :]) / (mine_ref[1:2, :] + theirs_ref[1:2, :])
    times = x_ref.shape[2] // LANES
    wide = functools.partial(jnp.tile, reps=(1, times))
    keep_state = wide(1.0 + STEP_SIZE * energy)
    scale_local = wide(STEP_SIZE * (energy - mine_ref[2:3, :]))
    scale_remote = wide(STEP_SIZE * (energy - theirs_ref[2:3, :]))

    def prepare(b, r, carry):
        local, remote = image_ref[b, r, :], remote_ref[b, r, :]
        x = x_ref[b, r, :].astype(F32)
        first_ref[b, r, :] = (keep_state * x - STEP_SIZE * (local + remote)).astype(BF16)
        acc_ref[b, r, :] = before_ref[b, r, :] + (scale_local * local + scale_remote * remote)
        return carry

    row_loop(dests, x_ref.shape[1], prepare, 0)
    steps = list_pairs(rel_ref, dests, dests + 1, *lists)
    add_pairs(steps, lists, kron_ref, other_ref, left_ref, right_t_ref, acc_ref, mixed_ref, part_ref)


def second_finish(
    rel_ref, rank_ref, kron_ref, other_ref, left_ref, right_t_ref, before_ref, first_ref,
    mine_ref, theirs_ref,
    kept_ref, kept_first_ref, out_sums_ref,
    acc_ref, mixed_ref, part_ref, chan_list, src_list, live_list, dest_list,
):
    lists = (chan_list, src_list, live_list, dest_list)
    dests = left_ref.shape[1]
    acc_ref[...] = before_ref[...]
    steps = list_pairs(rel_ref, dests + 1, 2 * dests, *lists)
    add_pairs(steps, lists, kron_ref, other_ref, left_ref, right_t_ref, acc_ref, mixed_ref, part_ref)
    energy = (mine_ref[0:1, :] + theirs_ref[0:1, :]) / (mine_ref[1:2, :] + theirs_ref[1:2, :])
    width = first_ref.shape[2]
    keep_first = jnp.tile(1.0 + STEP_SIZE * energy, (1, width // LANES))

    def sums(b, r, carry):
        first = first_ref[b, r, :].astype(F32)
        image = acc_ref[b, r, :]
        row = r.start + lax.broadcasted_iota(jnp.int32, (ROWS, width), 0)
        mask = row < rank_ref[b]
        kept = jnp.where(mask, keep_first * first - STEP_SIZE * image, 0.0)
        kept_first = jnp.where(mask, first, 0.0)
        kept_ref[b, r, :] = kept
        kept_first_ref[b, r, :] = kept_first.astype(BF16)
        return (
            carry[0] + fold(first * image),
            carry[1] + fold(first * first),
            carry[2] + fold(kept * kept),
            carry[3] + fold(kept * first),
            carry[4] + fold(kept_first * first),
        )

    totals = row_loop(dests, first_ref.shape[1], sums, 5)
    for n, total in enumerate(totals):
        out_sums_ref[n : n + 1, :] = jnp.full((1, LANES), 1.0, F32) * jnp.sum(total)
    out_sums_ref[5:6, :] = energy
    out_sums_ref[6:8, :] = jnp.zeros((2, LANES), F32)


def normalize(
    cells, kept_ref, first_ref, mine_ref, theirs_ref, state_ref, turned_ref,
):
    both = mine_ref[...] + theirs_ref[...]
    shift = STEP_SIZE * (both[0:1] / both[1:2] - mine_ref[5:6, :])
    norm = jnp.maximum(both[2:3] + shift * (2.0 * both[3:4] + shift * both[4:5]), 0.0)
    gain = jnp.sqrt(cells / (norm + EPSILON))
    times = kept_ref.shape[2] // LANES
    gain, shift = jnp.tile(gain, (1, times)), jnp.tile(shift, (1, times))

    def one(b, r, carry):
        state_ref[b, r, :] = (
            (kept_ref[b, r, :] + shift * first_ref[b, r, :].astype(F32)) * gain
        ).astype(BF16)
        return carry

    blocks, rows, _ = kept_ref.shape
    row_loop(blocks, rows, one, 0)

    def turn(n, carry):
        b, p = n // times, lax.rem(n, times)
        cols = pl.ds(pl.multiple_of(p * LANES, LANES), LANES)
        turned_ref[b, :, cols] = state_ref[b, :, cols].astype(F32).T.astype(BF16)
        return carry

    lax.fori_loop(0, blocks * times, turn, 0)


def environments(first, count, scale, env_ref, inner_ref, outer_ref, out_ref, mid_ref):
    dests = env_ref.shape[1]
    phys = inner_ref.shape[2] // LANES

    def step(n, carry):
        pair, b = n // dests, lax.rem(n, dests)
        k = first + 2 * pair
        env = jnp.concatenate([env_ref[k, b], env_ref[k + 1, b]], axis=0)
        for c in range(phys // 2):
            cols = slice(c * 2 * LANES, (c + 1) * 2 * LANES)
            mid = dot(env, inner_ref[b, :, cols]).astype(BF16)
            for h in range(2):
                p = 2 * c + h
                for i in range(2):
                    mid_ref[p * LANES : (p + 1) * LANES, i * LANES : (i + 1) * LANES] = mid[
                        i * LANES : (i + 1) * LANES, h * LANES : (h + 1) * LANES
                    ]
        out = (dot(outer_ref[b], mid_ref[...]) * scale).astype(BF16)
        out_ref[2 * pair, b] = out[:, :LANES]
        out_ref[2 * pair + 1, b] = out[:, LANES:]
        return carry

    lax.fori_loop(0, (count // 2) * dests, step, 0)


def normalize_and_left(
    first, count, scale, cells,
    kept_ref, first_ref, mine_ref, theirs_ref, env_ref,
    state_ref, turned_ref, out_ref,
    mid_ref,
):
    normalize(cells, kept_ref, first_ref, mine_ref, theirs_ref, state_ref, turned_ref)
    environments(first, count, scale, env_ref, state_ref, turned_ref, out_ref, mid_ref)


def shards(state, left_env, right_env, site_ops, sector_map, ranks):
    dests, rows, width = state.shape[1:]
    chan, phys = site_ops.shape[1:3]
    groups = lax.axis_size("blk")
    total_blocks = groups * dests
    first_block = lax.axis_index("blk") * dests
    x, left, right, ops = state[0], left_env[0], right_env[0], site_ops[0]
    local_map = lax.dynamic_slice_in_dim(sector_map[0], first_block, dests, 1)
    rel = lax.rem(local_map - first_block + total_blocks, total_blocks)

    swap = [(g, groups - 1 - g) for g in range(groups)]

    def trade(value):
        return lax.ppermute(value, "blk", swap)

    def shape(dims, kind):
        return jax.ShapeDtypeStruct(dims, kind)

    wave = (dests, rows, width)
    wave_f32 = shape(wave, F32)
    wave_b16 = shape(wave, BF16)
    sums_kind = shape((8, LANES), F32)
    lists = [pltpu.SMEM((chan * dests + 2 * dests + 1,), jnp.int32)] * 4
    pair_scratch = [pltpu.VMEM((2, rows, width), BF16)] * 2 + lists
    one_apply = 2 * chan * dests * rows * width * (ROWS * phys + 2 * rows)

    def call(body, specs, outs, scratch, share, *args):
        return pl.pallas_call(
            body,
            in_specs=specs,
            out_specs=jax.tree.map(lambda _: VMEM, outs),
            out_shape=outs,
            scratch_shapes=scratch,
            compiler_params=PARAMS,
            cost_estimate=pl.CostEstimate(
                flops=int(one_apply * share), bytes_accessed=8 * 1024 * 1024, transcendentals=0
            ),
        )(*args)

    other = [trade(x[b : b + 1]) for b in range(dests)]
    kron, right_t, image_local, sums_local = call(
        first_local, [SMEM] + [VMEM] * 4,
        (shape((chan, phys * ROWS, phys * ROWS), BF16), shape(right.shape, BF16), wave_f32, sums_kind),
        pair_scratch, 0.7, rel, ops, x, left, right,
    )
    image_remote = call(
        first_remote, [SMEM] + [VMEM] * 4, wave_f32, pair_scratch, 0.25,
        rel, kron, other[0], left, right_t,
    )
    image_remote, guess, mine = call(
        first_finish, [SMEM] + [VMEM] * 8, (wave_f32, wave_b16, sums_kind), pair_scratch, 0.3,
        rel, kron, other[1], left, right_t, image_remote, x, image_local, sums_local,
    )
    theirs = trade(mine)
    other = [trade(guess[b : b + 1]) for b in range(dests)]
    acc = call(
        second_local, [SMEM] + [VMEM] * 4, wave_f32, pair_scratch, 0.5,
        rel, kron, guess, left, right_t,
    )
    acc, first = call(
        second_remote, [SMEM] + [VMEM] * 10, (wave_f32, wave_b16), pair_scratch, 0.25,
        rel, kron, other[0], left, right_t, acc, x, image_local, image_remote, mine, theirs,
    )
    kept, kept_first, sums_mine = call(
        second_finish, [SMEM, SMEM] + [VMEM] * 8, (wave_f32, wave_b16, sums_kind),
        [pltpu.VMEM(wave, F32)] + pair_scratch, 0.3,
        rel, ranks[0], kron, other[1], left, right_t, acc, first, mine, theirs,
    )
    sums_theirs = trade(sums_mine)

    env_scale = 1.0 / math.sqrt(phys * rows)
    cells = float(total_blocks * rows * width)
    half = chan // 4 * 2
    cuts = [(0, half), (half, chan - half)]
    mid = [pltpu.VMEM((width, 2 * LANES), BF16)]

    def sent(value, steps):
        count = lax.axis_size("seg")
        begin, end = max(0, -steps), min(count, count - steps)
        return lax.ppermute(value, "seg", [(s, s + steps) for s in range(begin, end)])

    def env_kind(count):
        return shape((count,) + left.shape[1:], BF16)

    lefts, rights = [], []
    for n, (begin, count) in enumerate(cuts):
        if n == 0:
            new_state, turned, piece = call(
                functools.partial(normalize_and_left, begin, count, env_scale, cells),
                [VMEM] * 5, (wave_b16, wave_b16, env_kind(count)), mid, 0.3,
                kept, kept_first, sums_mine, sums_theirs, left,
            )
        else:
            piece = call(
                functools.partial(environments, begin, count, env_scale),
                [VMEM] * 3, env_kind(count), mid, 0.3, left, new_state, turned,
            )
        lefts.append(sent(piece, 1))
        piece = call(
            functools.partial(environments, begin, count, env_scale),
            [VMEM] * 3, env_kind(count), mid, 0.3, right, turned, new_state,
        )
        rights.append(sent(piece, -1))
    received_left = jnp.concatenate(lefts, axis=0).astype(F32)
    received_right = jnp.concatenate(rights, axis=0).astype(F32)
    return (new_state[None], received_left[None], received_right[None])


def solution(mesh):
    placed = (
        P("seg", "blk", None, None),
        P("seg", None, "blk", None, None),
        P("seg", None, "blk", None, None),
        P("seg", None, None, None),
        P("seg", None, None),
        P("seg", "blk"),
    )
    return jax.shard_map(
        shards,
        mesh=mesh,
        in_specs=placed,
        out_specs=(
            P("seg", "blk", None, None),
            P("seg", None, "blk", None, None),
            P("seg", None, "blk", None, None),
        ),
        check_vma=False,
    )
```

```python
import functools
import math

import jax
import jax.numpy as jnp
from jax import lax
from jax.experimental import pallas as pl
from jax.experimental.pallas import tpu as pltpu
from jax.sharding import PartitionSpec as P

STEP_SIZE = 0.25
EPSILON = 1e-06
LANES = 128
ROWS = 16
F32 = jnp.float32
BF16 = jnp.bfloat16
VMEM = pl.BlockSpec(memory_space=pltpu.VMEM)
SMEM = pl.BlockSpec(memory_space=pltpu.SMEM)
COST = pl.CostEstimate(flops=1024, bytes_accessed=1024, transcendentals=0)
PARAMS = pltpu.CompilerParams(vmem_limit_bytes=32 * 1024 * 1024)


def dot(left, right):
    return lax.dot_general(
        left, right, (((1,), (0,)), ((), ())), preferred_element_type=F32
    )


def make_kron(ops_ref, kron_ref):
    chan, phys, _ = ops_ref.shape
    wide = phys * ROWS
    spread_rows = (
        lax.broadcasted_iota(jnp.int32, (wide, phys), 0) // ROWS
        == lax.broadcasted_iota(jnp.int32, (wide, phys), 1)
    ).astype(F32).astype(BF16)
    spread_cols = (
        lax.broadcasted_iota(jnp.int32, (phys, wide), 1) // ROWS
        == lax.broadcasted_iota(jnp.int32, (phys, wide), 0)
    ).astype(F32).astype(BF16)
    diagonal = (
        lax.broadcasted_iota(jnp.int32, (wide, wide), 0) % ROWS
        == lax.broadcasted_iota(jnp.int32, (wide, wide), 1) % ROWS
    )

    def one(k, carry):
        tall = dot(spread_rows, ops_ref[k]).astype(BF16)
        full = dot(tall, spread_cols)
        kron_ref[k] = jnp.where(diagonal, full, 0.0).astype(BF16)
        return carry

    lax.fori_loop(0, chan, one, 0)


def list_pairs(rel_ref, low, high, chan_list, src_list, live_list, dest_list):
    chan, dests = rel_ref.shape
    place = jnp.int32(0)
    for b in range(dests):
        for k in range(chan):
            source = rel_ref[k, b]
            chan_list[place] = k
            src_list[place] = source - low
            live_list[place] = 1
            dest_list[place] = b
            place = place + jnp.where((source >= low) & (source < high), 1, 0)
        chan_list[place] = 0
        src_list[place] = 0
        live_list[place] = 0
        dest_list[place] = b
        place = place + lax.rem(place, 2)
    return place // 2


def add_pairs(steps, lists, kron_ref, x_ref, left_ref, right_t_ref, acc_ref, mixed_ref, part_ref):
    chan_list, src_list, live_list, dest_list = lists
    rows = x_ref.shape[1]
    phys = x_ref.shape[2] // LANES

    def step(s, carry):
        dest = dest_list[2 * s]
        weights = []
        for i in range(2):
            k = chan_list[2 * s + i]
            source = src_list[2 * s + i]
            kron = kron_ref[k]
            for g in range(rows // (2 * ROWS)):
                halves = []
                for j in range(2):
                    r0 = (2 * g + j) * ROWS
                    halves.append(
                        jnp.concatenate(
                            [
                                x_ref[source, r0 : r0 + ROWS, q * LANES : (q + 1) * LANES]
                                for q in range(phys)
                            ],
                            axis=0,
                        )
                    )
                out = dot(kron, jnp.concatenate(halves, axis=1)).astype(BF16)
                for j in range(2):
                    r0 = (2 * g + j) * ROWS
                    for p in range(phys):
                        mixed_ref[i, r0 : r0 + ROWS, p * LANES : (p + 1) * LANES] = out[
                            p * ROWS : (p + 1) * ROWS, j * LANES : (j + 1) * LANES
                        ]
            left = left_ref[k, dest]
            part = dot(left, mixed_ref[i]).astype(BF16)
            for p in range(phys):
                part_ref[p * rows : (p + 1) * rows, i * LANES : (i + 1) * LANES] = part[
                    :, p * LANES : (p + 1) * LANES
                ]
            right = right_t_ref[k, dest]
            if i == 1:
                right = jnp.where(live_list[2 * s + 1] > 0, right, jnp.zeros_like(right))
            weights.append(right)
        image = dot(part_ref[...], jnp.concatenate(weights, axis=0))
        for p in range(phys):
            acc_ref[dest, :, p * LANES : (p + 1) * LANES] += image[p * rows : (p + 1) * rows]
        return carry

    lax.fori_loop(0, steps, step, 0)


def fold(values):
    total = values[:, :LANES]
    for p in range(1, values.shape[1] // LANES):
        total = total + values[:, p * LANES : (p + 1) * LANES]
    return total


def row_loop(blocks, rows, body, count):
    zeros = tuple(jnp.zeros((ROWS, LANES), F32) for _ in range(count))
    per = rows // ROWS

    def step(n, carry):
        return body(n // per, pl.ds(pl.multiple_of(lax.rem(n, per) * ROWS, ROWS), ROWS), carry)

    return lax.fori_loop(0, blocks * per, step, zeros)


def put_sums(out_ref, values):
    for n, value in enumerate(values):
        out_ref[n : n + 1, :] = jnp.full((1, LANES), 1.0, F32) * value


def quotient(num, den):
    return jnp.where(den > 0, num / jnp.where(den > 0, den, 1.0), 0.0)


def first_local(
    rel_ref, ops_ref, x_ref, left_ref, right_ref,
    kron_ref, right_t_ref, image_ref, sums_ref,
    mixed_ref, part_ref, chan_list, src_list, live_list, dest_list,
):
    lists = (chan_list, src_list, live_list, dest_list)
    make_kron(ops_ref, kron_ref)
    chan, dests = left_ref.shape[:2]

    def turn(n, carry):
        k, b = n // dests, lax.rem(n, dests)
        right_t_ref[k, b] = right_ref[k, b].T
        return carry

    lax.fori_loop(0, chan * dests, turn, 0)
    image_ref[...] = jnp.zeros_like(image_ref)
    steps = list_pairs(rel_ref, 0, dests, *lists)
    add_pairs(steps, lists, kron_ref, x_ref, left_ref, right_t_ref, image_ref, mixed_ref, part_ref)

    def sums(b, r, carry):
        x = x_ref[b, r, :].astype(F32)
        return carry[0] + fold(x * image_ref[b, r, :]), carry[1] + fold(x * x)

    num, den = row_loop(dests, x_ref.shape[1], sums, 2)
    put_sums(sums_ref, (jnp.sum(num), jnp.sum(den)))


def first_remote(
    rel_ref, kron_ref, other_ref, left_ref, right_t_ref,
    acc_ref,
    mixed_ref, part_ref, chan_list, src_list, live_list, dest_list,
):
    lists = (chan_list, src_list, live_list, dest_list)
    dests = left_ref.shape[1]
    acc_ref[...] = jnp.zeros_like(acc_ref)
    steps = list_pairs(rel_ref, dests, dests + 1, *lists)
    add_pairs(steps, lists, kron_ref, other_ref, left_ref, right_t_ref, acc_ref, mixed_ref, part_ref)


def first_finish(
    rel_ref, kron_ref, other_ref, left_ref, right_t_ref, before_ref, x_ref, image_ref, sums_ref,
    acc_ref, guess_ref, out_sums_ref,
    mixed_ref, part_ref, chan_list, src_list, live_list, dest_list,
):
    lists = (chan_list, src_list, live_list, dest_list)
    dests = left_ref.shape[1]
    acc_ref[...] = before_ref[...]
    steps = list_pairs(rel_ref, dests + 1, 2 * dests, *lists)
    add_pairs(steps, lists, kron_ref, other_ref, left_ref, right_t_ref, acc_ref, mixed_ref, part_ref)
    num_local, den = sums_ref[0:1, :], sums_ref[1:2, :]
    shift = quotient(num_local, den)
    keep_state = jnp.tile(1.0 + STEP_SIZE * shift, (1, x_ref.shape[2] // LANES))

    def sums(b, r, carry):
        x = x_ref[b, r, :].astype(F32)
        remote = acc_ref[b, r, :]
        guess_ref[b, r, :] = (keep_state * x - STEP_SIZE * (image_ref[b, r, :] + remote)).astype(BF16)
        return (carry[0] + fold(x * remote),)

    (num,) = row_loop(dests, x_ref.shape[1], sums, 1)
    out_sums_ref[0:1, :] = num_local + jnp.sum(num)
    out_sums_ref[1:2, :] = den
    out_sums_ref[2:3, :] = shift
    out_sums_ref[3:8, :] = jnp.zeros((5, LANES), F32)


def second_local(
    rel_ref, kron_ref, guess_ref, left_ref, right_t_ref,
    acc_ref,
    mixed_ref, part_ref, chan_list, src_list, live_list, dest_list,
):
    lists = (chan_list, src_list, live_list, dest_list)
    dests = left_ref.shape[1]
    acc_ref[...] = jnp.zeros_like(acc_ref)
    steps = list_pairs(rel_ref, 0, dests, *lists)
    add_pairs(steps, lists, kron_ref, guess_ref, left_ref, right_t_ref, acc_ref, mixed_ref, part_ref)


def second_remote(
    rel_ref, kron_ref, other_ref, left_ref, right_t_ref, before_ref, x_ref, image_ref, remote_ref,
    mine_ref, theirs_ref,
    acc_ref, first_ref,
    mixed_ref, part_ref, chan_list, src_list, live_list, dest_list,
):
    lists = (chan_list, src_list, live_list, dest_list)
    dests = left_ref.shape[1]
    energy = (mine_ref[0:1, :] + theirs_ref[0:1, :]) / (mine_ref[1:2, :] + theirs_ref[1:2, :])
    times = x_ref.shape[2] // LANES
    wide = functools.partial(jnp.tile, reps=(1, times))
    keep_state = wide(1.0 + STEP_SIZE * energy)
    scale_local = wide(STEP_SIZE * (energy - mine_ref[2:3, :]))
    scale_remote = wide(STEP_SIZE * (energy - theirs_ref[2:3, :]))

    def prepare(b, r, carry):
        local, remote = image_ref[b, r, :], remote_ref[b, r, :]
        x = x_ref[b, r, :].astype(F32)
        first_ref[b, r, :] = (keep_state * x - STEP_SIZE * (local + remote)).astype(BF16)
        acc_ref[b, r, :] = before_ref[b, r, :] + (scale_local * local + scale_remote * remote)
        return carry

    row_loop(dests, x_ref.shape[1], prepare, 0)
    steps = list_pairs(rel_ref, dests, dests + 1, *lists)
    add_pairs(steps, lists, kron_ref, other_ref, left_ref, right_t_ref, acc_ref, mixed_ref, part_ref)


def second_finish(
    rel_ref, rank_ref, kron_ref, other_ref, left_ref, right_t_ref, before_ref, first_ref,
    mine_ref, theirs_ref,
    kept_ref, kept_first_ref, out_sums_ref,
    acc_ref, mixed_ref, part_ref, chan_list, src_list, live_list, dest_list,
):
    lists = (chan_list, src_list, live_list, dest_list)
    dests = left_ref.shape[1]
    acc_ref[...] = before_ref[...]
    steps = list_pairs(rel_ref, dests + 1, 2 * dests, *lists)
    add_pairs(steps, lists, kron_ref, other_ref, left_ref, right_t_ref, acc_ref, mixed_ref, part_ref)
    energy = (mine_ref[0:1, :] + theirs_ref[0:1, :]) / (mine_ref[1:2, :] + theirs_ref[1:2, :])
    width = first_ref.shape[2]
    keep_first = jnp.tile(1.0 + STEP_SIZE * energy, (1, width // LANES))

    def sums(b, r, carry):
        first = first_ref[b, r, :].astype(F32)
        image = acc_ref[b, r, :]
        row = r.start + lax.broadcasted_iota(jnp.int32, (ROWS, width), 0)
        mask = row < rank_ref[b]
        kept = jnp.where(mask, keep_first * first - STEP_SIZE * image, 0.0)
        kept_first = jnp.where(mask, first, 0.0)
        kept_ref[b, r, :] = kept
        kept_first_ref[b, r, :] = kept_first.astype(BF16)
        return (
            carry[0] + fold(first * image),
            carry[1] + fold(first * first),
            carry[2] + fold(kept * kept),
            carry[3] + fold(kept * first),
            carry[4] + fold(kept_first * first),
        )

    totals = row_loop(dests, first_ref.shape[1], sums, 5)
    for n, total in enumerate(totals):
        out_sums_ref[n : n + 1, :] = jnp.full((1, LANES), 1.0, F32) * jnp.sum(total)
    out_sums_ref[5:6, :] = energy
    out_sums_ref[6:8, :] = jnp.zeros((2, LANES), F32)


def normalize(
    cells, kept_ref, first_ref, mine_ref, theirs_ref, state_ref, turned_ref,
):
    both = mine_ref[...] + theirs_ref[...]
    shift = STEP_SIZE * (both[0:1] / both[1:2] - mine_ref[5:6, :])
    norm = jnp.maximum(both[2:3] + shift * (2.0 * both[3:4] + shift * both[4:5]), 0.0)
    gain = jnp.sqrt(cells / (norm + EPSILON))
    times = kept_ref.shape[2] // LANES
    gain, shift = jnp.tile(gain, (1, times)), jnp.tile(shift, (1, times))

    def one(b, r, carry):
        state_ref[b, r, :] = (
            (kept_ref[b, r, :] + shift * first_ref[b, r, :].astype(F32)) * gain
        ).astype(BF16)
        return carry

    blocks, rows, _ = kept_ref.shape
    row_loop(blocks, rows, one, 0)

    def turn(n, carry):
        b, p = n // times, lax.rem(n, times)
        cols = pl.ds(pl.multiple_of(p * LANES, LANES), LANES)
        turned_ref[b, :, cols] = state_ref[b, :, cols].T
        return carry

    lax.fori_loop(0, blocks * times, turn, 0)


def environments(first, count, scale, env_ref, outer_ref, inner_ref, out_ref, mid_ref):
    dests, rows, width = outer_ref.shape
    phys = width // LANES

    def step(n, carry):
        pair, b = n // dests, lax.rem(n, dests)
        k = first + 2 * pair
        env = jnp.concatenate([env_ref[k, b], env_ref[k + 1, b]], axis=1)
        tall = jnp.concatenate(
            [outer_ref[b, :, p * LANES : (p + 1) * LANES] for p in range(phys)], axis=0
        )
        mid = dot(tall, env).astype(BF16)
        for p in range(phys):
            for i in range(2):
                mid_ref[i * rows : (i + 1) * rows, p * LANES : (p + 1) * LANES] = mid[
                    p * rows : (p + 1) * rows, i * LANES : (i + 1) * LANES
                ]
        last = jnp.concatenate(
            [inner_ref[b, :, p * LANES : (p + 1) * LANES] for p in range(phys)], axis=0
        )
        out = (dot(mid_ref[...], last) * scale).astype(BF16)
        out_ref[2 * pair, b] = out[:rows]
        out_ref[2 * pair + 1, b] = out[rows:]
        return carry

    lax.fori_loop(0, (count // 2) * dests, step, 0)


def normalize_and_left(
    first, count, scale, cells,
    kept_ref, first_ref, mine_ref, theirs_ref, env_ref,
    new_ref, state_ref, turned_ref, out_ref,
    mid_ref, sem,
):
    normalize(cells, kept_ref, first_ref, mine_ref, theirs_ref, state_ref, turned_ref)
    copy = pltpu.make_async_copy(state_ref, new_ref, sem)
    copy.start()
    environments(first, count, scale, env_ref, turned_ref, state_ref, out_ref, mid_ref)
    copy.wait()


def widen(places, *refs):
    pieces, outs, wides, sems = refs[:4], refs[4:6], refs[6:8], refs[8]
    copies = []
    for n, (piece, (side, begin)) in enumerate(zip(pieces, places)):
        count = piece.shape[0]

        def one(k, carry):
            wides[side][begin + k] = piece[k].astype(F32)
            return carry

        lax.fori_loop(0, count, one, 0)
        span = pl.ds(begin, count)
        copy = pltpu.make_async_copy(wides[side].at[span], outs[side].at[span], sems.at[n])
        copy.start()
        copies.append(copy)
    for copy in copies:
        copy.wait()


def shards(state, left_env, right_env, site_ops, sector_map, ranks):
    dests, rows, width = state.shape[1:]
    chan, phys = site_ops.shape[1:3]
    groups = lax.axis_size("blk")
    total_blocks = groups * dests
    first_block = lax.axis_index("blk") * dests
    x, left, right, ops = state[0], left_env[0], right_env[0], site_ops[0]
    local_map = lax.dynamic_slice_in_dim(sector_map[0], first_block, dests, 1)
    rel = lax.rem(local_map - first_block + total_blocks, total_blocks)

    swap = [(g, groups - 1 - g) for g in range(groups)]

    def trade(value):
        return lax.ppermute(value, "blk", swap)

    def shape(dims, kind):
        return jax.ShapeDtypeStruct(dims, kind)

    wave = (dests, rows, width)
    wave_f32 = shape(wave, F32)
    wave_b16 = shape(wave, BF16)
    sums_kind = shape((8, LANES), F32)
    lists = [pltpu.SMEM((chan * dests + 2 * dests + 1,), jnp.int32)] * 4
    pair_scratch = [
        pltpu.VMEM((2, rows, width), BF16), pltpu.VMEM((phys * rows, 2 * LANES), BF16)
    ] + lists

    def call(body, specs, outs, scratch, *args):
        return pl.pallas_call(
            body,
            in_specs=specs,
            out_specs=jax.tree.map(lambda _: VMEM, outs),
            out_shape=outs,
            scratch_shapes=scratch,
            compiler_params=PARAMS,
            cost_estimate=COST,
        )(*args)

    other = [trade(x[b : b + 1]) for b in range(dests)]
    kron, right_t, image_local, sums_local = call(
        first_local, [SMEM] + [VMEM] * 4,
        (shape((chan, phys * ROWS, phys * ROWS), BF16), shape(right.shape, BF16), wave_f32, sums_kind),
        pair_scratch, rel, ops, x, left, right,
    )
    image_remote = call(
        first_remote, [SMEM] + [VMEM] * 4, wave_f32, pair_scratch,
        rel, kron, other[0], left, right_t,
    )
    image_remote, guess, mine = call(
        first_finish, [SMEM] + [VMEM] * 8, (wave_f32, wave_b16, sums_kind), pair_scratch,
        rel, kron, other[1], left, right_t, image_remote, x, image_local, sums_local,
    )
    theirs = trade(mine)
    other = [trade(guess[b : b + 1]) for b in range(dests)]
    acc = call(
        second_local, [SMEM] + [VMEM] * 4, wave_f32, pair_scratch,
        rel, kron, guess, left, right_t,
    )
    acc, first = call(
        second_remote, [SMEM] + [VMEM] * 10, (wave_f32, wave_b16), pair_scratch,
        rel, kron, other[0], left, right_t, acc, x, image_local, image_remote, mine, theirs,
    )
    kept, kept_first, sums_mine = call(
        second_finish, [SMEM, SMEM] + [VMEM] * 8, (wave_f32, wave_b16, sums_kind),
        [pltpu.VMEM(wave, F32)] + pair_scratch,
        rel, ranks[0], kron, other[1], left, right_t, acc, first, mine, theirs,
    )
    sums_theirs = trade(sums_mine)

    env_scale = 1.0 / math.sqrt(phys * rows)
    cells = float(total_blocks * rows * width)
    early, later = 10, 8
    mid = [pltpu.VMEM((2 * rows, width), BF16)]

    def sent(value, steps):
        count = lax.axis_size("seg")
        begin, end = max(0, -steps), min(count, count - steps)
        return lax.ppermute(value, "seg", [(s, s + steps) for s in range(begin, end)])

    def env_kind(count):
        return shape((count,) + left.shape[1:], BF16)

    def env_call(begin, count, env, outer, inner):
        return call(
            functools.partial(environments, begin, count, env_scale),
            [VMEM] * 3, env_kind(count), mid, env, outer, inner,
        )

    new_state, state_kept, turned, piece = pl.pallas_call(
        functools.partial(normalize_and_left, 0, early, env_scale, cells),
        in_specs=[VMEM] * 5,
        out_specs=(pl.BlockSpec(memory_space=pltpu.HBM), VMEM, VMEM, VMEM),
        out_shape=(wave_b16, wave_b16, wave_b16, env_kind(early)),
        scratch_shapes=mid + [pltpu.SemaphoreType.DMA],
        compiler_params=PARAMS,
        cost_estimate=COST,
    )(kept, kept_first, sums_mine, sums_theirs, left)
    lefts = [sent(piece, 1)]
    rights = [
        sent(env_call(0, later, right, state_kept, turned), -1),
        sent(env_call(later, chan - later, right, state_kept, turned), -1),
    ]
    lefts.append(sent(env_call(early, chan - early, left, turned, state_kept), 1))
    env_f32 = shape(left.shape, F32)
    received_left, received_right = pl.pallas_call(
        functools.partial(widen, ((0, 0), (1, 0), (1, later), (0, early))),
        in_specs=[VMEM] * 4,
        out_specs=(pl.BlockSpec(memory_space=pltpu.HBM),) * 2,
        out_shape=(env_f32, env_f32),
        scratch_shapes=[pltpu.VMEM(left.shape, F32)] * 2 + [pltpu.SemaphoreType.DMA((4,))],
        compiler_params=PARAMS,
        cost_estimate=COST,
    )(lefts[0], rights[0], rights[1], lefts[1])
    return (new_state[None], received_left[None], received_right[None])


def solution(mesh):
    placed = (
        P("seg", "blk", None, None),
        P("seg", None, "blk", None, None),
        P("seg", None, "blk", None, None),
        P("seg", None, None, None),
        P("seg", None, None),
        P("seg", "blk"),
    )
    return jax.shard_map(
        shards,
        mesh=mesh,
        in_specs=placed,
        out_specs=(
            P("seg", "blk", None, None),
            P("seg", None, "blk", None, None),
            P("seg", None, "blk", None, None),
        ),
        check_vma=False,
    )
```

```python
import functools
import math

import jax
import jax.numpy as jnp
from jax import lax
from jax.experimental import pallas as pl
from jax.experimental.pallas import tpu as pltpu
from jax.sharding import PartitionSpec as P

STEP_SIZE = 0.25
EPSILON = 1e-06
LANES = 128
ROWS = 16
CHUNK = 32
F32 = jnp.float32
BF16 = jnp.bfloat16
VMEM = pl.BlockSpec(memory_space=pltpu.VMEM)
HBM = pl.BlockSpec(memory_space=pltpu.HBM)
SMEM = pl.BlockSpec(memory_space=pltpu.SMEM)
COST = pl.CostEstimate(flops=1024, bytes_accessed=1024, transcendentals=0)
PARAMS = pltpu.CompilerParams(vmem_limit_bytes=32 * 1024 * 1024)


def dot(left, right):
    return lax.dot_general(
        left, right, (((1,), (0,)), ((), ())), preferred_element_type=F32
    )


def make_kron(ops_ref, kron_ref):
    chan, phys, _ = ops_ref.shape
    wide = phys * ROWS
    spread_rows = (
        lax.broadcasted_iota(jnp.int32, (wide, phys), 0) // ROWS
        == lax.broadcasted_iota(jnp.int32, (wide, phys), 1)
    ).astype(F32).astype(BF16)
    spread_cols = (
        lax.broadcasted_iota(jnp.int32, (phys, wide), 1) // ROWS
        == lax.broadcasted_iota(jnp.int32, (phys, wide), 0)
    ).astype(F32).astype(BF16)
    diagonal = (
        lax.broadcasted_iota(jnp.int32, (wide, wide), 0) % ROWS
        == lax.broadcasted_iota(jnp.int32, (wide, wide), 1) % ROWS
    )

    def one(k, carry):
        tall = dot(spread_rows, ops_ref[k]).astype(BF16)
        full = dot(tall, spread_cols)
        kron_ref[k] = jnp.where(diagonal, full, 0.0).astype(BF16)
        return carry

    lax.fori_loop(0, chan, one, 0)


def list_pairs(rel_ref, low, high, chan_list, src_list, live_list, dest_list):
    chan, dests = rel_ref.shape
    place = jnp.int32(0)
    for b in range(dests):
        for k in range(chan):
            source = rel_ref[k, b]
            chan_list[place] = k
            src_list[place] = source - low
            live_list[place] = 1
            dest_list[place] = b
            place = place + jnp.where((source >= low) & (source < high), 1, 0)
        chan_list[place] = 0
        src_list[place] = 0
        live_list[place] = 0
        dest_list[place] = b
        place = place + lax.rem(place, 2)
    for n in range(2):
        chan_list[place + n] = 0
        src_list[place + n] = 0
    return place // 2


def add_pairs(steps, lists, kron_ref, x_ref, left_ref, right_t_ref, acc_ref, mixed_ref, part_ref):
    chan_list, src_list, live_list, dest_list = lists
    rows = x_ref.shape[1]
    phys = x_ref.shape[2] // LANES

    def mix(s):
        for i in range(2):
            source = src_list[2 * s + i]
            kron = kron_ref[chan_list[2 * s + i]]
            for g in range(rows // (2 * ROWS)):
                halves = []
                for j in range(2):
                    r0 = (2 * g + j) * ROWS
                    halves.append(
                        jnp.concatenate(
                            [
                                x_ref[source, r0 : r0 + ROWS, q * LANES : (q + 1) * LANES]
                                for q in range(phys)
                            ],
                            axis=0,
                        )
                    )
                out = dot(kron, jnp.concatenate(halves, axis=1)).astype(BF16)
                for j in range(2):
                    r0 = (2 * g + j) * ROWS
                    for p in range(phys):
                        mixed_ref[i, r0 : r0 + ROWS, p * LANES : (p + 1) * LANES] = out[
                            p * ROWS : (p + 1) * ROWS, j * LANES : (j + 1) * LANES
                        ]

    def step(s, carry):
        dest = dest_list[2 * s]
        weights = []
        for i in range(2):
            k = chan_list[2 * s + i]
            part = dot(left_ref[k, dest], mixed_ref[i]).astype(BF16)
            for p in range(phys):
                part_ref[p * rows : (p + 1) * rows, i * LANES : (i + 1) * LANES] = part[
                    :, p * LANES : (p + 1) * LANES
                ]
            right = right_t_ref[k, dest]
            if i == 1:
                right = jnp.where(live_list[2 * s + 1] > 0, right, jnp.zeros_like(right))
            weights.append(right)
        mix(s + 1)
        image = dot(part_ref[...], jnp.concatenate(weights, axis=0))
        for p in range(phys):
            acc_ref[dest, :, p * LANES : (p + 1) * LANES] += image[p * rows : (p + 1) * rows]
        return carry

    mix(0)
    lax.fori_loop(0, steps, step, 0)


def fold(values):
    total = values[:, :LANES]
    for p in range(1, values.shape[1] // LANES):
        total = total + values[:, p * LANES : (p + 1) * LANES]
    return total


def row_loop(blocks, rows, body, count):
    zeros = tuple(jnp.zeros((CHUNK, LANES), F32) for _ in range(count))
    per = rows // CHUNK

    def step(n, carry):
        return body(n // per, pl.ds(pl.multiple_of(lax.rem(n, per) * CHUNK, CHUNK), CHUNK), carry)

    return lax.fori_loop(0, blocks * per, step, zeros)


def put_sums(out_ref, values):
    for n, value in enumerate(values):
        out_ref[n : n + 1, :] = jnp.full((1, LANES), 1.0, F32) * value


def quotient(num, den):
    return jnp.where(den > 0, num / jnp.where(den > 0, den, 1.0), 0.0)


def cut(b, x_ref, out_ref, sem):
    copy = pltpu.make_async_copy(x_ref.at[pl.ds(b, 1)], out_ref, sem)
    copy.start()
    copy.wait()


def first_local(
    rel_ref, ops_ref, x_ref, left_ref, right_ref,
    kron_ref, right_t_ref, image_ref, sums_ref,
    mixed_ref, part_ref, chan_list, src_list, live_list, dest_list, fetched_ref, sem,
):
    lists = (chan_list, src_list, live_list, dest_list)
    fetch = pltpu.make_async_copy(right_ref, fetched_ref, sem)
    fetch.start()
    make_kron(ops_ref, kron_ref)
    chan, dests = left_ref.shape[:2]
    fetch.wait()

    def turn(n, carry):
        k, b = n // dests, lax.rem(n, dests)
        right_t_ref[k, b] = fetched_ref[k, b].T
        return carry

    lax.fori_loop(0, chan * dests, turn, 0)
    image_ref[...] = jnp.zeros_like(image_ref)
    steps = list_pairs(rel_ref, 0, dests, *lists)
    add_pairs(steps, lists, kron_ref, x_ref, left_ref, right_t_ref, image_ref, mixed_ref, part_ref)

    def sums(b, r, carry):
        x = x_ref[b, r, :].astype(F32)
        return carry[0] + fold(x * image_ref[b, r, :]), carry[1] + fold(x * x)

    num, den = row_loop(dests, x_ref.shape[1], sums, 2)
    put_sums(sums_ref, (jnp.sum(num), jnp.sum(den)))


def first_remote(
    rel_ref, kron_ref, other_ref, left_ref, right_t_ref,
    acc_ref,
    mixed_ref, part_ref, chan_list, src_list, live_list, dest_list,
):
    lists = (chan_list, src_list, live_list, dest_list)
    dests = left_ref.shape[1]
    acc_ref[...] = jnp.zeros_like(acc_ref)
    steps = list_pairs(rel_ref, dests, dests + 1, *lists)
    add_pairs(steps, lists, kron_ref, other_ref, left_ref, right_t_ref, acc_ref, mixed_ref, part_ref)


def first_finish(
    rel_ref, kron_ref, other_ref, left_ref, right_t_ref, before_ref, x_ref, image_ref, sums_ref,
    acc_ref, guess_ref, out_sums_ref,
    mixed_ref, part_ref, chan_list, src_list, live_list, dest_list,
):
    lists = (chan_list, src_list, live_list, dest_list)
    dests = left_ref.shape[1]
    acc_ref[...] = before_ref[...]
    steps = list_pairs(rel_ref, dests + 1, 2 * dests, *lists)
    add_pairs(steps, lists, kron_ref, other_ref, left_ref, right_t_ref, acc_ref, mixed_ref, part_ref)
    num_local, den = sums_ref[0:1, :], sums_ref[1:2, :]
    shift = quotient(num_local, den)
    keep_state = jnp.tile(1.0 + STEP_SIZE * shift, (1, x_ref.shape[2] // LANES))

    def sums(b, r, carry):
        x = x_ref[b, r, :].astype(F32)
        remote = acc_ref[b, r, :]
        guess_ref[b, r, :] = (keep_state * x - STEP_SIZE * (image_ref[b, r, :] + remote)).astype(BF16)
        return (carry[0] + fold(x * remote),)

    (num,) = row_loop(dests, x_ref.shape[1], sums, 1)
    out_sums_ref[0:1, :] = num_local + jnp.sum(num)
    out_sums_ref[1:2, :] = den
    out_sums_ref[2:3, :] = shift
    out_sums_ref[3:8, :] = jnp.zeros((5, LANES), F32)


def second_local(
    rel_ref, kron_ref, guess_ref, left_ref, right_t_ref,
    acc_ref,
    mixed_ref, part_ref, chan_list, src_list, live_list, dest_list,
):
    lists = (chan_list, src_list, live_list, dest_list)
    dests = left_ref.shape[1]
    acc_ref[...] = jnp.zeros_like(acc_ref)
    steps = list_pairs(rel_ref, 0, dests, *lists)
    add_pairs(steps, lists, kron_ref, guess_ref, left_ref, right_t_ref, acc_ref, mixed_ref, part_ref)


def second_remote(
    rel_ref, kron_ref, other_ref, left_ref, right_t_ref, before_ref,
    acc_ref,
    mixed_ref, part_ref, chan_list, src_list, live_list, dest_list,
):
    lists = (chan_list, src_list, live_list, dest_list)
    dests = left_ref.shape[1]
    acc_ref[...] = before_ref[...]
    steps = list_pairs(rel_ref, dests, dests + 1, *lists)
    add_pairs(steps, lists, kron_ref, other_ref, left_ref, right_t_ref, acc_ref, mixed_ref, part_ref)


def second_finish(
    rel_ref, rank_ref, kron_ref, other_ref, left_ref, right_t_ref, acc_ref, x_ref, image_ref,
    remote_ref, mine_ref, theirs_ref,
    kept_ref, kept_first_ref, out_sums_ref,
    mixed_ref, part_ref, chan_list, src_list, live_list, dest_list,
):
    lists = (chan_list, src_list, live_list, dest_list)
    dests, rows, width = x_ref.shape
    steps = list_pairs(rel_ref, dests + 1, 2 * dests, *lists)
    kept_ref[...] = acc_ref[...]
    add_pairs(steps, lists, kron_ref, other_ref, left_ref, right_t_ref, kept_ref, mixed_ref, part_ref)
    energy = (mine_ref[0:1, :] + theirs_ref[0:1, :]) / (mine_ref[1:2, :] + theirs_ref[1:2, :])
    wide = functools.partial(jnp.tile, reps=(1, width // LANES))
    keep_state = wide(1.0 + STEP_SIZE * energy)
    scale_local = wide(STEP_SIZE * (energy - mine_ref[2:3, :]))
    scale_remote = wide(STEP_SIZE * (energy - theirs_ref[2:3, :]))

    def sums(b, r, carry):
        local, remote = image_ref[b, r, :], remote_ref[b, r, :]
        x = x_ref[b, r, :].astype(F32)
        first_low = (keep_state * x - STEP_SIZE * (local + remote)).astype(BF16)
        first = first_low.astype(F32)
        image = kept_ref[b, r, :] + (scale_local * local + scale_remote * remote)
        row = r.start + lax.broadcasted_iota(jnp.int32, (CHUNK, width), 0)
        mask = row < rank_ref[b]
        kept = jnp.where(mask, keep_state * first - STEP_SIZE * image, 0.0)
        kept_first = jnp.where(mask, first, 0.0)
        kept_ref[b, r, :] = kept
        kept_first_ref[b, r, :] = kept_first.astype(BF16)
        return (
            carry[0] + fold(first * image),
            carry[1] + fold(first * first),
            carry[2] + fold(kept * kept),
            carry[3] + fold(kept * first),
            carry[4] + fold(kept_first * first),
        )

    totals = row_loop(dests, rows, sums, 5)
    for n, total in enumerate(totals):
        out_sums_ref[n : n + 1, :] = jnp.full((1, LANES), 1.0, F32) * jnp.sum(total)
    out_sums_ref[5:6, :] = energy
    out_sums_ref[6:8, :] = jnp.zeros((2, LANES), F32)


def normalize(
    cells, kept_ref, first_ref, mine_ref, theirs_ref, state_ref, turned_ref,
):
    both = mine_ref[...] + theirs_ref[...]
    shift = STEP_SIZE * (both[0:1] / both[1:2] - mine_ref[5:6, :])
    norm = jnp.maximum(both[2:3] + shift * (2.0 * both[3:4] + shift * both[4:5]), 0.0)
    gain = jnp.sqrt(cells / (norm + EPSILON))
    times = kept_ref.shape[2] // LANES
    gain, shift = jnp.tile(gain, (1, times)), jnp.tile(shift, (1, times))

    def one(b, r, carry):
        state_ref[b, r, :] = (
            (kept_ref[b, r, :] + shift * first_ref[b, r, :].astype(F32)) * gain
        ).astype(BF16)
        return carry

    blocks, rows, _ = kept_ref.shape
    row_loop(blocks, rows, one, 0)

    def turn(n, carry):
        b, p = n // times, lax.rem(n, times)
        cols = pl.ds(pl.multiple_of(p * LANES, LANES), LANES)
        turned_ref[b, :, cols] = state_ref[b, :, cols].T
        return carry

    lax.fori_loop(0, blocks * times, turn, 0)


def environments(first, count, scale, env_ref, inner_ref, outer_ref, out_ref, mid_ref):
    dests, rows, width = outer_ref.shape
    phys = width // LANES

    def step(n, carry):
        k = first + 2 * n
        for b in range(dests):
            env = jnp.concatenate([env_ref[k, b], env_ref[k + 1, b]], axis=0)
            mid = dot(env, inner_ref[b]).astype(BF16)
            for p in range(phys):
                for i in range(2):
                    mid_ref[b, p * rows : (p + 1) * rows, i * LANES : (i + 1) * LANES] = mid[
                        i * rows : (i + 1) * rows, p * LANES : (p + 1) * LANES
                    ]
        for b in range(dests):
            out = (dot(outer_ref[b], mid_ref[b]) * scale).astype(BF16)
            out_ref[2 * n, b] = out[:, :LANES]
            out_ref[2 * n + 1, b] = out[:, LANES:]
        return carry

    lax.fori_loop(0, count // 2, step, 0)


def normalize_and_left(
    first, count, scale, cells,
    kept_ref, first_ref, mine_ref, theirs_ref, env_ref,
    new_ref, state_ref, turned_ref, out_ref,
    mid_ref, sem,
):
    normalize(cells, kept_ref, first_ref, mine_ref, theirs_ref, state_ref, turned_ref)
    copy = pltpu.make_async_copy(state_ref, new_ref, sem)
    copy.start()
    environments(first, count, scale, env_ref, state_ref, turned_ref, out_ref, mid_ref)
    copy.wait()


def widen(places, *refs):
    pieces, outs, wides, sems = refs[:4], refs[4:6], refs[6:8], refs[8]
    copies = []
    for n, (piece, (side, begin)) in enumerate(zip(pieces, places)):
        count = piece.shape[0]

        def one(k, carry):
            wides[side][begin + k] = piece[k].astype(F32)
            return carry

        lax.fori_loop(0, count, one, 0)
        span = pl.ds(begin, count)
        copy = pltpu.make_async_copy(wides[side].at[span], outs[side].at[span], sems.at[n])
        copy.start()
        copies.append(copy)
    for copy in copies:
        copy.wait()


def shards(state, left_env, right_env, site_ops, sector_map, ranks):
    dests, rows, width = state.shape[1:]
    chan, phys = site_ops.shape[1:3]
    groups = lax.axis_size("blk")
    total_blocks = groups * dests
    first_block = lax.axis_index("blk") * dests
    x, left, right, ops = state[0], left_env[0], right_env[0], site_ops[0]
    local_map = lax.dynamic_slice_in_dim(sector_map[0], first_block, dests, 1)
    rel = lax.rem(local_map - first_block + total_blocks, total_blocks)

    swap = [(g, groups - 1 - g) for g in range(groups)]

    def trade(value):
        return lax.ppermute(value, "blk", swap)

    def shape(dims, kind):
        return jax.ShapeDtypeStruct(dims, kind)

    wave = (dests, rows, width)
    wave_f32 = shape(wave, F32)
    wave_b16 = shape(wave, BF16)
    sums_kind = shape((8, LANES), F32)
    lists = [pltpu.SMEM((chan * dests + 2 * dests + 1,), jnp.int32)] * 4
    pair_scratch = [
        pltpu.VMEM((2, rows, width), BF16), pltpu.VMEM((phys * rows, 2 * LANES), BF16)
    ] + lists

    def call(body, specs, outs, scratch, *args):
        return pl.pallas_call(
            body,
            in_specs=specs,
            out_specs=jax.tree.map(lambda _: VMEM, outs),
            out_shape=outs,
            scratch_shapes=scratch,
            compiler_params=PARAMS,
            cost_estimate=COST,
        )(*args)

    def block_of(b):
        return call(
            functools.partial(cut, b), [HBM], shape((1, rows, width), BF16),
            [pltpu.SemaphoreType.DMA], x,
        )

    other = [trade(block_of(b)) for b in range(dests)]
    kron, right_t, image_local, sums_local = call(
        first_local, [SMEM] + [VMEM] * 3 + [HBM],
        (shape((chan, phys * ROWS, phys * ROWS), BF16), shape(right.shape, BF16), wave_f32, sums_kind),
        pair_scratch + [pltpu.VMEM(right.shape, BF16), pltpu.SemaphoreType.DMA],
        rel, ops, x, left, right,
    )
    image_remote = call(
        first_remote, [SMEM] + [VMEM] * 4, wave_f32, pair_scratch,
        rel, kron, other[0], left, right_t,
    )
    image_remote, guess, mine = call(
        first_finish, [SMEM] + [VMEM] * 8, (wave_f32, wave_b16, sums_kind), pair_scratch,
        rel, kron, other[1], left, right_t, image_remote, x, image_local, sums_local,
    )
    theirs = trade(mine)
    other = [trade(guess[b : b + 1]) for b in range(dests)]
    acc = call(
        second_local, [SMEM] + [VMEM] * 4, wave_f32, pair_scratch,
        rel, kron, guess, left, right_t,
    )
    acc = call(
        second_remote, [SMEM] + [VMEM] * 5, wave_f32, pair_scratch,
        rel, kron, other[0], left, right_t, acc,
    )
    kept, kept_first, sums_mine = call(
        second_finish, [SMEM, SMEM] + [VMEM] * 10, (wave_f32, wave_b16, sums_kind), pair_scratch,
        rel, ranks[0], kron, other[1], left, right_t, acc, x, image_local, image_remote,
        mine, theirs,
    )
    sums_theirs = trade(sums_mine)

    env_scale = 1.0 / math.sqrt(phys * rows)
    cells = float(total_blocks * rows * width)
    early, later = 10, 8
    mid = [pltpu.VMEM((dests, width, 2 * LANES), BF16)]

    def sent(value, steps):
        count = lax.axis_size("seg")
        begin, end = max(0, -steps), min(count, count - steps)
        return lax.ppermute(value, "seg", [(s, s + steps) for s in range(begin, end)])

    def env_kind(count):
        return shape((count,) + left.shape[1:], BF16)

    def env_call(begin, count, env, inner, outer):
        return call(
            functools.partial(environments, begin, count, env_scale),
            [VMEM] * 3, env_kind(count), mid, env, inner, outer,
        )

    new_state, state_kept, turned, piece = pl.pallas_call(
        functools.partial(normalize_and_left, 0, early, env_scale, cells),
        in_specs=[VMEM] * 5,
        out_specs=(HBM, VMEM, VMEM, VMEM),
        out_shape=(wave_b16, wave_b16, wave_b16, env_kind(early)),
        scratch_shapes=mid + [pltpu.SemaphoreType.DMA],
        compiler_params=PARAMS,
        cost_estimate=COST,
    )(kept, kept_first, sums_mine, sums_theirs, left)
    lefts = [sent(piece, 1)]
    rights = [
        sent(env_call(0, later, right, turned, state_kept), -1),
        sent(env_call(later, chan - later, right, turned, state_kept), -1),
    ]
    lefts.append(sent(env_call(early, chan - early, left, state_kept, turned), 1))
    env_f32 = shape(left.shape, F32)
    received_left, received_right = pl.pallas_call(
        functools.partial(widen, ((0, 0), (1, 0), (1, later), (0, early))),
        in_specs=[VMEM] * 4,
        out_specs=(HBM,) * 2,
        out_shape=(env_f32, env_f32),
        scratch_shapes=[pltpu.VMEM(left.shape, F32)] * 2 + [pltpu.SemaphoreType.DMA((4,))],
        compiler_params=PARAMS,
        cost_estimate=COST,
    )(lefts[0], rights[0], rights[1], lefts[1])
    return (new_state[None], received_left[None], received_right[None])


def solution(mesh):
    placed = (
        P("seg", "blk", None, None),
        P("seg", None, "blk", None, None),
        P("seg", None, "blk", None, None),
        P("seg", None, None, None),
        P("seg", None, None),
        P("seg", "blk"),
    )
    return jax.shard_map(
        shards,
        mesh=mesh,
        in_specs=placed,
        out_specs=(
            P("seg", "blk", None, None),
            P("seg", None, "blk", None, None),
            P("seg", None, "blk", None, None),
        ),
        check_vma=False,
    )
```

```python
import functools
import math

import jax
import jax.numpy as jnp
from jax import lax
from jax.experimental import pallas as pl
from jax.experimental.pallas import tpu as pltpu
from jax.sharding import PartitionSpec as P

STEP_SIZE = 0.25
EPSILON = 1e-06
LANES = 128
ROWS = 16
CHUNK = 32
F32 = jnp.float32
BF16 = jnp.bfloat16
VMEM = pl.BlockSpec(memory_space=pltpu.VMEM)
HBM = pl.BlockSpec(memory_space=pltpu.HBM)
SMEM = pl.BlockSpec(memory_space=pltpu.SMEM)
COST = pl.CostEstimate(flops=1024, bytes_accessed=1024, transcendentals=0)
PARAMS = pltpu.CompilerParams(vmem_limit_bytes=32 * 1024 * 1024)


def dot(left, right):
    return lax.dot_general(
        left, right, (((1,), (0,)), ((), ())), preferred_element_type=F32
    )


def make_kron(ops_ref, kron_ref, spread_ref):
    chan, phys, _ = ops_ref.shape
    wide = phys * ROWS
    columns = lax.broadcasted_iota(jnp.int32, (phys, wide), 1)
    spread = (columns // ROWS == lax.broadcasted_iota(jnp.int32, (phys, wide), 0)).astype(F32)
    spread_ref[...] = dot(ops_ref[...].reshape(chan * phys, phys), spread.astype(BF16))
    same = lax.broadcasted_iota(jnp.int32, (ROWS, wide), 1) % ROWS == lax.broadcasted_iota(
        jnp.int32, (ROWS, wide), 0
    )

    def one(k, carry):
        rows = spread_ref[pl.ds(pl.multiple_of(k * phys, phys), phys), :]
        for p in range(phys):
            full = jnp.broadcast_to(rows[p : p + 1], (ROWS, wide))
            kron_ref[k, p * ROWS : (p + 1) * ROWS, :] = jnp.where(same, full, 0.0).astype(BF16)
        return carry

    lax.fori_loop(0, chan, one, 0)


def list_pairs(rel_ref, low, high, chan_list, src_list, live_list, dest_list, only=None):
    chan, dests = rel_ref.shape
    place = jnp.int32(0)
    for b in range(dests) if only is None else only:
        for k in range(chan):
            source = rel_ref[k, b]
            chan_list[place] = k
            src_list[place] = source - low
            live_list[place] = 1
            dest_list[place] = b
            place = place + jnp.where((source >= low) & (source < high), 1, 0)
        chan_list[place] = 0
        src_list[place] = 0
        live_list[place] = 0
        dest_list[place] = b
        place = place + lax.rem(place, 2)
    for n in range(2):
        chan_list[place + n] = 0
        src_list[place + n] = 0
    return place // 2


def add_pairs(steps, lists, kron_ref, x_ref, left_ref, right_t_ref, acc_ref, mixed_ref, part_ref):
    chan_list, src_list, live_list, dest_list = lists
    rows = x_ref.shape[1]
    phys = x_ref.shape[2] // LANES

    def mix(s):
        for i in range(2):
            source = src_list[2 * s + i]
            kron = kron_ref[chan_list[2 * s + i]]
            for g in range(rows // (2 * ROWS)):
                halves = []
                for j in range(2):
                    r0 = (2 * g + j) * ROWS
                    halves.append(
                        jnp.concatenate(
                            [
                                x_ref[source, r0 : r0 + ROWS, q * LANES : (q + 1) * LANES]
                                for q in range(phys)
                            ],
                            axis=0,
                        )
                    )
                out = dot(kron, jnp.concatenate(halves, axis=1)).astype(BF16)
                for j in range(2):
                    r0 = (2 * g + j) * ROWS
                    for p in range(phys):
                        mixed_ref[i, r0 : r0 + ROWS, p * LANES : (p + 1) * LANES] = out[
                            p * ROWS : (p + 1) * ROWS, j * LANES : (j + 1) * LANES
                        ]

    def step(s, carry):
        dest = dest_list[2 * s]
        weights = []
        for i in range(2):
            k = chan_list[2 * s + i]
            part = dot(left_ref[k, dest], mixed_ref[i]).astype(BF16)
            for p in range(phys):
                part_ref[p * rows : (p + 1) * rows, i * LANES : (i + 1) * LANES] = part[
                    :, p * LANES : (p + 1) * LANES
                ]
            right = right_t_ref[k, dest]
            if i == 1:
                right = jnp.where(live_list[2 * s + 1] > 0, right, jnp.zeros_like(right))
            weights.append(right)
        mix(s + 1)
        image = dot(part_ref[...], jnp.concatenate(weights, axis=0))
        for p in range(phys):
            acc_ref[dest, :, p * LANES : (p + 1) * LANES] += image[p * rows : (p + 1) * rows]
        return carry

    mix(0)
    lax.fori_loop(0, steps, step, 0)


def fold(values):
    total = values[:, :LANES]
    for p in range(1, values.shape[1] // LANES):
        total = total + values[:, p * LANES : (p + 1) * LANES]
    return total


def row_loop(blocks, rows, body, count, first=0):
    zeros = tuple(jnp.zeros((CHUNK, LANES), F32) for _ in range(count))
    per = rows // CHUNK

    def step(n, carry):
        return body(first + n // per, pl.ds(pl.multiple_of(lax.rem(n, per) * CHUNK, CHUNK), CHUNK), carry)

    return lax.fori_loop(0, blocks * per, step, zeros)


def put_sums(out_ref, values):
    for n, value in enumerate(values):
        out_ref[n : n + 1, :] = jnp.full((1, LANES), 1.0, F32) * value


def quotient(num, den):
    return jnp.where(den > 0, num / jnp.where(den > 0, den, 1.0), 0.0)


def cut(x_ref, *out_refs):
    for b, out_ref in enumerate(out_refs):
        out_ref[0] = x_ref[b]


def first_local(
    rel_ref, ops_ref, x_ref, left_ref, right_ref,
    kron_ref, right_t_ref, image_ref, sums_ref,
    mixed_ref, part_ref, chan_list, src_list, live_list, dest_list, spread_ref, fetched_ref, sem,
):
    lists = (chan_list, src_list, live_list, dest_list)
    fetch = pltpu.make_async_copy(right_ref, fetched_ref, sem)
    fetch.start()
    make_kron(ops_ref, kron_ref, spread_ref)
    chan, dests = left_ref.shape[:2]
    fetch.wait()

    def turn(n, carry):
        for k in range(2):
            for b in range(dests):
                right_t_ref[2 * n + k, b] = fetched_ref[2 * n + k, b].T
        return carry

    lax.fori_loop(0, chan // 2, turn, 0)
    image_ref[...] = jnp.zeros_like(image_ref)
    steps = list_pairs(rel_ref, 0, dests, *lists)
    add_pairs(steps, lists, kron_ref, x_ref, left_ref, right_t_ref, image_ref, mixed_ref, part_ref)

    def sums(b, r, carry):
        x = x_ref[b, r, :].astype(F32)
        return carry[0] + fold(x * image_ref[b, r, :]), carry[1] + fold(x * x)

    num, den = row_loop(dests, x_ref.shape[1], sums, 2)
    put_sums(sums_ref, (jnp.sum(num), jnp.sum(den)))


def first_remote(
    rel_ref, kron_ref, other_ref, left_ref, right_t_ref,
    acc_ref,
    mixed_ref, part_ref, chan_list, src_list, live_list, dest_list,
):
    lists = (chan_list, src_list, live_list, dest_list)
    dests = left_ref.shape[1]
    acc_ref[...] = jnp.zeros_like(acc_ref)
    steps = list_pairs(rel_ref, dests, dests + 1, *lists)
    add_pairs(steps, lists, kron_ref, other_ref, left_ref, right_t_ref, acc_ref, mixed_ref, part_ref)


def first_finish(
    dest, rel_ref, kron_ref, other_ref, left_ref, right_t_ref, before_ref, x_ref, image_ref,
    sums_ref, *refs,
):
    dests = left_ref.shape[1]
    last = dest == dests - 1
    if last:
        earlier_ref, earlier_sums_ref, acc_ref, guess_ref, out_sums_ref, all_ref = refs[:6]
    else:
        acc_ref, guess_ref, out_sums_ref = refs[:3]
    mixed_ref, part_ref = refs[-6:-4]
    lists = refs[-4:]
    steps = list_pairs(rel_ref, dests + 1, 2 * dests, *lists, only=(dest,))
    add_pairs(steps, lists, kron_ref, other_ref, left_ref, right_t_ref, acc_ref, mixed_ref, part_ref)
    num_local, den = sums_ref[0:1, :], sums_ref[1:2, :]
    shift = quotient(num_local, den)
    keep_state = jnp.tile(1.0 + STEP_SIZE * shift, (1, x_ref.shape[2] // LANES))

    def sums(b, r, carry):
        x = x_ref[b, r, :].astype(F32)
        remote = acc_ref[b, r, :]
        guess = (keep_state * x - STEP_SIZE * (image_ref[b, r, :] + remote)).astype(BF16)
        guess_ref[0, r, :] = guess
        if last:
            all_ref[b, r, :] = guess
        return (carry[0] + fold(x * remote),)

    (num,) = row_loop(1, x_ref.shape[1], sums, 1, first=dest)
    out_sums_ref[0:1, :] = jnp.full((1, LANES), 1.0, F32) * jnp.sum(num)
    if last:
        out_sums_ref[0:1, :] += earlier_sums_ref[0:1, :] + num_local
        all_ref[0:dest] = earlier_ref[...]
    out_sums_ref[1:2, :] = den
    out_sums_ref[2:3, :] = shift
    out_sums_ref[3:8, :] = jnp.zeros((5, LANES), F32)


def second_local(
    rel_ref, kron_ref, guess_ref, left_ref, right_t_ref,
    acc_ref,
    mixed_ref, part_ref, chan_list, src_list, live_list, dest_list,
):
    lists = (chan_list, src_list, live_list, dest_list)
    dests = left_ref.shape[1]
    acc_ref[...] = jnp.zeros_like(acc_ref)
    steps = list_pairs(rel_ref, 0, dests, *lists)
    add_pairs(steps, lists, kron_ref, guess_ref, left_ref, right_t_ref, acc_ref, mixed_ref, part_ref)


def second_remote(
    rel_ref, kron_ref, other_ref, left_ref, right_t_ref, before_ref,
    acc_ref,
    mixed_ref, part_ref, chan_list, src_list, live_list, dest_list,
):
    lists = (chan_list, src_list, live_list, dest_list)
    dests = left_ref.shape[1]
    steps = list_pairs(rel_ref, dests, dests + 1, *lists)
    add_pairs(steps, lists, kron_ref, other_ref, left_ref, right_t_ref, acc_ref, mixed_ref, part_ref)


def second_finish(
    rel_ref, rank_ref, kron_ref, other_ref, left_ref, right_t_ref, acc_ref, x_ref, image_ref,
    remote_ref, mine_ref, theirs_ref,
    kept_ref, kept_first_ref, out_sums_ref,
    mixed_ref, part_ref, chan_list, src_list, live_list, dest_list,
):
    lists = (chan_list, src_list, live_list, dest_list)
    dests, rows, width = x_ref.shape
    steps = list_pairs(rel_ref, dests + 1, 2 * dests, *lists)
    add_pairs(steps, lists, kron_ref, other_ref, left_ref, right_t_ref, kept_ref, mixed_ref, part_ref)
    energy = (mine_ref[0:1, :] + theirs_ref[0:1, :]) / (mine_ref[1:2, :] + theirs_ref[1:2, :])
    wide = functools.partial(jnp.tile, reps=(1, width // LANES))
    keep_state = wide(1.0 + STEP_SIZE * energy)
    scale_local = wide(STEP_SIZE * (energy - mine_ref[2:3, :]))
    scale_remote = wide(STEP_SIZE * (energy - theirs_ref[2:3, :]))

    def sums(b, r, carry):
        local, remote = image_ref[b, r, :], remote_ref[b, r, :]
        x = x_ref[b, r, :].astype(F32)
        first_low = (keep_state * x - STEP_SIZE * (local + remote)).astype(BF16)
        first = first_low.astype(F32)
        image = kept_ref[b, r, :] + (scale_local * local + scale_remote * remote)
        row = r.start + lax.broadcasted_iota(jnp.int32, (CHUNK, width), 0)
        mask = row < rank_ref[b]
        kept = jnp.where(mask, keep_state * first - STEP_SIZE * image, 0.0)
        kept_first = jnp.where(mask, first, 0.0)
        kept_ref[b, r, :] = kept
        kept_first_ref[b, r, :] = kept_first.astype(BF16)
        return (
            carry[0] + fold(first * image),
            carry[1] + fold(first * first),
            carry[2] + fold(kept * kept),
            carry[3] + fold(kept * first),
            carry[4] + fold(kept_first * first),
        )

    totals = row_loop(dests, rows, sums, 5)
    for n, total in enumerate(totals):
        out_sums_ref[n : n + 1, :] = jnp.full((1, LANES), 1.0, F32) * jnp.sum(total)
    out_sums_ref[5:6, :] = energy
    out_sums_ref[6:8, :] = jnp.zeros((2, LANES), F32)


def normalize(
    cells, kept_ref, first_ref, mine_ref, theirs_ref, state_ref, turned_ref,
):
    both = mine_ref[...] + theirs_ref[...]
    shift = STEP_SIZE * (both[0:1] / both[1:2] - mine_ref[5:6, :])
    norm = jnp.maximum(both[2:3] + shift * (2.0 * both[3:4] + shift * both[4:5]), 0.0)
    gain = jnp.sqrt(cells / (norm + EPSILON))
    blocks, rows, width = kept_ref.shape
    group = 4 * LANES
    per = width // group

    def one(n, carry):
        b = n // per
        for p in range(4):
            cols = pl.ds(pl.multiple_of(lax.rem(n, per) * group + p * LANES, LANES), LANES)
            kept = kept_ref[b, :, cols] + shift * first_ref[b, :, cols].astype(F32)
            state = (kept * gain).astype(BF16)
            state_ref[b, :, cols] = state
            turned_ref[b, :, cols] = state.T
        return carry

    lax.fori_loop(0, blocks * per, one, 0)


def environments(first, count, scale, env_ref, inner_ref, outer_ref, out_ref, mid_ref):
    dests, rows, width = outer_ref.shape
    phys = width // LANES

    def step(n, carry):
        k = first + 2 * n
        for b in range(dests):
            env = jnp.concatenate([env_ref[k, b], env_ref[k + 1, b]], axis=0)
            mid = dot(env, inner_ref[b]).astype(BF16)
            for p in range(phys):
                for i in range(2):
                    mid_ref[b, p * rows : (p + 1) * rows, i * LANES : (i + 1) * LANES] = mid[
                        i * rows : (i + 1) * rows, p * LANES : (p + 1) * LANES
                    ]
        for b in range(dests):
            out = (dot(outer_ref[b], mid_ref[b]) * scale).astype(BF16)
            out_ref[2 * n, b] = out[:, :LANES]
            out_ref[2 * n + 1, b] = out[:, LANES:]
        return carry

    lax.fori_loop(0, count // 2, step, 0)


def normalize_and_left(
    first, count, scale, cells,
    kept_ref, first_ref, mine_ref, theirs_ref, env_ref,
    new_ref, state_ref, turned_ref, out_ref,
    mid_ref, sem,
):
    normalize(cells, kept_ref, first_ref, mine_ref, theirs_ref, state_ref, turned_ref)
    copy = pltpu.make_async_copy(state_ref, new_ref, sem)
    copy.start()
    environments(first, count, scale, env_ref, state_ref, turned_ref, out_ref, mid_ref)
    copy.wait()


def widen(places, *refs):
    pieces, outs, wides, sems = refs[:4], refs[4:6], refs[6:8], refs[8]
    copies = []
    for piece, (side, begin) in zip(pieces, places):
        for n in range(0, piece.shape[0], 2):
            span = pl.ds(begin + n, 2)
            wides[side][begin + n : begin + n + 2] = piece[n : n + 2].astype(F32)
            copy = pltpu.make_async_copy(
                wides[side].at[span], outs[side].at[span], sems.at[len(copies)]
            )
            copy.start()
            copies.append(copy)
    for copy in copies:
        copy.wait()


def shards(state, left_env, right_env, site_ops, sector_map, ranks):
    dests, rows, width = state.shape[1:]
    chan, phys = site_ops.shape[1:3]
    groups = lax.axis_size("blk")
    total_blocks = groups * dests
    first_block = lax.axis_index("blk") * dests
    x, left, right, ops = state[0], left_env[0], right_env[0], site_ops[0]
    local_map = lax.dynamic_slice_in_dim(sector_map[0], first_block, dests, 1)
    rel = lax.rem(local_map - first_block + total_blocks, total_blocks)

    swap = [(g, groups - 1 - g) for g in range(groups)]

    def trade(value):
        return lax.ppermute(value, "blk", swap)

    def shape(dims, kind):
        return jax.ShapeDtypeStruct(dims, kind)

    wave = (dests, rows, width)
    wave_f32 = shape(wave, F32)
    wave_b16 = shape(wave, BF16)
    sums_kind = shape((8, LANES), F32)
    lists = [pltpu.SMEM((chan * dests + 2 * dests + 1,), jnp.int32)] * 4
    pair_scratch = [
        pltpu.VMEM((2, rows, width), BF16), pltpu.VMEM((phys * rows, 2 * LANES), BF16)
    ] + lists

    def call(body, specs, outs, scratch, *args, aliases={}):
        return pl.pallas_call(
            body,
            in_specs=specs,
            out_specs=jax.tree.map(lambda _: VMEM, outs),
            out_shape=outs,
            scratch_shapes=scratch,
            compiler_params=PARAMS,
            cost_estimate=COST,
            input_output_aliases=aliases,
        )(*args)

    block = shape((1, rows, width), BF16)
    own = call(cut, [VMEM], (block,) * dests, [], x)
    other = [trade(value) for value in own]
    kron, right_t, image_local, sums_local = call(
        first_local, [SMEM] + [VMEM] * 3 + [HBM],
        (shape((chan, phys * ROWS, phys * ROWS), BF16), shape(right.shape, BF16), wave_f32, sums_kind),
        pair_scratch
        + [
            pltpu.VMEM((chan * phys, phys * ROWS), F32),
            pltpu.VMEM(right.shape, BF16),
            pltpu.SemaphoreType.DMA,
        ],
        rel, ops, x, left, right,
    )
    image_remote = call(
        first_remote, [SMEM] + [VMEM] * 4, wave_f32, pair_scratch,
        rel, kron, other[0], left, right_t,
    )
    image_remote, first_guess, some = call(
        functools.partial(first_finish, 0), [SMEM] + [VMEM] * 8,
        (wave_f32, block, sums_kind), pair_scratch,
        rel, kron, other[1], left, right_t, image_remote, x, image_local, sums_local,
        aliases={5: 0},
    )
    image_remote, last_guess, mine, guess = call(
        functools.partial(first_finish, 1), [SMEM] + [VMEM] * 10,
        (wave_f32, block, sums_kind, wave_b16), pair_scratch,
        rel, kron, other[1], left, right_t, image_remote, x, image_local, sums_local,
        first_guess, some, aliases={5: 0},
    )
    other = [trade(first_guess), trade(last_guess)]
    theirs = trade(mine)
    acc = call(
        second_local, [SMEM] + [VMEM] * 4, wave_f32, pair_scratch,
        rel, kron, guess, left, right_t,
    )
    acc = call(
        second_remote, [SMEM] + [VMEM] * 5, wave_f32, pair_scratch,
        rel, kron, other[0], left, right_t, acc, aliases={5: 0},
    )
    kept, kept_first, sums_mine = call(
        second_finish, [SMEM, SMEM] + [VMEM] * 10, (wave_f32, wave_b16, sums_kind), pair_scratch,
        rel, ranks[0], kron, other[1], left, right_t, acc, x, image_local, image_remote,
        mine, theirs, aliases={6: 0},
    )
    sums_theirs = trade(sums_mine)

    env_scale = 1.0 / math.sqrt(phys * rows)
    cells = float(total_blocks * rows * width)
    early, later = 10, 8
    mid = [pltpu.VMEM((dests, width, 2 * LANES), BF16)]

    def sent(value, steps):
        count = lax.axis_size("seg")
        begin, end = max(0, -steps), min(count, count - steps)
        return lax.ppermute(value, "seg", [(s, s + steps) for s in range(begin, end)])

    def env_kind(count):
        return shape((count,) + left.shape[1:], BF16)

    def env_call(begin, count, env, inner, outer):
        return call(
            functools.partial(environments, begin, count, env_scale),
            [VMEM] * 3, env_kind(count), mid, env, inner, outer,
        )

    new_state, state_kept, turned, piece = pl.pallas_call(
        functools.partial(normalize_and_left, 0, early, env_scale, cells),
        in_specs=[VMEM] * 5,
        out_specs=(HBM, VMEM, VMEM, VMEM),
        out_shape=(wave_b16, wave_b16, wave_b16, env_kind(early)),
        scratch_shapes=mid + [pltpu.SemaphoreType.DMA],
        compiler_params=PARAMS,
        cost_estimate=COST,
    )(kept, kept_first, sums_mine, sums_theirs, left)
    lefts = [sent(piece, 1)]
    rights = [
        sent(env_call(0, later, right, turned, state_kept), -1),
        sent(env_call(later, chan - later, right, turned, state_kept), -1),
    ]
    lefts.append(sent(env_call(early, chan - early, left, state_kept, turned), 1))
    env_f32 = shape(left.shape, F32)
    received_left, received_right = pl.pallas_call(
        functools.partial(widen, ((0, 0), (1, 0), (1, later), (0, early))),
        in_specs=[VMEM] * 4,
        out_specs=(HBM,) * 2,
        out_shape=(env_f32, env_f32),
        scratch_shapes=[pltpu.VMEM(left.shape, F32)] * 2 + [pltpu.SemaphoreType.DMA((chan,))],
        compiler_params=PARAMS,
        cost_estimate=COST,
    )(lefts[0], rights[0], rights[1], lefts[1])
    return (new_state[None], received_left[None], received_right[None])


def solution(mesh):
    placed = (
        P("seg", "blk", None, None),
        P("seg", None, "blk", None, None),
        P("seg", None, "blk", None, None),
        P("seg", None, None, None),
        P("seg", None, None),
        P("seg", "blk"),
    )
    return jax.shard_map(
        shards,
        mesh=mesh,
        in_specs=placed,
        out_specs=(
            P("seg", "blk", None, None),
            P("seg", None, "blk", None, None),
            P("seg", None, "blk", None, None),
        ),
        check_vma=False,
    )
```

```python
import functools
import math

import jax
import jax.numpy as jnp
from jax import lax
from jax.experimental import pallas as pl
from jax.experimental.pallas import tpu as pltpu
from jax.sharding import PartitionSpec as P

STEP_SIZE = 0.25
EPSILON = 1e-06
LANES = 128
ROWS = 16
CHUNK = 32
F32 = jnp.float32
BF16 = jnp.bfloat16
VMEM = pl.BlockSpec(memory_space=pltpu.VMEM)
HBM = pl.BlockSpec(memory_space=pltpu.HBM)
SMEM = pl.BlockSpec(memory_space=pltpu.SMEM)
COST = pl.CostEstimate(flops=1024, bytes_accessed=1024, transcendentals=0)
PARAMS = pltpu.CompilerParams(vmem_limit_bytes=32 * 1024 * 1024)


def dot(left, right):
    return lax.dot_general(
        left, right, (((1,), (0,)), ((), ())), preferred_element_type=F32
    )


def make_kron(ops_ref, kron_ref, spread_ref):
    chan, phys, _ = ops_ref.shape
    wide = phys * ROWS
    columns = lax.broadcasted_iota(jnp.int32, (phys, wide), 1)
    spread = (columns // ROWS == lax.broadcasted_iota(jnp.int32, (phys, wide), 0)).astype(F32)
    spread_ref[...] = dot(ops_ref[...].reshape(chan * phys, phys), spread.astype(BF16))
    same = lax.broadcasted_iota(jnp.int32, (ROWS, wide), 1) % ROWS == lax.broadcasted_iota(
        jnp.int32, (ROWS, wide), 0
    )

    def one(k, carry):
        rows = spread_ref[pl.ds(pl.multiple_of(k * phys, phys), phys), :]
        for p in range(phys):
            full = jnp.broadcast_to(rows[p : p + 1], (ROWS, wide))
            kron_ref[k, p * ROWS : (p + 1) * ROWS, :] = jnp.where(same, full, 0.0).astype(BF16)
        return carry

    lax.fori_loop(0, chan, one, 0)


def list_pairs(rel_ref, low, high, chan_list, src_list, live_list, dest_list, only=None):
    chan, dests = rel_ref.shape
    place = jnp.int32(0)
    for b in range(dests) if only is None else only:
        for k in range(chan):
            source = rel_ref[k, b]
            chan_list[place] = k
            src_list[place] = source - low
            live_list[place] = 1
            dest_list[place] = b
            place = place + jnp.where((source >= low) & (source < high), 1, 0)
        chan_list[place] = 0
        src_list[place] = 0
        live_list[place] = 0
        dest_list[place] = b
        place = place + lax.rem(place, 2)
    return place // 2


def add_pairs(steps, lists, kron_ref, x_ref, left_ref, right_t_ref, acc_ref, mixed_ref, part_ref):
    chan_list, src_list, live_list, dest_list = lists
    rows = x_ref.shape[1]
    phys = x_ref.shape[2] // LANES

    def mix(s):
        for i in range(2):
            source = src_list[2 * s + i]
            kron = kron_ref[chan_list[2 * s + i]]
            for g in range(rows // (2 * ROWS)):
                halves = []
                for j in range(2):
                    r0 = (2 * g + j) * ROWS
                    halves.append(
                        jnp.concatenate(
                            [
                                x_ref[source, r0 : r0 + ROWS, q * LANES : (q + 1) * LANES]
                                for q in range(phys)
                            ],
                            axis=0,
                        )
                    )
                out = dot(kron, jnp.concatenate(halves, axis=1)).astype(BF16)
                for j in range(2):
                    r0 = (2 * g + j) * ROWS
                    for p in range(phys):
                        mixed_ref[i, r0 : r0 + ROWS, p * LANES : (p + 1) * LANES] = out[
                            p * ROWS : (p + 1) * ROWS, j * LANES : (j + 1) * LANES
                        ]

    def step(s, follow):
        dest = dest_list[2 * s]
        weights = []
        for i in range(2):
            k = chan_list[2 * s + i]
            part = dot(left_ref[k, dest], mixed_ref[i]).astype(BF16)
            for p in range(phys):
                part_ref[p * rows : (p + 1) * rows, i * LANES : (i + 1) * LANES] = part[
                    :, p * LANES : (p + 1) * LANES
                ]
            right = right_t_ref[k, dest]
            if i == 1:
                right = jnp.where(live_list[2 * s + 1] > 0, right, jnp.zeros_like(right))
            weights.append(right)
        if follow:
            mix(s + 1)
        image = dot(part_ref[...], jnp.concatenate(weights, axis=0))
        for p in range(phys):
            acc_ref[dest, :, p * LANES : (p + 1) * LANES] += image[p * rows : (p + 1) * rows]

    def middle(s, carry):
        step(s, True)
        return carry

    @pl.when(steps > 0)
    def _():
        mix(0)
        lax.fori_loop(0, steps - 1, middle, 0)
        step(steps - 1, False)


def fold(values):
    total = values[:, :LANES]
    for p in range(1, values.shape[1] // LANES):
        total = total + values[:, p * LANES : (p + 1) * LANES]
    return total


def row_loop(blocks, rows, body, count, first=0):
    zeros = tuple(jnp.zeros((CHUNK, LANES), F32) for _ in range(count))
    per = rows // CHUNK

    def step(n, carry):
        start = pl.multiple_of(lax.rem(n, per) * CHUNK, CHUNK)
        return body(first + n // per, pl.ds(start, CHUNK), start, carry)

    return lax.fori_loop(0, blocks * per, step, zeros)


def kept_rows(rank, start):
    row = start + lax.broadcasted_iota(jnp.int32, (CHUNK, LANES), 0)
    return (row < rank).astype(F32)


def put_sums(out_ref, values, first=0):
    for n, value in enumerate(values):
        out_ref[first + n : first + n + 1, :] = jnp.full((1, LANES), 1.0, F32) * jnp.sum(value)


def common_shift(mine_ref, theirs_ref):
    num = mine_ref[0:1, :] + theirs_ref[0:1, :]
    den = mine_ref[1:2, :] + theirs_ref[1:2, :]
    return jnp.where(den > 0, num / jnp.where(den > 0, den, 1.0), 0.0)


def cut(x_ref, *out_refs):
    for b, out_ref in enumerate(out_refs):
        out_ref[0] = x_ref[b]


def first_local(
    rel_ref, ops_ref, x_ref, left_ref, right_ref,
    kron_ref, right_t_ref, image_ref, sums_ref,
    mixed_ref, part_ref, chan_list, src_list, live_list, dest_list, spread_ref, fetched_ref, sem,
):
    lists = (chan_list, src_list, live_list, dest_list)
    fetch = pltpu.make_async_copy(right_ref, fetched_ref, sem)
    fetch.start()
    make_kron(ops_ref, kron_ref, spread_ref)
    chan, dests = left_ref.shape[:2]
    fetch.wait()

    def turn(n, carry):
        for k in range(2):
            for b in range(dests):
                right_t_ref[2 * n + k, b] = fetched_ref[2 * n + k, b].T
        return carry

    lax.fori_loop(0, chan // 2, turn, 0)
    image_ref[...] = jnp.zeros_like(image_ref)
    steps = list_pairs(rel_ref, 0, dests, *lists)
    add_pairs(steps, lists, kron_ref, x_ref, left_ref, right_t_ref, image_ref, mixed_ref, part_ref)

    def sums(b, r, start, carry):
        x = x_ref[b, r, :].astype(F32)
        return carry[0] + fold(x * image_ref[b, r, :]), carry[1] + fold(x * x)

    totals = row_loop(dests, x_ref.shape[1], sums, 2)
    sums_ref[...] = jnp.zeros_like(sums_ref)
    put_sums(sums_ref, totals)


def local_sources(
    rel_ref, kron_ref, x_ref, left_ref, right_t_ref,
    acc_ref,
    mixed_ref, part_ref, *lists,
):
    acc_ref[...] = jnp.zeros_like(acc_ref)
    steps = list_pairs(rel_ref, 0, left_ref.shape[1], *lists)
    add_pairs(steps, lists, kron_ref, x_ref, left_ref, right_t_ref, acc_ref, mixed_ref, part_ref)


def remote_sources(
    rel_ref, kron_ref, other_ref, left_ref, right_t_ref, before_ref,
    acc_ref,
    mixed_ref, part_ref, *lists,
):
    dests = left_ref.shape[1]
    steps = list_pairs(rel_ref, dests, dests + 1, *lists)
    add_pairs(steps, lists, kron_ref, other_ref, left_ref, right_t_ref, acc_ref, mixed_ref, part_ref)


def first_finish(
    dest, rel_ref, kron_ref, other_ref, left_ref, right_t_ref, before_ref, x_ref, mine_ref,
    theirs_ref, *refs,
):
    dests = left_ref.shape[1]
    last = dest == dests - 1
    if last:
        earlier_ref, acc_ref, guess_ref, all_ref = refs[:4]
        all_ref[0:dest] = earlier_ref[...]
    else:
        acc_ref, guess_ref = refs[:2]
    mixed_ref, part_ref = refs[-6:-4]
    lists = refs[-4:]
    steps = list_pairs(rel_ref, dests + 1, 2 * dests, *lists, only=(dest,))
    add_pairs(steps, lists, kron_ref, other_ref, left_ref, right_t_ref, acc_ref, mixed_ref, part_ref)
    shift = common_shift(mine_ref, theirs_ref)
    keep_state = jnp.tile(1.0 + STEP_SIZE * shift, (1, x_ref.shape[2] // LANES))

    def update(b, r, start, carry):
        x = x_ref[b, r, :].astype(F32)
        guess = (keep_state * x - STEP_SIZE * acc_ref[b, r, :]).astype(BF16)
        guess_ref[0, r, :] = guess
        if last:
            all_ref[b, r, :] = guess
        return carry

    row_loop(1, x_ref.shape[1], update, 0, first=dest)


def second_remote(
    rel_ref, rank_ref, kron_ref, other_ref, left_ref, right_t_ref, before_ref, x_ref, image_ref,
    guess_ref,
    acc_ref, sums_ref,
    mixed_ref, part_ref, *lists,
):
    dests, rows, _ = x_ref.shape
    steps = list_pairs(rel_ref, dests, dests + 1, *lists)
    add_pairs(steps, lists, kron_ref, other_ref, left_ref, right_t_ref, acc_ref, mixed_ref, part_ref)

    def sums(b, r, start, carry):
        x = x_ref[b, r, :].astype(F32)
        guess = guess_ref[b, r, :].astype(F32)
        image = image_ref[b, r, :]
        keep = kept_rows(rank_ref[b], start)
        xx, xg, gg = fold(x * x), fold(x * guess), fold(guess * guess)
        new = (fold(x * image), xx, fold(guess * image), xg, gg, keep * gg, keep * xx, keep * xg)
        return tuple(total + value for total, value in zip(carry, new))

    put_sums(sums_ref, row_loop(dests, rows, sums, 8))


def second_finish(
    rel_ref, rank_ref, kron_ref, other_ref, left_ref, right_t_ref, before_ref, x_ref, guess_ref,
    mine_ref, theirs_ref, early_ref,
    kept_ref, sums_ref,
    mixed_ref, part_ref, *lists,
):
    dests, rows, width = x_ref.shape
    steps = list_pairs(rel_ref, dests + 1, 2 * dests, *lists)
    add_pairs(steps, lists, kron_ref, other_ref, left_ref, right_t_ref, kept_ref, mixed_ref, part_ref)
    shift = common_shift(mine_ref, theirs_ref)
    keep_guess = jnp.tile(1.0 + STEP_SIZE * shift, (1, width // LANES))

    def sums(b, r, start, carry):
        x = x_ref[b, r, :].astype(F32)
        guess = guess_ref[b, r, :].astype(F32)
        kept = keep_guess * guess - STEP_SIZE * kept_ref[b, r, :]
        kept_ref[b, r, :] = kept
        keep = kept_rows(rank_ref[b], start)
        kg, kx = fold(kept * guess), fold(kept * x)
        new = (kg, kx, keep * kg, keep * kx, keep * fold(kept * kept))
        return tuple(total + value for total, value in zip(carry, new))

    totals = row_loop(dests, rows, sums, 5)
    sums_ref[0:8, :] = early_ref[...]
    put_sums(sums_ref, totals, first=8)
    sums_ref[13:16, :] = jnp.zeros((3, LANES), F32)


def normalize(
    cells, rank_ref, kept_ref, guess_ref, x_ref, mine_ref, theirs_ref, my_sums_ref, their_sums_ref,
    state_ref, turned_ref,
):
    both = my_sums_ref[...] + their_sums_ref[...]
    xv, xx, gv, xg, gg, gg_kept, xx_kept, xg_kept, kg, kx, kg_kept, kx_kept, kk_kept = (
        both[n : n + 1] for n in range(13)
    )
    shift = common_shift(mine_ref, theirs_ref)
    delta = STEP_SIZE * (xv / xx - shift)
    scale = (1.0 + STEP_SIZE * shift) / STEP_SIZE
    gw, xw = scale * gg - kg / STEP_SIZE, scale * xg - kx / STEP_SIZE
    num = gw + delta * (xw + gv + delta * xv)
    den = gg + delta * (2.0 * xg + delta * xx)
    beta = STEP_SIZE * (num / den - shift)
    of_guess, of_state = beta + delta, beta * delta
    norm = (
        kk_kept
        + of_guess * (2.0 * kg_kept + of_guess * gg_kept)
        + of_state * (2.0 * kx_kept + of_state * xx_kept + 2.0 * of_guess * xg_kept)
    )
    gain = jnp.sqrt(cells / (jnp.maximum(norm, 0.0) + EPSILON))
    blocks, rows, width = kept_ref.shape
    group = 4 * LANES
    per = width // group
    row = lax.broadcasted_iota(jnp.int32, (rows, LANES), 0)

    def one(n, carry):
        b = n // per
        factor = jnp.where(row < rank_ref[b], gain, 0.0)
        for p in range(4):
            cols = pl.ds(pl.multiple_of(lax.rem(n, per) * group + p * LANES, LANES), LANES)
            kept = (
                kept_ref[b, :, cols]
                + of_guess * guess_ref[b, :, cols].astype(F32)
                + of_state * x_ref[b, :, cols].astype(F32)
            )
            state = (kept * factor).astype(BF16)
            state_ref[b, :, cols] = state
            turned_ref[b, :, cols] = state.T
        return carry

    lax.fori_loop(0, blocks * per, one, 0)


def environments(first, count, scale, env_ref, inner_ref, outer_ref, out_ref, mid_ref):
    dests, rows, width = outer_ref.shape
    phys = width // LANES

    def step(n, carry):
        k = first + 2 * n
        for b in range(dests):
            env = jnp.concatenate([env_ref[k, b], env_ref[k + 1, b]], axis=0)
            mid = dot(env, inner_ref[b]).astype(BF16)
            for p in range(phys):
                for i in range(2):
                    mid_ref[b, p * rows : (p + 1) * rows, i * LANES : (i + 1) * LANES] = mid[
                        i * rows : (i + 1) * rows, p * LANES : (p + 1) * LANES
                    ]
        for b in range(dests):
            out = (dot(outer_ref[b], mid_ref[b]) * scale).astype(BF16)
            out_ref[2 * n, b] = out[:, :LANES]
            out_ref[2 * n + 1, b] = out[:, LANES:]
        return carry

    lax.fori_loop(0, count // 2, step, 0)


def normalize_and_left(
    first, count, scale, cells,
    rank_ref, kept_ref, guess_ref, x_ref, mine_ref, theirs_ref, my_sums_ref, their_sums_ref, env_ref,
    new_ref, state_ref, turned_ref, out_ref,
    mid_ref, sem,
):
    normalize(
        cells, rank_ref, kept_ref, guess_ref, x_ref, mine_ref, theirs_ref, my_sums_ref,
        their_sums_ref, state_ref, turned_ref,
    )
    copy = pltpu.make_async_copy(state_ref, new_ref, sem)
    copy.start()
    environments(first, count, scale, env_ref, state_ref, turned_ref, out_ref, mid_ref)
    copy.wait()


def widen(places, *refs):
    pieces, (outs, wides, sems) = refs[: len(places)], (refs[-5:-3], refs[-3:-1], refs[-1])
    copies = []
    for piece, (side, begin) in zip(pieces, places):
        for n in range(0, piece.shape[0], 2):
            span = pl.ds(begin + n, 2)
            wides[side][begin + n : begin + n + 2] = piece[n : n + 2].astype(F32)
            copy = pltpu.make_async_copy(
                wides[side].at[span], outs[side].at[span], sems.at[len(copies)]
            )
            copy.start()
            copies.append(copy)
    for copy in copies:
        copy.wait()


def shards(state, left_env, right_env, site_ops, sector_map, ranks):
    dests, rows, width = state.shape[1:]
    chan, phys = site_ops.shape[1:3]
    groups = lax.axis_size("blk")
    total_blocks = groups * dests
    first_block = lax.axis_index("blk") * dests
    x, left, right, ops = state[0], left_env[0], right_env[0], site_ops[0]
    local_map = lax.dynamic_slice_in_dim(sector_map[0], first_block, dests, 1)
    rel = lax.rem(local_map - first_block + total_blocks, total_blocks)

    swap = [(g, groups - 1 - g) for g in range(groups)]

    def trade(value):
        return lax.ppermute(value, "blk", swap)

    def shape(dims, kind):
        return jax.ShapeDtypeStruct(dims, kind)

    wave = (dests, rows, width)
    wave_f32 = shape(wave, F32)
    wave_b16 = shape(wave, BF16)
    sums_kind = shape((8, LANES), F32)
    lists = [pltpu.SMEM((chan * dests + 2 * dests + 1,), jnp.int32)] * 4
    pair_scratch = [
        pltpu.VMEM((2, rows, width), BF16), pltpu.VMEM((phys * rows, 2 * LANES), BF16)
    ] + lists

    def call(body, specs, outs, scratch, *args, aliases={}):
        return pl.pallas_call(
            body,
            in_specs=specs,
            out_specs=jax.tree.map(lambda _: VMEM, outs),
            out_shape=outs,
            scratch_shapes=scratch,
            compiler_params=PARAMS,
            cost_estimate=COST,
            input_output_aliases=aliases,
        )(*args)

    block = shape((1, rows, width), BF16)
    own = pl.pallas_call(
        cut,
        in_specs=[VMEM],
        out_specs=(VMEM,) * dests,
        out_shape=(block,) * dests,
        compiler_params=PARAMS,
        cost_estimate=pl.CostEstimate(
            flops=1024, bytes_accessed=4 * 1024 * 1024, transcendentals=0
        ),
    )(x)
    other = [trade(value) for value in own]
    kron, right_t, image, mine = call(
        first_local, [SMEM] + [VMEM] * 3 + [HBM],
        (shape((chan, phys * ROWS, phys * ROWS), BF16), shape(right.shape, BF16), wave_f32, sums_kind),
        pair_scratch
        + [
            pltpu.VMEM((chan * phys, phys * ROWS), F32),
            pltpu.VMEM(right.shape, BF16),
            pltpu.SemaphoreType.DMA,
        ],
        rel, ops, x, left, right,
    )
    theirs = trade(mine)
    image = call(
        remote_sources, [SMEM] + [VMEM] * 5, wave_f32, pair_scratch,
        rel, kron, other[0], left, right_t, image, aliases={5: 0},
    )
    image, first_guess = call(
        functools.partial(first_finish, 0), [SMEM] + [VMEM] * 8,
        (wave_f32, block), pair_scratch,
        rel, kron, other[1], left, right_t, image, x, mine, theirs, aliases={5: 0},
    )
    image, last_guess, guess = call(
        functools.partial(first_finish, 1), [SMEM] + [VMEM] * 9,
        (wave_f32, block, wave_b16), pair_scratch,
        rel, kron, other[1], left, right_t, image, x, mine, theirs, first_guess, aliases={5: 0},
    )
    other = [trade(first_guess), trade(last_guess)]
    acc = call(
        local_sources, [SMEM] + [VMEM] * 4, wave_f32, pair_scratch,
        rel, kron, guess, left, right_t,
    )
    acc, early_sums = call(
        second_remote, [SMEM] * 2 + [VMEM] * 8, (wave_f32, sums_kind), pair_scratch,
        rel, ranks[0], kron, other[0], left, right_t, acc, x, image, guess, aliases={6: 0},
    )
    kept, my_sums = call(
        second_finish, [SMEM] * 2 + [VMEM] * 10, (wave_f32, shape((16, LANES), F32)), pair_scratch,
        rel, ranks[0], kron, other[1], left, right_t, acc, x, guess, mine, theirs, early_sums,
        aliases={6: 0},
    )
    their_sums = trade(my_sums)

    env_scale = 1.0 / math.sqrt(phys * rows)
    cells = float(total_blocks * rows * width)
    early, later = 8, 8
    mid = [pltpu.VMEM((dests, width, 2 * LANES), BF16)]

    def sent(value, steps):
        count = lax.axis_size("seg")
        begin, end = max(0, -steps), min(count, count - steps)
        return lax.ppermute(value, "seg", [(s, s + steps) for s in range(begin, end)])

    def env_kind(count):
        return shape((count,) + left.shape[1:], BF16)

    def env_call(begin, count, env, inner, outer):
        return call(
            functools.partial(environments, begin, count, env_scale),
            [VMEM] * 3, env_kind(count), mid, env, inner, outer,
        )

    new_state, state_kept, turned, piece = pl.pallas_call(
        functools.partial(normalize_and_left, 0, early, env_scale, cells),
        in_specs=[SMEM] + [VMEM] * 8,
        out_specs=(HBM, VMEM, VMEM, VMEM),
        out_shape=(wave_b16, wave_b16, wave_b16, env_kind(early)),
        scratch_shapes=mid + [pltpu.SemaphoreType.DMA],
        compiler_params=PARAMS,
        cost_estimate=COST,
    )(ranks[0], kept, guess, x, mine, theirs, my_sums, their_sums, left)
    pieces = [
        sent(piece, 1),
        sent(env_call(0, later, right, turned, state_kept), -1),
        sent(env_call(early, chan - early, left, state_kept, turned), 1),
        sent(env_call(later, chan - later, right, turned, state_kept), -1),
    ]
    env_f32 = shape(left.shape, F32)

    def widened(places, values, filled):
        count = len(values)
        return pl.pallas_call(
            functools.partial(widen, places),
            in_specs=[VMEM] * count + [HBM] * len(filled),
            out_specs=(HBM, HBM),
            out_shape=(env_f32, env_f32),
            input_output_aliases={count + n: n for n in range(len(filled))},
            scratch_shapes=[pltpu.VMEM(left.shape, F32)] * 2 + [pltpu.SemaphoreType.DMA((chan,))],
            compiler_params=PARAMS,
            cost_estimate=COST,
        )(*values, *filled)

    filled = widened(((0, 0),), pieces[:1], ())
    received_left, received_right = widened(((1, 0), (0, early), (1, later)), pieces[1:], filled)
    return (new_state[None], received_left[None], received_right[None])


def solution(mesh):
    placed = (
        P("seg", "blk", None, None),
        P("seg", None, "blk", None, None),
        P("seg", None, "blk", None, None),
        P("seg", None, None, None),
        P("seg", None, None),
        P("seg", "blk"),
    )
    return jax.shard_map(
        shards,
        mesh=mesh,
        in_specs=placed,
        out_specs=(
            P("seg", "blk", None, None),
            P("seg", None, "blk", None, None),
            P("seg", None, "blk", None, None),
        ),
        check_vma=False,
    )
```

```python
import functools
import math

import jax
import jax.numpy as jnp
from jax import lax
from jax.experimental import pallas as pl
from jax.experimental.pallas import tpu as pltpu
from jax.sharding import PartitionSpec as P

STEP_SIZE = 0.25
EPSILON = 1e-06
LANES = 128
ROWS = 16
CHUNK = 32
F32 = jnp.float32
BF16 = jnp.bfloat16
VMEM = pl.BlockSpec(memory_space=pltpu.VMEM)
HBM = pl.BlockSpec(memory_space=pltpu.HBM)
SMEM = pl.BlockSpec(memory_space=pltpu.SMEM)
COST = pl.CostEstimate(flops=1024, bytes_accessed=1024, transcendentals=0)
PARAMS = pltpu.CompilerParams(vmem_limit_bytes=32 * 1024 * 1024)


def dot(left, right):
    return lax.dot_general(
        left, right, (((1,), (0,)), ((), ())), preferred_element_type=F32
    )


def make_kron(ops_ref, kron_ref, spread_ref):
    chan, phys, _ = ops_ref.shape
    wide = phys * ROWS
    columns = lax.broadcasted_iota(jnp.int32, (phys, wide), 1)
    spread = (columns // ROWS == lax.broadcasted_iota(jnp.int32, (phys, wide), 0)).astype(F32)
    spread_ref[...] = dot(ops_ref[...].reshape(chan * phys, phys), spread.astype(BF16))
    same = lax.broadcasted_iota(jnp.int32, (ROWS, wide), 1) % ROWS == lax.broadcasted_iota(
        jnp.int32, (ROWS, wide), 0
    )

    def one(k, carry):
        rows = spread_ref[pl.ds(pl.multiple_of(k * phys, phys), phys), :]
        for p in range(phys):
            full = jnp.broadcast_to(rows[p : p + 1], (ROWS, wide))
            kron_ref[k, p * ROWS : (p + 1) * ROWS, :] = jnp.where(same, full, 0.0).astype(BF16)
        return carry

    lax.fori_loop(0, chan, one, 0)


def list_pairs(rel_ref, low, high, chan_list, src_list, live_list, dest_list, only=None):
    chan, dests = rel_ref.shape
    place = jnp.int32(0)
    for b in range(dests) if only is None else only:
        for k in range(chan):
            source = rel_ref[k, b]
            chan_list[place] = k
            src_list[place] = source - low
            live_list[place] = 1
            dest_list[place] = b
            place = place + jnp.where((source >= low) & (source < high), 1, 0)
        chan_list[place] = 0
        src_list[place] = 0
        live_list[place] = 0
        dest_list[place] = b
        place = place + lax.rem(place, 2)
    return place // 2


def add_pairs(steps, lists, kron_ref, x_ref, left_ref, right_t_ref, acc_ref, mixed_ref, part_ref):
    chan_list, src_list, live_list, dest_list = lists
    rows = x_ref.shape[1]
    phys = x_ref.shape[2] // LANES

    def mix(s):
        for i in range(2):
            source = src_list[2 * s + i]
            kron = kron_ref[chan_list[2 * s + i]]
            for g in range(rows // (2 * ROWS)):
                halves = []
                for j in range(2):
                    r0 = (2 * g + j) * ROWS
                    halves.append(
                        jnp.concatenate(
                            [
                                x_ref[source, r0 : r0 + ROWS, q * LANES : (q + 1) * LANES]
                                for q in range(phys)
                            ],
                            axis=0,
                        )
                    )
                out = dot(kron, jnp.concatenate(halves, axis=1)).astype(BF16)
                for j in range(2):
                    r0 = (2 * g + j) * ROWS
                    for p in range(phys):
                        mixed_ref[i, r0 : r0 + ROWS, p * LANES : (p + 1) * LANES] = out[
                            p * ROWS : (p + 1) * ROWS, j * LANES : (j + 1) * LANES
                        ]

    def step(s, follow):
        dest = dest_list[2 * s]
        weights = []
        for i in range(2):
            k = chan_list[2 * s + i]
            part = dot(left_ref[k, dest], mixed_ref[i]).astype(BF16)
            for p in range(phys):
                part_ref[p * rows : (p + 1) * rows, i * LANES : (i + 1) * LANES] = part[
                    :, p * LANES : (p + 1) * LANES
                ]
            right = right_t_ref[k, dest]
            if i == 1:
                right = jnp.where(live_list[2 * s + 1] > 0, right, jnp.zeros_like(right))
            weights.append(right)
        if follow:
            mix(s + 1)
        image = dot(part_ref[...], jnp.concatenate(weights, axis=0))
        for p in range(phys):
            acc_ref[dest, :, p * LANES : (p + 1) * LANES] += image[p * rows : (p + 1) * rows]

    def middle(s, carry):
        step(s, True)
        return carry

    @pl.when(steps > 0)
    def _():
        mix(0)
        lax.fori_loop(0, steps - 1, middle, 0)
        step(steps - 1, False)


def fold(values):
    total = values[:, :LANES]
    for p in range(1, values.shape[1] // LANES):
        total = total + values[:, p * LANES : (p + 1) * LANES]
    return total


def row_loop(blocks, rows, body, count, first=0):
    zeros = tuple(jnp.zeros((CHUNK, LANES), F32) for _ in range(count))
    per = rows // CHUNK

    def step(n, carry):
        start = pl.multiple_of(lax.rem(n, per) * CHUNK, CHUNK)
        return body(first + n // per, pl.ds(start, CHUNK), start, carry)

    return lax.fori_loop(0, blocks * per, step, zeros)


def kept_rows(rank, start):
    row = start + lax.broadcasted_iota(jnp.int32, (CHUNK, LANES), 0)
    return (row < rank).astype(F32)


def put_sums(out_ref, values, first=0):
    for n, value in enumerate(values):
        out_ref[first + n : first + n + 1, :] = jnp.full((1, LANES), 1.0, F32) * jnp.sum(value)


def common_shift(mine_ref, theirs_ref):
    num = mine_ref[0:1, :] + theirs_ref[0:1, :]
    den = mine_ref[1:2, :] + theirs_ref[1:2, :]
    return jnp.where(den > 0, num / jnp.where(den > 0, den, 1.0), 0.0)


def cut(b, x_ref, out_ref):
    out_ref[0] = x_ref[b]


def first_local(
    rel_ref, ops_ref, x_ref, left_ref, right_ref,
    kron_ref, right_t_ref, image_ref, sums_ref,
    mixed_ref, part_ref, chan_list, src_list, live_list, dest_list, spread_ref, fetched_ref, sem,
):
    lists = (chan_list, src_list, live_list, dest_list)
    fetch = pltpu.make_async_copy(right_ref, fetched_ref, sem)
    fetch.start()
    make_kron(ops_ref, kron_ref, spread_ref)
    chan, dests = left_ref.shape[:2]
    fetch.wait()

    def turn(n, carry):
        for k in range(2):
            for b in range(dests):
                right_t_ref[2 * n + k, b] = fetched_ref[2 * n + k, b].T
        return carry

    lax.fori_loop(0, chan // 2, turn, 0)
    image_ref[...] = jnp.zeros_like(image_ref)
    steps = list_pairs(rel_ref, 0, dests, *lists)
    add_pairs(steps, lists, kron_ref, x_ref, left_ref, right_t_ref, image_ref, mixed_ref, part_ref)

    def sums(b, r, start, carry):
        x = x_ref[b, r, :].astype(F32)
        return carry[0] + fold(x * image_ref[b, r, :]), carry[1] + fold(x * x)

    totals = row_loop(dests, x_ref.shape[1], sums, 2)
    sums_ref[...] = jnp.zeros_like(sums_ref)
    put_sums(sums_ref, totals)


def local_sources(
    rel_ref, kron_ref, x_ref, left_ref, right_t_ref,
    acc_ref,
    mixed_ref, part_ref, *lists,
):
    acc_ref[...] = jnp.zeros_like(acc_ref)
    steps = list_pairs(rel_ref, 0, left_ref.shape[1], *lists)
    add_pairs(steps, lists, kron_ref, x_ref, left_ref, right_t_ref, acc_ref, mixed_ref, part_ref)


def first_remote(
    rel_ref, kron_ref, other_ref, left_ref, right_t_ref, before_ref, local_sums_ref,
    acc_ref, sums_ref,
    mixed_ref, part_ref, *lists,
):
    dests = left_ref.shape[1]
    sums_ref[...] = local_sums_ref[...]
    steps = list_pairs(rel_ref, dests, dests + 1, *lists)
    add_pairs(steps, lists, kron_ref, other_ref, left_ref, right_t_ref, acc_ref, mixed_ref, part_ref)


def first_finish(
    dest, rel_ref, kron_ref, other_ref, left_ref, right_t_ref, before_ref, x_ref, mine_ref,
    theirs_ref, *refs,
):
    dests = left_ref.shape[1]
    last = dest == dests - 1
    if last:
        earlier_ref, acc_ref, guess_ref, all_ref = refs[:4]
        all_ref[0:dest] = earlier_ref[...]
    else:
        acc_ref, guess_ref = refs[:2]
    mixed_ref, part_ref = refs[-6:-4]
    lists = refs[-4:]
    steps = list_pairs(rel_ref, dests + 1, 2 * dests, *lists, only=(dest,))
    add_pairs(steps, lists, kron_ref, other_ref, left_ref, right_t_ref, acc_ref, mixed_ref, part_ref)
    shift = common_shift(mine_ref, theirs_ref)
    keep_state = jnp.tile(1.0 + STEP_SIZE * shift, (1, x_ref.shape[2] // LANES))

    def update(b, r, start, carry):
        x = x_ref[b, r, :].astype(F32)
        guess = (keep_state * x - STEP_SIZE * acc_ref[b, r, :]).astype(BF16)
        guess_ref[0, r, :] = guess
        if last:
            all_ref[b, r, :] = guess
        return carry

    row_loop(1, x_ref.shape[1], update, 0, first=dest)


def second_remote(
    rel_ref, rank_ref, kron_ref, other_ref, left_ref, right_t_ref, before_ref, x_ref, image_ref,
    guess_ref,
    acc_ref, sums_ref,
    mixed_ref, part_ref, *lists,
):
    dests, rows, _ = x_ref.shape
    steps = list_pairs(rel_ref, dests, dests + 1, *lists)
    add_pairs(steps, lists, kron_ref, other_ref, left_ref, right_t_ref, acc_ref, mixed_ref, part_ref)

    def sums(b, r, start, carry):
        x = x_ref[b, r, :].astype(F32)
        guess = guess_ref[b, r, :].astype(F32)
        image = image_ref[b, r, :]
        keep = kept_rows(rank_ref[b], start)
        xx, xg, gg = fold(x * x), fold(x * guess), fold(guess * guess)
        new = (fold(x * image), xx, fold(guess * image), xg, gg, keep * gg, keep * xx, keep * xg)
        return tuple(total + value for total, value in zip(carry, new))

    put_sums(sums_ref, row_loop(dests, rows, sums, 8))


def second_finish(
    rel_ref, rank_ref, kron_ref, other_ref, left_ref, right_t_ref, before_ref, x_ref, guess_ref,
    mine_ref, theirs_ref, early_ref,
    kept_ref, sums_ref,
    mixed_ref, part_ref, *lists,
):
    dests, rows, width = x_ref.shape
    steps = list_pairs(rel_ref, dests + 1, 2 * dests, *lists)
    add_pairs(steps, lists, kron_ref, other_ref, left_ref, right_t_ref, kept_ref, mixed_ref, part_ref)
    shift = common_shift(mine_ref, theirs_ref)
    keep_guess = jnp.tile(1.0 + STEP_SIZE * shift, (1, width // LANES))

    def sums(b, r, start, carry):
        x = x_ref[b, r, :].astype(F32)
        guess = guess_ref[b, r, :].astype(F32)
        kept = keep_guess * guess - STEP_SIZE * kept_ref[b, r, :]
        kept_ref[b, r, :] = kept
        keep = kept_rows(rank_ref[b], start)
        kg, kx = fold(kept * guess), fold(kept * x)
        new = (kg, kx, keep * kg, keep * kx, keep * fold(kept * kept))
        return tuple(total + value for total, value in zip(carry, new))

    totals = row_loop(dests, rows, sums, 5)
    sums_ref[0:8, :] = early_ref[...]
    put_sums(sums_ref, totals, first=8)
    sums_ref[13:16, :] = jnp.zeros((3, LANES), F32)


def normalize(
    cells, rank_ref, kept_ref, guess_ref, x_ref, mine_ref, theirs_ref, my_sums_ref, their_sums_ref,
    state_ref, turned_ref,
):
    both = my_sums_ref[...] + their_sums_ref[...]
    xv, xx, gv, xg, gg, gg_kept, xx_kept, xg_kept, kg, kx, kg_kept, kx_kept, kk_kept = (
        both[n : n + 1] for n in range(13)
    )
    shift = common_shift(mine_ref, theirs_ref)
    delta = STEP_SIZE * (xv / xx - shift)
    scale = (1.0 + STEP_SIZE * shift) / STEP_SIZE
    gw, xw = scale * gg - kg / STEP_SIZE, scale * xg - kx / STEP_SIZE
    num = gw + delta * (xw + gv + delta * xv)
    den = gg + delta * (2.0 * xg + delta * xx)
    beta = STEP_SIZE * (num / den - shift)
    of_guess, of_state = beta + delta, beta * delta
    norm = (
        kk_kept
        + of_guess * (2.0 * kg_kept + of_guess * gg_kept)
        + of_state * (2.0 * kx_kept + of_state * xx_kept + 2.0 * of_guess * xg_kept)
    )
    gain = jnp.sqrt(cells / (jnp.maximum(norm, 0.0) + EPSILON))
    blocks, rows, width = kept_ref.shape
    group = 8 * LANES
    per = width // group
    row = lax.broadcasted_iota(jnp.int32, (rows, LANES), 0)

    def one(n, carry):
        b = n // per
        factor = jnp.where(row < rank_ref[b], gain, 0.0)
        for p in range(8):
            cols = pl.ds(pl.multiple_of(lax.rem(n, per) * group + p * LANES, LANES), LANES)
            kept = (
                kept_ref[b, :, cols]
                + of_guess * guess_ref[b, :, cols].astype(F32)
                + of_state * x_ref[b, :, cols].astype(F32)
            )
            state = (kept * factor).astype(BF16)
            state_ref[b, :, cols] = state
            turned_ref[b, :, cols] = state.T
        return carry

    lax.fori_loop(0, blocks * per, one, 0)


def environments(first, count, scale, env_ref, inner_ref, outer_ref, out_ref, mid_ref):
    dests, rows, width = outer_ref.shape
    phys = width // LANES
    pairs = mid_ref.shape[0] // dests

    def step(n, carry):
        for j in range(pairs):
            k = first + 2 * (n * pairs + j)
            for b in range(dests):
                env = jnp.concatenate([env_ref[k, b], env_ref[k + 1, b]], axis=0)
                mid = dot(env, inner_ref[b]).astype(BF16)
                for p in range(phys):
                    for i in range(2):
                        mid_ref[
                            j * dests + b, p * rows : (p + 1) * rows, i * LANES : (i + 1) * LANES
                        ] = mid[i * rows : (i + 1) * rows, p * LANES : (p + 1) * LANES]
        for j in range(pairs):
            place = 2 * (n * pairs + j)
            for b in range(dests):
                out = (dot(outer_ref[b], mid_ref[j * dests + b]) * scale).astype(BF16)
                out_ref[place, b] = out[:, :LANES]
                out_ref[place + 1, b] = out[:, LANES:]
        return carry

    lax.fori_loop(0, count // (2 * pairs), step, 0)


def normalize_and_left(
    first, count, scale, cells,
    rank_ref, kept_ref, guess_ref, x_ref, mine_ref, theirs_ref, my_sums_ref, their_sums_ref, env_ref,
    new_ref, state_ref, turned_ref, out_ref,
    mid_ref, sem,
):
    normalize(
        cells, rank_ref, kept_ref, guess_ref, x_ref, mine_ref, theirs_ref, my_sums_ref,
        their_sums_ref, state_ref, turned_ref,
    )
    copy = pltpu.make_async_copy(state_ref, new_ref, sem)
    copy.start()
    environments(first, count, scale, env_ref, state_ref, turned_ref, out_ref, mid_ref)
    copy.wait()


def widen(places, *refs):
    pieces, (outs, wides, sems) = refs[: len(places)], (refs[-5:-3], refs[-3:-1], refs[-1])
    copies = []
    for piece, (side, begin) in zip(pieces, places):
        for n in range(0, piece.shape[0], 2):
            span = pl.ds(begin + n, 2)
            wides[side][begin + n : begin + n + 2] = piece[n : n + 2].astype(F32)
            copy = pltpu.make_async_copy(
                wides[side].at[span], outs[side].at[span], sems.at[len(copies)]
            )
            copy.start()
            copies.append(copy)
    for copy in copies:
        copy.wait()


def shards(state, left_env, right_env, site_ops, sector_map, ranks):
    dests, rows, width = state.shape[1:]
    chan, phys = site_ops.shape[1:3]
    groups = lax.axis_size("blk")
    total_blocks = groups * dests
    first_block = lax.axis_index("blk") * dests
    x, left, right, ops = state[0], left_env[0], right_env[0], site_ops[0]
    local_map = lax.dynamic_slice_in_dim(sector_map[0], first_block, dests, 1)
    rel = lax.rem(local_map - first_block + total_blocks, total_blocks)

    swap = [(g, groups - 1 - g) for g in range(groups)]

    def trade(value):
        return lax.ppermute(value, "blk", swap)

    def shape(dims, kind):
        return jax.ShapeDtypeStruct(dims, kind)

    wave = (dests, rows, width)
    wave_f32 = shape(wave, F32)
    wave_b16 = shape(wave, BF16)
    sums_kind = shape((8, LANES), F32)
    lists = [pltpu.SMEM((chan * dests + 2 * dests + 1,), jnp.int32)] * 4
    pair_scratch = [
        pltpu.VMEM((2, rows, width), BF16), pltpu.VMEM((phys * rows, 2 * LANES), BF16)
    ] + lists

    def call(body, specs, outs, scratch, *args, aliases={}):
        return pl.pallas_call(
            body,
            in_specs=specs,
            out_specs=jax.tree.map(lambda _: VMEM, outs),
            out_shape=outs,
            scratch_shapes=scratch,
            compiler_params=PARAMS,
            cost_estimate=COST,
            input_output_aliases=aliases,
        )(*args)

    block = shape((1, rows, width), BF16)
    own = [
        call(functools.partial(cut, b), [VMEM], block, [], x) for b in range(dests)
    ]
    other = [trade(value) for value in own]
    kron, right_t, image, mine = call(
        first_local, [SMEM] + [VMEM] * 3 + [HBM],
        (shape((chan, phys * ROWS, phys * ROWS), BF16), shape(right.shape, BF16), wave_f32, sums_kind),
        pair_scratch
        + [
            pltpu.VMEM((chan * phys, phys * ROWS), F32),
            pltpu.VMEM(right.shape, BF16),
            pltpu.SemaphoreType.DMA,
        ],
        rel, ops, x, left, right,
    )
    image, mine = call(
        first_remote, [SMEM] + [VMEM] * 6, (wave_f32, sums_kind), pair_scratch,
        rel, kron, other[0], left, right_t, image, mine, aliases={5: 0},
    )
    theirs = trade(mine)
    image, first_guess = call(
        functools.partial(first_finish, 0), [SMEM] + [VMEM] * 8,
        (wave_f32, block), pair_scratch,
        rel, kron, other[1], left, right_t, image, x, mine, theirs, aliases={5: 0},
    )
    image, last_guess, guess = call(
        functools.partial(first_finish, 1), [SMEM] + [VMEM] * 9,
        (wave_f32, block, wave_b16), pair_scratch,
        rel, kron, other[1], left, right_t, image, x, mine, theirs, first_guess, aliases={5: 0},
    )
    other = [trade(first_guess), trade(last_guess)]
    acc = call(
        local_sources, [SMEM] + [VMEM] * 4, wave_f32, pair_scratch,
        rel, kron, guess, left, right_t,
    )
    acc, early_sums = call(
        second_remote, [SMEM] * 2 + [VMEM] * 8, (wave_f32, sums_kind), pair_scratch,
        rel, ranks[0], kron, other[0], left, right_t, acc, x, image, guess, aliases={6: 0},
    )
    kept, my_sums = call(
        second_finish, [SMEM] * 2 + [VMEM] * 10, (wave_f32, shape((16, LANES), F32)), pair_scratch,
        rel, ranks[0], kron, other[1], left, right_t, acc, x, guess, mine, theirs, early_sums,
        aliases={6: 0},
    )
    their_sums = trade(my_sums)

    env_scale = 1.0 / math.sqrt(phys * rows)
    cells = float(total_blocks * rows * width)
    early, later = 8, 8

    def mid(count):
        pairs = next(n for n in (2, 3, 1) if count % (2 * n) == 0)
        return [pltpu.VMEM((pairs * dests, width, 2 * LANES), BF16)]

    def sent(value, steps):
        count = lax.axis_size("seg")
        begin, end = max(0, -steps), min(count, count - steps)
        return lax.ppermute(value, "seg", [(s, s + steps) for s in range(begin, end)])

    def env_kind(count):
        return shape((count,) + left.shape[1:], BF16)

    def env_call(begin, count, env, inner, outer):
        return call(
            functools.partial(environments, begin, count, env_scale),
            [VMEM] * 3, env_kind(count), mid(count), env, inner, outer,
        )

    new_state, state_kept, turned, piece = pl.pallas_call(
        functools.partial(normalize_and_left, 0, early, env_scale, cells),
        in_specs=[SMEM] + [VMEM] * 8,
        out_specs=(HBM, VMEM, VMEM, VMEM),
        out_shape=(wave_b16, wave_b16, wave_b16, env_kind(early)),
        scratch_shapes=mid(early) + [pltpu.SemaphoreType.DMA],
        compiler_params=PARAMS,
        cost_estimate=COST,
    )(ranks[0], kept, guess, x, mine, theirs, my_sums, their_sums, left)
    pieces = [
        sent(piece, 1),
        sent(env_call(0, later, right, turned, state_kept), -1),
        sent(env_call(early, chan - early, left, state_kept, turned), 1),
        sent(env_call(later, chan - later, right, turned, state_kept), -1),
    ]
    env_f32 = shape(left.shape, F32)

    def widened(places, values, filled):
        count = len(values)
        return pl.pallas_call(
            functools.partial(widen, places),
            in_specs=[VMEM] * count + [HBM] * len(filled),
            out_specs=(HBM, HBM),
            out_shape=(env_f32, env_f32),
            input_output_aliases={count + n: n for n in range(len(filled))},
            scratch_shapes=[pltpu.VMEM(left.shape, F32)] * 2 + [pltpu.SemaphoreType.DMA((chan,))],
            compiler_params=PARAMS,
            cost_estimate=COST,
        )(*values, *filled)

    filled = widened(((0, 0),), pieces[:1], ())
    filled = widened(((1, 0),), pieces[1:2], filled)
    received_left, received_right = widened(((0, early), (1, later)), pieces[2:], filled)
    return (new_state[None], received_left[None], received_right[None])


def solution(mesh):
    placed = (
        P("seg", "blk", None, None),
        P("seg", None, "blk", None, None),
        P("seg", None, "blk", None, None),
        P("seg", None, None, None),
        P("seg", None, None),
        P("seg", "blk"),
    )
    return jax.shard_map(
        shards,
        mesh=mesh,
        in_specs=placed,
        out_specs=(
            P("seg", "blk", None, None),
            P("seg", None, "blk", None, None),
            P("seg", None, "blk", None, None),
        ),
        check_vma=False,
    )
```

```python
import functools
import math

import jax
import jax.numpy as jnp
from jax import lax
from jax.experimental import pallas as pl
from jax.experimental.pallas import tpu as pltpu
from jax.sharding import PartitionSpec as P

STEP_SIZE = 0.25
EPSILON = 1e-06
LANES = 128
ROWS = 16
CHUNK = 32
F32 = jnp.float32
BF16 = jnp.bfloat16
VMEM = pl.BlockSpec(memory_space=pltpu.VMEM)
HBM = pl.BlockSpec(memory_space=pltpu.HBM)
SMEM = pl.BlockSpec(memory_space=pltpu.SMEM)
COST = pl.CostEstimate(flops=1024, bytes_accessed=1024, transcendentals=0)
PARAMS = pltpu.CompilerParams(vmem_limit_bytes=32 * 1024 * 1024)


def dot(left, right):
    return lax.dot_general(
        left, right, (((1,), (0,)), ((), ())), preferred_element_type=F32
    )


def make_kron(ops_ref, kron_ref, spread_ref):
    chan, phys, _ = ops_ref.shape
    wide = phys * ROWS
    columns = lax.broadcasted_iota(jnp.int32, (phys, wide), 1)
    spread = (columns // ROWS == lax.broadcasted_iota(jnp.int32, (phys, wide), 0)).astype(F32)
    spread_ref[...] = dot(ops_ref[...].reshape(chan * phys, phys), spread.astype(BF16))
    same = lax.broadcasted_iota(jnp.int32, (ROWS, wide), 1) % ROWS == lax.broadcasted_iota(
        jnp.int32, (ROWS, wide), 0
    )

    def one(k, carry):
        rows = spread_ref[pl.ds(pl.multiple_of(k * phys, phys), phys), :]
        for p in range(phys):
            full = jnp.broadcast_to(rows[p : p + 1], (ROWS, wide))
            kron_ref[k, p * ROWS : (p + 1) * ROWS, :] = jnp.where(same, full, 0.0).astype(BF16)
        return carry

    lax.fori_loop(0, chan, one, 0)


def list_pairs(rel_ref, low, high, chan_list, src_list, live_list, dest_list, only=None):
    chan, dests = rel_ref.shape
    place = jnp.int32(0)
    for b in range(dests) if only is None else only:
        for k in range(chan):
            source = rel_ref[k, b]
            chan_list[place] = k
            src_list[place] = source - low
            live_list[place] = 1
            dest_list[place] = b
            place = place + jnp.where((source >= low) & (source < high), 1, 0)
        chan_list[place] = 0
        src_list[place] = 0
        live_list[place] = 0
        dest_list[place] = b
        place = place + lax.rem(place, 2)
    return place // 2


def add_pairs(steps, lists, kron_ref, x_ref, left_ref, right_t_ref, acc_ref, mixed_ref, part_ref):
    chan_list, src_list, live_list, dest_list = lists
    rows = x_ref.shape[1]
    phys = x_ref.shape[2] // LANES

    def mix(s):
        for i in range(2):
            source = src_list[2 * s + i]
            kron = kron_ref[chan_list[2 * s + i]]
            for g in range(rows // (2 * ROWS)):
                halves = []
                for j in range(2):
                    r0 = (2 * g + j) * ROWS
                    halves.append(
                        jnp.concatenate(
                            [
                                x_ref[source, r0 : r0 + ROWS, q * LANES : (q + 1) * LANES]
                                for q in range(phys)
                            ],
                            axis=0,
                        )
                    )
                out = dot(kron, jnp.concatenate(halves, axis=1)).astype(BF16)
                for j in range(2):
                    r0 = (2 * g + j) * ROWS
                    for p in range(phys):
                        mixed_ref[i, r0 : r0 + ROWS, p * LANES : (p + 1) * LANES] = out[
                            p * ROWS : (p + 1) * ROWS, j * LANES : (j + 1) * LANES
                        ]

    def step(s, follow):
        dest = dest_list[2 * s]
        weights = []
        for i in range(2):
            k = chan_list[2 * s + i]
            part = dot(left_ref[k, dest], mixed_ref[i]).astype(BF16)
            for p in range(phys):
                part_ref[p * rows : (p + 1) * rows, i * LANES : (i + 1) * LANES] = part[
                    :, p * LANES : (p + 1) * LANES
                ]
            right = right_t_ref[k, dest]
            if i == 1:
                right = jnp.where(live_list[2 * s + 1] > 0, right, jnp.zeros_like(right))
            weights.append(right)
        if follow:
            mix(s + 1)
        image = dot(part_ref[...], jnp.concatenate(weights, axis=0))
        for p in range(phys):
            acc_ref[dest, :, p * LANES : (p + 1) * LANES] += image[p * rows : (p + 1) * rows]

    def double(n, carry):
        step(2 * n, True)
        step(2 * n + 1, True)
        return carry

    @pl.when(steps > 0)
    def _():
        mix(0)
        lax.fori_loop(0, (steps - 1) // 2, double, 0)

    @pl.when(lax.rem(steps, 2) == 1)
    def _():
        step(steps - 1, False)

    @pl.when((steps > 0) & (lax.rem(steps, 2) == 0))
    def _():
        step(steps - 2, True)
        step(steps - 1, False)


def fold(values):
    total = values[:, :LANES]
    for p in range(1, values.shape[1] // LANES):
        total = total + values[:, p * LANES : (p + 1) * LANES]
    return total


def row_loop(blocks, rows, body, count, first=0):
    zeros = tuple(jnp.zeros((CHUNK, LANES), F32) for _ in range(count))
    per = rows // CHUNK

    def step(n, carry):
        start = pl.multiple_of(lax.rem(n, per) * CHUNK, CHUNK)
        return body(first + n // per, pl.ds(start, CHUNK), start, carry)

    return lax.fori_loop(0, blocks * per, step, zeros)


def kept_rows(rank, start):
    row = start + lax.broadcasted_iota(jnp.int32, (CHUNK, LANES), 0)
    return (row < rank).astype(F32)


def put_sums(out_ref, values, first=0):
    for n, value in enumerate(values):
        out_ref[first + n : first + n + 1, :] = jnp.full((1, LANES), 1.0, F32) * jnp.sum(value)


def common_shift(mine_ref, theirs_ref):
    num = mine_ref[0:1, :] + theirs_ref[0:1, :]
    den = mine_ref[1:2, :] + theirs_ref[1:2, :]
    return jnp.where(den > 0, num / jnp.where(den > 0, den, 1.0), 0.0)


def cut(x_ref, *out_refs):
    for b, out_ref in enumerate(out_refs):
        out_ref[0] = x_ref[b]


def first_local(
    rel_ref, kron_ref, x_ref, left_ref, right_ref,
    right_t_ref, image_ref, sums_ref,
    mixed_ref, part_ref, *lists,
):
    chan, dests = left_ref.shape[:2]

    def turn(n, carry):
        for k in range(2):
            for b in range(dests):
                right_t_ref[2 * n + k, b] = right_ref[2 * n + k, b].T
        return carry

    lax.fori_loop(0, chan // 2, turn, 0)
    image_ref[...] = jnp.zeros_like(image_ref)
    steps = list_pairs(rel_ref, 0, dests, *lists)
    add_pairs(steps, lists, kron_ref, x_ref, left_ref, right_t_ref, image_ref, mixed_ref, part_ref)

    def sums(b, r, start, carry):
        x = x_ref[b, r, :].astype(F32)
        return carry[0] + fold(x * image_ref[b, r, :]), carry[1] + fold(x * x)

    totals = row_loop(dests, x_ref.shape[1], sums, 2)
    sums_ref[...] = jnp.zeros_like(sums_ref)
    put_sums(sums_ref, totals)


def local_sources(
    rel_ref, kron_ref, x_ref, left_ref, right_t_ref,
    acc_ref,
    mixed_ref, part_ref, *lists,
):
    acc_ref[...] = jnp.zeros_like(acc_ref)
    steps = list_pairs(rel_ref, 0, left_ref.shape[1], *lists)
    add_pairs(steps, lists, kron_ref, x_ref, left_ref, right_t_ref, acc_ref, mixed_ref, part_ref)


def first_remote(
    rel_ref, kron_ref, other_ref, left_ref, right_t_ref, before_ref, local_sums_ref,
    acc_ref, sums_ref,
    mixed_ref, part_ref, *lists,
):
    dests = left_ref.shape[1]
    sums_ref[...] = local_sums_ref[...]
    steps = list_pairs(rel_ref, dests, dests + 1, *lists)
    add_pairs(steps, lists, kron_ref, other_ref, left_ref, right_t_ref, acc_ref, mixed_ref, part_ref)


def first_finish(
    dest, rel_ref, kron_ref, other_ref, left_ref, right_t_ref, before_ref, x_ref, mine_ref,
    theirs_ref, *refs,
):
    dests = left_ref.shape[1]
    last = dest == dests - 1
    if last:
        earlier_ref, acc_ref, guess_ref, all_ref = refs[:4]
        all_ref[0:dest] = earlier_ref[...]
    else:
        acc_ref, guess_ref = refs[:2]
    mixed_ref, part_ref = refs[-6:-4]
    lists = refs[-4:]
    steps = list_pairs(rel_ref, dests + 1, 2 * dests, *lists, only=(dest,))
    add_pairs(steps, lists, kron_ref, other_ref, left_ref, right_t_ref, acc_ref, mixed_ref, part_ref)
    shift = common_shift(mine_ref, theirs_ref)
    keep_state = jnp.tile(1.0 + STEP_SIZE * shift, (1, x_ref.shape[2] // LANES))

    def update(b, r, start, carry):
        x = x_ref[b, r, :].astype(F32)
        guess = (keep_state * x - STEP_SIZE * acc_ref[b, r, :]).astype(BF16)
        guess_ref[0, r, :] = guess
        if last:
            all_ref[b, r, :] = guess
        return carry

    row_loop(1, x_ref.shape[1], update, 0, first=dest)


def second_remote(
    rel_ref, rank_ref, kron_ref, other_ref, left_ref, right_t_ref, before_ref, x_ref, image_ref,
    guess_ref,
    acc_ref, sums_ref,
    mixed_ref, part_ref, *lists,
):
    dests, rows, _ = x_ref.shape
    steps = list_pairs(rel_ref, dests, dests + 1, *lists)
    add_pairs(steps, lists, kron_ref, other_ref, left_ref, right_t_ref, acc_ref, mixed_ref, part_ref)

    def sums(b, r, start, carry):
        x = x_ref[b, r, :].astype(F32)
        guess = guess_ref[b, r, :].astype(F32)
        image = image_ref[b, r, :]
        keep = kept_rows(rank_ref[b], start)
        xx, xg, gg = fold(x * x), fold(x * guess), fold(guess * guess)
        new = (fold(x * image), xx, fold(guess * image), xg, gg, keep * gg, keep * xx, keep * xg)
        return tuple(total + value for total, value in zip(carry, new))

    put_sums(sums_ref, row_loop(dests, rows, sums, 8))


def second_finish(
    rel_ref, rank_ref, kron_ref, other_ref, left_ref, right_t_ref, before_ref, x_ref, guess_ref,
    mine_ref, theirs_ref, early_ref,
    kept_ref, sums_ref,
    mixed_ref, part_ref, *lists,
):
    dests, rows, width = x_ref.shape
    steps = list_pairs(rel_ref, dests + 1, 2 * dests, *lists)
    add_pairs(steps, lists, kron_ref, other_ref, left_ref, right_t_ref, kept_ref, mixed_ref, part_ref)
    shift = common_shift(mine_ref, theirs_ref)
    keep_guess = jnp.tile(1.0 + STEP_SIZE * shift, (1, width // LANES))

    def sums(b, r, start, carry):
        x = x_ref[b, r, :].astype(F32)
        guess = guess_ref[b, r, :].astype(F32)
        kept = keep_guess * guess - STEP_SIZE * kept_ref[b, r, :]
        kept_ref[b, r, :] = kept
        keep = kept_rows(rank_ref[b], start)
        kg, kx = fold(kept * guess), fold(kept * x)
        new = (kg, kx, keep * kg, keep * kx, keep * fold(kept * kept))
        return tuple(total + value for total, value in zip(carry, new))

    totals = row_loop(dests, rows, sums, 5)
    sums_ref[0:8, :] = early_ref[...]
    put_sums(sums_ref, totals, first=8)
    sums_ref[13:16, :] = jnp.zeros((3, LANES), F32)


def normalize(
    cells, rank_ref, kept_ref, guess_ref, x_ref, mine_ref, theirs_ref, my_sums_ref, their_sums_ref,
    state_ref, turned_ref,
):
    both = my_sums_ref[...] + their_sums_ref[...]
    xv, xx, gv, xg, gg, gg_kept, xx_kept, xg_kept, kg, kx, kg_kept, kx_kept, kk_kept = (
        both[n : n + 1] for n in range(13)
    )
    shift = common_shift(mine_ref, theirs_ref)
    delta = STEP_SIZE * (xv / xx - shift)
    scale = (1.0 + STEP_SIZE * shift) / STEP_SIZE
    gw, xw = scale * gg - kg / STEP_SIZE, scale * xg - kx / STEP_SIZE
    num = gw + delta * (xw + gv + delta * xv)
    den = gg + delta * (2.0 * xg + delta * xx)
    beta = STEP_SIZE * (num / den - shift)
    of_guess, of_state = beta + delta, beta * delta
    norm = (
        kk_kept
        + of_guess * (2.0 * kg_kept + of_guess * gg_kept)
        + of_state * (2.0 * kx_kept + of_state * xx_kept + 2.0 * of_guess * xg_kept)
    )
    gain = jnp.sqrt(cells / (jnp.maximum(norm, 0.0) + EPSILON))
    blocks, rows, width = kept_ref.shape
    group = 8 * LANES
    per = width // group
    row = lax.broadcasted_iota(jnp.int32, (rows, LANES), 0)

    def one(n, carry):
        b = n // per
        factor = jnp.where(row < rank_ref[b], gain, 0.0)
        for p in range(8):
            cols = pl.ds(pl.multiple_of(lax.rem(n, per) * group + p * LANES, LANES), LANES)
            kept = (
                kept_ref[b, :, cols]
                + of_guess * guess_ref[b, :, cols].astype(F32)
                + of_state * x_ref[b, :, cols].astype(F32)
            )
            state = (kept * factor).astype(BF16)
            state_ref[b, :, cols] = state
            turned_ref[b, :, cols] = state.T
        return carry

    lax.fori_loop(0, blocks * per, one, 0)


def environments(first, count, scale, env_ref, inner_ref, outer_ref, out_ref, mid_ref):
    dests, rows, width = outer_ref.shape
    phys = width // LANES
    pairs = mid_ref.shape[0] // dests

    def step(n, carry):
        for j in range(pairs):
            k = first + 2 * (n * pairs + j)
            for b in range(dests):
                env = jnp.concatenate([env_ref[k, b], env_ref[k + 1, b]], axis=0)
                mid = dot(env, inner_ref[b]).astype(BF16)
                for p in range(phys):
                    for i in range(2):
                        mid_ref[
                            j * dests + b, p * rows : (p + 1) * rows, i * LANES : (i + 1) * LANES
                        ] = mid[i * rows : (i + 1) * rows, p * LANES : (p + 1) * LANES]
        for j in range(pairs):
            place = 2 * (n * pairs + j)
            for b in range(dests):
                out = (dot(outer_ref[b], mid_ref[j * dests + b]) * scale).astype(BF16)
                out_ref[place, b] = out[:, :LANES]
                out_ref[place + 1, b] = out[:, LANES:]
        return carry

    lax.fori_loop(0, count // (2 * pairs), step, 0)


def both_environments(
    first, count, scale, left_ref, right_ref, state_ref, turned_ref, out_left_ref, out_right_ref, mid_ref
):
    environments(first, count, scale, left_ref, state_ref, turned_ref, out_left_ref, mid_ref)
    environments(first, count, scale, right_ref, turned_ref, state_ref, out_right_ref, mid_ref)


def normalize_and_left(
    first, count, scale, cells,
    rank_ref, kept_ref, guess_ref, x_ref, mine_ref, theirs_ref, my_sums_ref, their_sums_ref, env_ref,
    new_ref, state_ref, turned_ref, out_ref,
    mid_ref, sem,
):
    normalize(
        cells, rank_ref, kept_ref, guess_ref, x_ref, mine_ref, theirs_ref, my_sums_ref,
        their_sums_ref, state_ref, turned_ref,
    )
    copy = pltpu.make_async_copy(state_ref, new_ref, sem)
    copy.start()
    environments(first, count, scale, env_ref, state_ref, turned_ref, out_ref, mid_ref)
    copy.wait()


def widen(places, *refs):
    pieces, (outs, wides, sems) = refs[: len(places)], (refs[-5:-3], refs[-3:-1], refs[-1])
    copies = []
    for piece, (side, begin) in zip(pieces, places):
        for n in range(0, piece.shape[0], 2):
            span = pl.ds(begin + n, 2)
            wides[side][begin + n : begin + n + 2] = piece[n : n + 2].astype(F32)
            copy = pltpu.make_async_copy(
                wides[side].at[span], outs[side].at[span], sems.at[len(copies)]
            )
            copy.start()
            copies.append(copy)
    for copy in copies:
        copy.wait()


def shards(state, left_env, right_env, site_ops, sector_map, ranks):
    dests, rows, width = state.shape[1:]
    chan, phys = site_ops.shape[1:3]
    groups = lax.axis_size("blk")
    total_blocks = groups * dests
    first_block = lax.axis_index("blk") * dests
    x, left, right, ops = state[0], left_env[0], right_env[0], site_ops[0]
    local_map = lax.dynamic_slice_in_dim(sector_map[0], first_block, dests, 1)
    rel = lax.rem(local_map - first_block + total_blocks, total_blocks)

    swap = [(g, groups - 1 - g) for g in range(groups)]

    def trade(value):
        return lax.ppermute(value, "blk", swap)

    def shape(dims, kind):
        return jax.ShapeDtypeStruct(dims, kind)

    wave = (dests, rows, width)
    wave_f32 = shape(wave, F32)
    wave_b16 = shape(wave, BF16)
    sums_kind = shape((8, LANES), F32)
    lists = [pltpu.SMEM((chan * dests + 2 * dests + 1,), jnp.int32)] * 4
    pair_scratch = [
        pltpu.VMEM((2, rows, width), BF16), pltpu.VMEM((phys * rows, 2 * LANES), BF16)
    ] + lists

    def call(body, specs, outs, scratch, *args, aliases={}):
        return pl.pallas_call(
            body,
            in_specs=specs,
            out_specs=jax.tree.map(lambda _: VMEM, outs),
            out_shape=outs,
            scratch_shapes=scratch,
            compiler_params=PARAMS,
            cost_estimate=COST,
            input_output_aliases=aliases,
        )(*args)

    block = shape((1, rows, width), BF16)
    own = call(cut, [VMEM], (block,) * dests, [], x)
    other = [trade(value) for value in own]
    kron = call(
        make_kron, [VMEM], shape((chan, phys * ROWS, phys * ROWS), BF16),
        [pltpu.VMEM((chan * phys, phys * ROWS), F32)], ops,
    )
    right_t, image, mine = call(
        first_local, [SMEM] + [VMEM] * 4,
        (shape(right.shape, BF16), wave_f32, sums_kind), pair_scratch,
        rel, kron, x, left, right,
    )
    image, mine = call(
        first_remote, [SMEM] + [VMEM] * 6, (wave_f32, sums_kind), pair_scratch,
        rel, kron, other[0], left, right_t, image, mine, aliases={5: 0},
    )
    theirs = trade(mine)
    image, first_guess = call(
        functools.partial(first_finish, 0), [SMEM] + [VMEM] * 8,
        (wave_f32, block), pair_scratch,
        rel, kron, other[1], left, right_t, image, x, mine, theirs, aliases={5: 0},
    )
    image, last_guess, guess = call(
        functools.partial(first_finish, 1), [SMEM] + [VMEM] * 9,
        (wave_f32, block, wave_b16), pair_scratch,
        rel, kron, other[1], left, right_t, image, x, mine, theirs, first_guess, aliases={5: 0},
    )
    other = [trade(first_guess), trade(last_guess)]
    acc = call(
        local_sources, [SMEM] + [VMEM] * 4, wave_f32, pair_scratch,
        rel, kron, guess, left, right_t,
    )
    acc, early_sums = call(
        second_remote, [SMEM] * 2 + [VMEM] * 8, (wave_f32, sums_kind), pair_scratch,
        rel, ranks[0], kron, other[0], left, right_t, acc, x, image, guess, aliases={6: 0},
    )
    kept, my_sums = call(
        second_finish, [SMEM] * 2 + [VMEM] * 10, (wave_f32, shape((16, LANES), F32)), pair_scratch,
        rel, ranks[0], kron, other[1], left, right_t, acc, x, guess, mine, theirs, early_sums,
        aliases={6: 0},
    )
    their_sums = trade(my_sums)

    env_scale = 1.0 / math.sqrt(phys * rows)
    cells = float(total_blocks * rows * width)
    early = 10

    def mid(count):
        pairs = next(n for n in (5, 2, 3, 1) if count % (2 * n) == 0)
        return [pltpu.VMEM((pairs * dests, width, 2 * LANES), BF16)]

    def sent(value, steps):
        count = lax.axis_size("seg")
        begin, end = max(0, -steps), min(count, count - steps)
        return lax.ppermute(value, "seg", [(s, s + steps) for s in range(begin, end)])

    def env_kind(count):
        return shape((count,) + left.shape[1:], BF16)

    new_state, state_kept, turned, piece = pl.pallas_call(
        functools.partial(normalize_and_left, 0, early, env_scale, cells),
        in_specs=[SMEM] + [VMEM] * 8,
        out_specs=(HBM, VMEM, VMEM, VMEM),
        out_shape=(wave_b16, wave_b16, wave_b16, env_kind(early)),
        scratch_shapes=mid(early) + [pltpu.SemaphoreType.DMA],
        compiler_params=PARAMS,
        cost_estimate=COST,
    )(ranks[0], kept, guess, x, mine, theirs, my_sums, their_sums, left)
    second = call(
        functools.partial(environments, 0, early, env_scale),
        [VMEM] * 3, env_kind(early), mid(early), right, turned, state_kept,
    )
    rest = call(
        functools.partial(both_environments, early, chan - early, env_scale),
        [VMEM] * 4, (env_kind(chan - early),) * 2, mid(chan - early),
        left, right, state_kept, turned,
    )
    pieces = [sent(piece, 1), sent(second, -1), sent(rest[0], 1), sent(rest[1], -1)]
    env_f32 = shape(left.shape, F32)

    def widened(places, values, filled):
        count = len(values)
        return pl.pallas_call(
            functools.partial(widen, places),
            in_specs=[VMEM] * count + [HBM] * len(filled),
            out_specs=(HBM, HBM),
            out_shape=(env_f32, env_f32),
            input_output_aliases={count + n: n for n in range(len(filled))},
            scratch_shapes=[pltpu.VMEM(left.shape, F32)] * 2 + [pltpu.SemaphoreType.DMA((chan,))],
            compiler_params=PARAMS,
            cost_estimate=COST,
        )(*values, *filled)

    filled = widened(((0, 0),), pieces[:1], ())
    filled = widened(((1, 0),), pieces[1:2], filled)
    received_left, received_right = widened(((0, early), (1, early)), pieces[2:], filled)
    return (new_state[None], received_left[None], received_right[None])


def solution(mesh):
    placed = (
        P("seg", "blk", None, None),
        P("seg", None, "blk", None, None),
        P("seg", None, "blk", None, None),
        P("seg", None, None, None),
        P("seg", None, None),
        P("seg", "blk"),
    )
    return jax.shard_map(
        shards,
        mesh=mesh,
        in_specs=placed,
        out_specs=(
            P("seg", "blk", None, None),
            P("seg", None, "blk", None, None),
            P("seg", None, "blk", None, None),
        ),
        check_vma=False,
    )
```

```python
import functools
import math

import jax
import jax.numpy as jnp
from jax import lax
from jax.experimental import pallas as pl
from jax.experimental.pallas import tpu as pltpu
from jax.sharding import PartitionSpec as P

STEP_SIZE = 0.25
EPSILON = 1e-06
LANES = 128
GROUP = 8
CHUNK = 32
F32 = jnp.float32
BF16 = jnp.bfloat16
VMEM = pl.BlockSpec(memory_space=pltpu.VMEM)
HBM = pl.BlockSpec(memory_space=pltpu.HBM)
SMEM = pl.BlockSpec(memory_space=pltpu.SMEM)
COST = pl.CostEstimate(flops=1024, bytes_accessed=1024, transcendentals=0)
PARAMS = pltpu.CompilerParams(vmem_limit_bytes=32 * 1024 * 1024)


def dot(left, right):
    return lax.dot_general(
        left, right, (((1,), (0,)), ((), ())), preferred_element_type=F32
    )


def make_kron(ops_ref, kron_ref, spread_ref):
    chan, phys, _ = ops_ref.shape
    wide = phys * GROUP
    columns = lax.broadcasted_iota(jnp.int32, (phys, wide), 1)
    spread = (columns // GROUP == lax.broadcasted_iota(jnp.int32, (phys, wide), 0)).astype(F32)
    spread_ref[...] = dot(ops_ref[...].reshape(chan * phys, phys), spread.astype(BF16))
    same = lax.broadcasted_iota(jnp.int32, (GROUP, wide), 1) % GROUP == lax.broadcasted_iota(
        jnp.int32, (GROUP, wide), 0
    )

    def one(k, carry):
        rows = spread_ref[pl.ds(pl.multiple_of(k * phys, phys), phys), :]
        full = [
            jnp.where(same, jnp.broadcast_to(rows[p : p + 1], (GROUP, wide)), 0.0)
            for p in range(phys)
        ]
        kron_ref[k] = jnp.concatenate(full, axis=0).astype(BF16)
        return carry

    lax.fori_loop(0, chan, one, 0)


def list_pairs(rel_ref, low, high, chan_list, src_list, live_list, dest_list, only=None):
    chan, dests = rel_ref.shape
    place = jnp.int32(0)
    for b in range(dests) if only is None else only:
        for source in range(low, high):
            for k in range(chan):
                chan_list[place] = k
                src_list[place] = source - low
                live_list[place] = 1
                dest_list[place] = b
                place = place + jnp.where(rel_ref[k, b] == source, 1, 0)
            chan_list[place] = 0
            src_list[place] = source - low
            live_list[place] = 0
            dest_list[place] = b
            place = place + lax.rem(place, 2)
    return place // 2


def add_pairs(steps, lists, kron_ref, x_ref, left_ref, right_t_ref, acc_ref, turned_ref, mixed_ref):
    chan_list, src_list, live_list, dest_list = lists
    rows = x_ref.shape[1]
    phys = x_ref.shape[2] // LANES
    groups = rows // GROUP

    def lanes(n):
        return slice(n * LANES, (n + 1) * LANES)

    def act_right(s):
        source, dest = src_list[2 * s], dest_list[2 * s]
        tall = jnp.concatenate([x_ref[source, :, lanes(q)] for q in range(phys)], axis=0)
        second = right_t_ref[chan_list[2 * s + 1], dest]
        second = jnp.where(live_list[2 * s + 1] > 0, second, jnp.zeros_like(second))
        out = dot(tall, jnp.concatenate([right_t_ref[chan_list[2 * s], dest], second], axis=1))
        for i in range(2):
            for g in range(groups):
                turned_ref[i, g] = jnp.concatenate(
                    [
                        out[q * rows + g * GROUP : q * rows + (g + 1) * GROUP, lanes(i)]
                        for q in range(phys)
                    ],
                    axis=0,
                ).astype(BF16)

    def act_site(s):
        for i in range(2):
            kron = kron_ref[chan_list[2 * s + i]]
            for h in range(groups // 2):
                both = jnp.concatenate([turned_ref[i, 2 * h], turned_ref[i, 2 * h + 1]], axis=1)
                out = dot(kron, both)
                r0 = i * rows + 2 * h * GROUP
                for p in range(phys):
                    row = slice(p * GROUP, (p + 1) * GROUP)
                    mixed_ref[r0 : r0 + 2 * GROUP, lanes(p)] = jnp.concatenate(
                        [out[row, lanes(0)], out[row, lanes(1)]], axis=0
                    ).astype(BF16)

    def act_left(s):
        dest = dest_list[2 * s]
        left = jnp.concatenate(
            [left_ref[chan_list[2 * s], dest], left_ref[chan_list[2 * s + 1], dest]], axis=1
        )
        acc_ref[dest] += dot(left, mixed_ref[...])

    def middle(s, carry):
        act_site(s)
        act_right(s + 1)
        act_left(s)
        return carry

    @pl.when(steps > 0)
    def _():
        act_right(0)
        lax.fori_loop(0, steps - 1, middle, 0)
        act_site(steps - 1)
        act_left(steps - 1)


def fold(values):
    total = values[:, :LANES]
    for p in range(1, values.shape[1] // LANES):
        total = total + values[:, p * LANES : (p + 1) * LANES]
    return total


def row_loop(blocks, rows, body, count, first=0):
    zeros = tuple(jnp.zeros((CHUNK, LANES), F32) for _ in range(count))
    per = rows // CHUNK

    def step(n, carry):
        start = pl.multiple_of(lax.rem(n, per) * CHUNK, CHUNK)
        return body(first + n // per, pl.ds(start, CHUNK), start, carry)

    return lax.fori_loop(0, blocks * per, step, zeros)


def kept_rows(rank, start):
    row = start + lax.broadcasted_iota(jnp.int32, (CHUNK, LANES), 0)
    return (row < rank).astype(F32)


def put_sums(out_ref, values, first=0):
    for n, value in enumerate(values):
        out_ref[first + n : first + n + 1, :] = jnp.full((1, LANES), 1.0, F32) * jnp.sum(value)


def common_shift(mine_ref, theirs_ref):
    num = mine_ref[0:1, :] + theirs_ref[0:1, :]
    den = mine_ref[1:2, :] + theirs_ref[1:2, :]
    return jnp.where(den > 0, num / jnp.where(den > 0, den, 1.0), 0.0)


def cut(x_ref, *out_refs):
    for b, out_ref in enumerate(out_refs):
        out_ref[0] = x_ref[b]


def first_local(
    rel_ref, kron_ref, x_ref, left_ref, right_ref,
    right_t_ref, image_ref, sums_ref,
    turned_ref, mixed_ref, *lists,
):
    chan, dests = left_ref.shape[:2]

    def turn(n, carry):
        for k in range(2):
            for b in range(dests):
                right_t_ref[2 * n + k, b] = right_ref[2 * n + k, b].T
        return carry

    lax.fori_loop(0, chan // 2, turn, 0)
    image_ref[...] = jnp.zeros_like(image_ref)
    steps = list_pairs(rel_ref, 0, dests, *lists)
    add_pairs(steps, lists, kron_ref, x_ref, left_ref, right_t_ref, image_ref, turned_ref, mixed_ref)

    def sums(b, r, start, carry):
        x = x_ref[b, r, :].astype(F32)
        return carry[0] + fold(x * image_ref[b, r, :]), carry[1] + fold(x * x)

    totals = row_loop(dests, x_ref.shape[1], sums, 2)
    sums_ref[...] = jnp.zeros_like(sums_ref)
    put_sums(sums_ref, totals)


def local_sources(
    rel_ref, kron_ref, x_ref, left_ref, right_t_ref,
    acc_ref,
    turned_ref, mixed_ref, *lists,
):
    acc_ref[...] = jnp.zeros_like(acc_ref)
    steps = list_pairs(rel_ref, 0, left_ref.shape[1], *lists)
    add_pairs(steps, lists, kron_ref, x_ref, left_ref, right_t_ref, acc_ref, turned_ref, mixed_ref)


def first_remote(
    rel_ref, kron_ref, other_ref, left_ref, right_t_ref, before_ref, local_sums_ref,
    acc_ref, sums_ref,
    turned_ref, mixed_ref, *lists,
):
    dests = left_ref.shape[1]
    sums_ref[...] = local_sums_ref[...]
    steps = list_pairs(rel_ref, dests, dests + 1, *lists)
    add_pairs(steps, lists, kron_ref, other_ref, left_ref, right_t_ref, acc_ref, turned_ref, mixed_ref)


def first_finish(
    dest, rel_ref, kron_ref, other_ref, left_ref, right_t_ref, before_ref, x_ref, mine_ref,
    theirs_ref, *refs,
):
    dests = left_ref.shape[1]
    last = dest == dests - 1
    if last:
        earlier_ref, acc_ref, guess_ref, all_ref = refs[:4]
        all_ref[0:dest] = earlier_ref[...]
    else:
        acc_ref, guess_ref = refs[:2]
    turned_ref, mixed_ref = refs[-6:-4]
    lists = refs[-4:]
    steps = list_pairs(rel_ref, dests + 1, 2 * dests, *lists, only=(dest,))
    add_pairs(steps, lists, kron_ref, other_ref, left_ref, right_t_ref, acc_ref, turned_ref, mixed_ref)
    shift = common_shift(mine_ref, theirs_ref)
    keep_state = jnp.tile(1.0 + STEP_SIZE * shift, (1, x_ref.shape[2] // LANES))

    def update(b, r, start, carry):
        x = x_ref[b, r, :].astype(F32)
        guess = (keep_state * x - STEP_SIZE * acc_ref[b, r, :]).astype(BF16)
        guess_ref[0, r, :] = guess
        if last:
            all_ref[b, r, :] = guess
        return carry

    row_loop(1, x_ref.shape[1], update, 0, first=dest)


def second_remote(
    rel_ref, rank_ref, kron_ref, other_ref, left_ref, right_t_ref, before_ref, x_ref, image_ref,
    guess_ref,
    acc_ref, sums_ref,
    turned_ref, mixed_ref, *lists,
):
    dests, rows, _ = x_ref.shape
    steps = list_pairs(rel_ref, dests, dests + 1, *lists)
    add_pairs(steps, lists, kron_ref, other_ref, left_ref, right_t_ref, acc_ref, turned_ref, mixed_ref)

    def sums(b, r, start, carry):
        x = x_ref[b, r, :].astype(F32)
        guess = guess_ref[b, r, :].astype(F32)
        image = image_ref[b, r, :]
        keep = kept_rows(rank_ref[b], start)
        xx, xg, gg = fold(x * x), fold(x * guess), fold(guess * guess)
        new = (fold(x * image), xx, fold(guess * image), xg, gg, keep * gg, keep * xx, keep * xg)
        return tuple(total + value for total, value in zip(carry, new))

    put_sums(sums_ref, row_loop(dests, rows, sums, 8))


def second_finish(
    rel_ref, rank_ref, kron_ref, other_ref, left_ref, right_t_ref, before_ref, x_ref, guess_ref,
    mine_ref, theirs_ref, early_ref,
    kept_ref, sums_ref,
    turned_ref, mixed_ref, *lists,
):
    dests, rows, width = x_ref.shape
    steps = list_pairs(rel_ref, dests + 1, 2 * dests, *lists)
    add_pairs(steps, lists, kron_ref, other_ref, left_ref, right_t_ref, kept_ref, turned_ref, mixed_ref)
    shift = common_shift(mine_ref, theirs_ref)
    keep_guess = jnp.tile(1.0 + STEP_SIZE * shift, (1, width // LANES))

    def sums(b, r, start, carry):
        x = x_ref[b, r, :].astype(F32)
        guess = guess_ref[b, r, :].astype(F32)
        kept = keep_guess * guess - STEP_SIZE * kept_ref[b, r, :]
        kept_ref[b, r, :] = kept
        keep = kept_rows(rank_ref[b], start)
        kg, kx = fold(kept * guess), fold(kept * x)
        new = (kg, kx, keep * kg, keep * kx, keep * fold(kept * kept))
        return tuple(total + value for total, value in zip(carry, new))

    totals = row_loop(dests, rows, sums, 5)
    sums_ref[0:8, :] = early_ref[...]
    put_sums(sums_ref, totals, first=8)
    sums_ref[13:16, :] = jnp.zeros((3, LANES), F32)


def normalize(
    cells, rank_ref, kept_ref, guess_ref, x_ref, mine_ref, theirs_ref, my_sums_ref, their_sums_ref,
    state_ref, turned_ref,
):
    both = my_sums_ref[...] + their_sums_ref[...]
    xv, xx, gv, xg, gg, gg_kept, xx_kept, xg_kept, kg, kx, kg_kept, kx_kept, kk_kept = (
        both[n : n + 1] for n in range(13)
    )
    shift = common_shift(mine_ref, theirs_ref)
    delta = STEP_SIZE * (xv / xx - shift)
    scale = (1.0 + STEP_SIZE * shift) / STEP_SIZE
    gw, xw = scale * gg - kg / STEP_SIZE, scale * xg - kx / STEP_SIZE
    num = gw + delta * (xw + gv + delta * xv)
    den = gg + delta * (2.0 * xg + delta * xx)
    beta = STEP_SIZE * (num / den - shift)
    of_guess, of_state = beta + delta, beta * delta
    norm = (
        kk_kept
        + of_guess * (2.0 * kg_kept + of_guess * gg_kept)
        + of_state * (2.0 * kx_kept + of_state * xx_kept + 2.0 * of_guess * xg_kept)
    )
    gain = jnp.sqrt(cells / (jnp.maximum(norm, 0.0) + EPSILON))
    blocks, rows, width = kept_ref.shape
    group = 8 * LANES
    per = width // group
    row = lax.broadcasted_iota(jnp.int32, (rows, LANES), 0)

    def one(n, carry):
        b = n // per
        factor = jnp.where(row < rank_ref[b], gain, 0.0)
        for p in range(8):
            cols = pl.ds(pl.multiple_of(lax.rem(n, per) * group + p * LANES, LANES), LANES)
            kept = (
                kept_ref[b, :, cols]
                + of_guess * guess_ref[b, :, cols].astype(F32)
                + of_state * x_ref[b, :, cols].astype(F32)
            )
            state = (kept * factor).astype(BF16)
            state_ref[b, :, cols] = state
            turned_ref[b, :, cols] = state.T
        return carry

    lax.fori_loop(0, blocks * per, one, 0)


def environments(first, count, scale, env_ref, inner_ref, outer_ref, out_ref, mid_ref):
    dests, rows, width = outer_ref.shape
    phys = width // LANES
    pairs = mid_ref.shape[0] // dests

    def step(n, carry):
        for j in range(pairs):
            k = first + 2 * (n * pairs + j)
            for b in range(dests):
                env = jnp.concatenate([env_ref[k, b], env_ref[k + 1, b]], axis=0)
                mid = dot(env, inner_ref[b]).astype(BF16)
                for p in range(phys):
                    for i in range(2):
                        mid_ref[
                            j * dests + b, p * rows : (p + 1) * rows, i * LANES : (i + 1) * LANES
                        ] = mid[i * rows : (i + 1) * rows, p * LANES : (p + 1) * LANES]
        for j in range(pairs):
            place = 2 * (n * pairs + j)
            for b in range(dests):
                out = (dot(outer_ref[b], mid_ref[j * dests + b]) * scale).astype(BF16)
                out_ref[place, b] = out[:, :LANES]
                out_ref[place + 1, b] = out[:, LANES:]
        return carry

    lax.fori_loop(0, count // (2 * pairs), step, 0)


def normalize_and_left(
    first, count, scale, cells,
    rank_ref, kept_ref, guess_ref, x_ref, mine_ref, theirs_ref, my_sums_ref, their_sums_ref, env_ref,
    new_ref, state_ref, turned_ref, out_ref,
    mid_ref, sem,
):
    normalize(
        cells, rank_ref, kept_ref, guess_ref, x_ref, mine_ref, theirs_ref, my_sums_ref,
        their_sums_ref, state_ref, turned_ref,
    )
    copy = pltpu.make_async_copy(state_ref, new_ref, sem)
    copy.start()
    environments(first, count, scale, env_ref, state_ref, turned_ref, out_ref, mid_ref)
    copy.wait()


def widen(places, *refs):
    pieces, (outs, wides, sems) = refs[: len(places)], (refs[-5:-3], refs[-3:-1], refs[-1])
    copies = []
    for piece, (side, begin) in zip(pieces, places):
        for n in range(0, piece.shape[0], 2):
            span = pl.ds(begin + n, 2)
            wides[side][begin + n : begin + n + 2] = piece[n : n + 2].astype(F32)
            copy = pltpu.make_async_copy(
                wides[side].at[span], outs[side].at[span], sems.at[len(copies)]
            )
            copy.start()
            copies.append(copy)
    for copy in copies:
        copy.wait()


def shards(state, left_env, right_env, site_ops, sector_map, ranks):
    dests, rows, width = state.shape[1:]
    chan, phys = site_ops.shape[1:3]
    groups = lax.axis_size("blk")
    total_blocks = groups * dests
    first_block = lax.axis_index("blk") * dests
    x, left, right, ops = state[0], left_env[0], right_env[0], site_ops[0]
    local_map = lax.dynamic_slice_in_dim(sector_map[0], first_block, dests, 1)
    rel = lax.rem(local_map - first_block + total_blocks, total_blocks)

    swap = [(g, groups - 1 - g) for g in range(groups)]

    def trade(value):
        return lax.ppermute(value, "blk", swap)

    def shape(dims, kind):
        return jax.ShapeDtypeStruct(dims, kind)

    wave = (dests, rows, width)
    wave_f32 = shape(wave, F32)
    wave_b16 = shape(wave, BF16)
    sums_kind = shape((8, LANES), F32)
    lists = [pltpu.SMEM((chan * dests + 2 * dests * dests + 1,), jnp.int32)] * 4
    pair_scratch = [
        pltpu.VMEM((2, rows // GROUP, phys * GROUP, LANES), BF16),
        pltpu.VMEM((2 * rows, width), BF16),
    ] + lists

    def call(body, specs, outs, scratch, *args, aliases={}):
        return pl.pallas_call(
            body,
            in_specs=specs,
            out_specs=jax.tree.map(lambda _: VMEM, outs),
            out_shape=outs,
            scratch_shapes=scratch,
            compiler_params=PARAMS,
            cost_estimate=COST,
            input_output_aliases=aliases,
        )(*args)

    block = shape((1, rows, width), BF16)
    own = call(cut, [VMEM], (block,) * dests, [], x)
    other = [trade(value) for value in own]
    kron = call(
        make_kron, [VMEM], shape((chan, phys * GROUP, phys * GROUP), BF16),
        [pltpu.VMEM((chan * phys, phys * GROUP), F32)], ops,
    )
    right_t, image, mine = call(
        first_local, [SMEM] + [VMEM] * 4,
        (shape(right.shape, BF16), wave_f32, sums_kind), pair_scratch,
        rel, kron, x, left, right,
    )
    image, mine = call(
        first_remote, [SMEM] + [VMEM] * 6, (wave_f32, sums_kind), pair_scratch,
        rel, kron, other[0], left, right_t, image, mine, aliases={5: 0},
    )
    theirs = trade(mine)
    image, first_guess = call(
        functools.partial(first_finish, 0), [SMEM] + [VMEM] * 8,
        (wave_f32, block), pair_scratch,
        rel, kron, other[1], left, right_t, image, x, mine, theirs, aliases={5: 0},
    )
    image, last_guess, guess = call(
        functools.partial(first_finish, 1), [SMEM] + [VMEM] * 9,
        (wave_f32, block, wave_b16), pair_scratch,
        rel, kron, other[1], left, right_t, image, x, mine, theirs, first_guess, aliases={5: 0},
    )
    other = [trade(first_guess), trade(last_guess)]
    acc = call(
        local_sources, [SMEM] + [VMEM] * 4, wave_f32, pair_scratch,
        rel, kron, guess, left, right_t,
    )
    acc, early_sums = call(
        second_remote, [SMEM] * 2 + [VMEM] * 8, (wave_f32, sums_kind), pair_scratch,
        rel, ranks[0], kron, other[0], left, right_t, acc, x, image, guess, aliases={6: 0},
    )
    kept, my_sums = call(
        second_finish, [SMEM] * 2 + [VMEM] * 10, (wave_f32, shape((16, LANES), F32)), pair_scratch,
        rel, ranks[0], kron, other[1], left, right_t, acc, x, guess, mine, theirs, early_sums,
        aliases={6: 0},
    )
    their_sums = trade(my_sums)

    env_scale = 1.0 / math.sqrt(phys * rows)
    cells = float(total_blocks * rows * width)
    early, later = 8, 8

    def mid(count):
        pairs = next(n for n in (2, 3, 1) if count % (2 * n) == 0)
        return [pltpu.VMEM((pairs * dests, width, 2 * LANES), BF16)]

    def sent(value, steps):
        count = lax.axis_size("seg")
        begin, end = max(0, -steps), min(count, count - steps)
        return lax.ppermute(value, "seg", [(s, s + steps) for s in range(begin, end)])

    def env_kind(count):
        return shape((count,) + left.shape[1:], BF16)

    def env_call(begin, count, env, inner, outer):
        return call(
            functools.partial(environments, begin, count, env_scale),
            [VMEM] * 3, env_kind(count), mid(count), env, inner, outer,
        )

    new_state, state_kept, turned, piece = pl.pallas_call(
        functools.partial(normalize_and_left, 0, early, env_scale, cells),
        in_specs=[SMEM] + [VMEM] * 8,
        out_specs=(HBM, VMEM, VMEM, VMEM),
        out_shape=(wave_b16, wave_b16, wave_b16, env_kind(early)),
        scratch_shapes=mid(early) + [pltpu.SemaphoreType.DMA],
        compiler_params=PARAMS,
        cost_estimate=COST,
    )(ranks[0], kept, guess, x, mine, theirs, my_sums, their_sums, left)
    pieces = [
        sent(piece, 1),
        sent(env_call(0, later, right, turned, state_kept), -1),
        sent(env_call(early, chan - early, left, state_kept, turned), 1),
        sent(env_call(later, chan - later, right, turned, state_kept), -1),
    ]
    env_f32 = shape(left.shape, F32)

    def widened(places, values, filled):
        count = len(values)
        return pl.pallas_call(
            functools.partial(widen, places),
            in_specs=[VMEM] * count + [HBM] * len(filled),
            out_specs=(HBM, HBM),
            out_shape=(env_f32, env_f32),
            input_output_aliases={count + n: n for n in range(len(filled))},
            scratch_shapes=[pltpu.VMEM(left.shape, F32)] * 2 + [pltpu.SemaphoreType.DMA((chan,))],
            compiler_params=PARAMS,
            cost_estimate=COST,
        )(*values, *filled)

    filled = widened(((0, 0),), pieces[:1], ())
    filled = widened(((1, 0),), pieces[1:2], filled)
    received_left, received_right = widened(((0, early), (1, later)), pieces[2:], filled)
    return (new_state[None], received_left[None], received_right[None])


def solution(mesh):
    placed = (
        P("seg", "blk", None, None),
        P("seg", None, "blk", None, None),
        P("seg", None, "blk", None, None),
        P("seg", None, None, None),
        P("seg", None, None),
        P("seg", "blk"),
    )
    return jax.shard_map(
        shards,
        mesh=mesh,
        in_specs=placed,
        out_specs=(
            P("seg", "blk", None, None),
            P("seg", None, "blk", None, None),
            P("seg", None, "blk", None, None),
        ),
        check_vma=False,
    )
```

```python
import functools
import math

import jax
import jax.numpy as jnp
from jax import lax
from jax.experimental import pallas as pl
from jax.experimental.pallas import tpu as pltpu
from jax.sharding import PartitionSpec as P

STEP_SIZE = 0.25
EPSILON = 1e-06
LANES = 128
GROUP = 8
CHUNK = 32
F32 = jnp.float32
BF16 = jnp.bfloat16
VMEM = pl.BlockSpec(memory_space=pltpu.VMEM)
HBM = pl.BlockSpec(memory_space=pltpu.HBM)
SMEM = pl.BlockSpec(memory_space=pltpu.SMEM)
COST = pl.CostEstimate(flops=1024, bytes_accessed=1024, transcendentals=0)
PARAMS = pltpu.CompilerParams(vmem_limit_bytes=32 * 1024 * 1024)


def dot(left, right):
    return lax.dot_general(
        left, right, (((1,), (0,)), ((), ())), preferred_element_type=F32
    )


def pieces_of(blocks, rows):
    last = rows - rows // 4
    whole = [(b, 0, rows) for b in range(blocks - 1)]
    return whole + [(blocks - 1, 0, last), (blocks - 1, last, rows)]


def make_kron(ops_ref, kron_ref, spread_ref):
    chan, phys, _ = ops_ref.shape
    wide = phys * GROUP
    columns = lax.broadcasted_iota(jnp.int32, (phys, wide), 1)
    spread = (columns // GROUP == lax.broadcasted_iota(jnp.int32, (phys, wide), 0)).astype(F32)
    spread_ref[...] = dot(ops_ref[...].reshape(chan * phys, phys), spread.astype(BF16))
    same = lax.broadcasted_iota(jnp.int32, (GROUP, wide), 1) % GROUP == lax.broadcasted_iota(
        jnp.int32, (GROUP, wide), 0
    )

    def one(k, carry):
        rows = spread_ref[pl.ds(pl.multiple_of(k * phys, phys), phys), :]
        full = [
            jnp.where(same, jnp.broadcast_to(rows[p : p + 1], (GROUP, wide)), 0.0)
            for p in range(phys)
        ]
        kron_ref[k] = jnp.concatenate(full, axis=0).astype(BF16)
        return carry

    lax.fori_loop(0, chan, one, 0)


def list_pairs(rel_ref, low, high, chan_list, src_list, live_list, dest_list, only=None):
    chan, dests = rel_ref.shape
    place = jnp.int32(0)
    for b in range(dests) if only is None else only:
        for source in range(low, high):
            for k in range(chan):
                chan_list[place] = k
                src_list[place] = source - low
                live_list[place] = 1
                dest_list[place] = b
                place = place + jnp.where(rel_ref[k, b] == source, 1, 0)
            chan_list[place] = 0
            src_list[place] = source - low
            live_list[place] = 0
            dest_list[place] = b
            place = place + lax.rem(place, 2)
    return place // 2


def add_pairs(
    steps, lists, kron_ref, x_ref, left_ref, right_t_ref, acc_ref, turned_ref, mixed_ref, start=0
):
    chan_list, src_list, live_list, dest_list = lists
    rows = x_ref.shape[1]
    phys = x_ref.shape[2] // LANES
    groups = rows // GROUP

    def lanes(n):
        return slice(n * LANES, (n + 1) * LANES)

    def act_right(s):
        source, dest = src_list[2 * s], dest_list[2 * s]
        tall = jnp.concatenate([x_ref[source, :, lanes(q)] for q in range(phys)], axis=0)
        second = right_t_ref[chan_list[2 * s + 1], dest]
        second = jnp.where(live_list[2 * s + 1] > 0, second, jnp.zeros_like(second))
        out = dot(tall, jnp.concatenate([right_t_ref[chan_list[2 * s], dest], second], axis=1))
        for i in range(2):
            for g in range(groups):
                turned_ref[i, g] = jnp.concatenate(
                    [
                        out[q * rows + g * GROUP : q * rows + (g + 1) * GROUP, lanes(i)]
                        for q in range(phys)
                    ],
                    axis=0,
                ).astype(BF16)

    def act_site(s):
        for i in range(2):
            kron = kron_ref[chan_list[2 * s + i]]
            for h in range(groups // 2):
                both = jnp.concatenate([turned_ref[i, 2 * h], turned_ref[i, 2 * h + 1]], axis=1)
                out = dot(kron, both)
                r0 = i * rows + 2 * h * GROUP
                for p in range(phys):
                    row = slice(p * GROUP, (p + 1) * GROUP)
                    mixed_ref[r0 : r0 + 2 * GROUP, lanes(p)] = jnp.concatenate(
                        [out[row, lanes(0)], out[row, lanes(1)]], axis=0
                    ).astype(BF16)

    def act_left(s):
        dest = dest_list[2 * s]
        left = jnp.concatenate(
            [left_ref[chan_list[2 * s + i], dest][:, start : start + rows] for i in range(2)], axis=1
        )
        acc_ref[dest] += dot(left, mixed_ref[0 : 2 * rows, :])

    def middle(s, carry):
        act_site(s)
        act_right(s + 1)
        act_left(s)
        return carry

    @pl.when(steps > 0)
    def _():
        act_right(0)
        lax.fori_loop(0, steps - 1, middle, 0)
        act_site(steps - 1)
        act_left(steps - 1)


def fold(values):
    total = values[:, :LANES]
    for p in range(1, values.shape[1] // LANES):
        total = total + values[:, p * LANES : (p + 1) * LANES]
    return total


def row_loop(blocks, rows, body, count, first=0):
    zeros = tuple(jnp.zeros((CHUNK, LANES), F32) for _ in range(count))
    per = rows // CHUNK

    def step(n, carry):
        start = pl.multiple_of(lax.rem(n, per) * CHUNK, CHUNK)
        return body(first + n // per, pl.ds(start, CHUNK), start, carry)

    return lax.fori_loop(0, blocks * per, step, zeros)


def kept_rows(rank, start):
    row = start + lax.broadcasted_iota(jnp.int32, (CHUNK, LANES), 0)
    return (row < rank).astype(F32)


def put_sums(out_ref, values, first=0):
    for n, value in enumerate(values):
        out_ref[first + n : first + n + 1, :] = jnp.full((1, LANES), 1.0, F32) * jnp.sum(value)


def common_shift(mine_ref, theirs_ref):
    num = mine_ref[0:1, :] + theirs_ref[0:1, :]
    den = mine_ref[1:2, :] + theirs_ref[1:2, :]
    return jnp.where(den > 0, num / jnp.where(den > 0, den, 1.0), 0.0)


def cut(x_ref, *out_refs):
    for (b, begin, end), out_ref in zip(pieces_of(*x_ref.shape[:2]), out_refs):
        out_ref[0] = x_ref[b, begin:end]


def first_local(
    rel_ref, kron_ref, x_ref, left_ref, right_ref,
    right_t_ref, image_ref, sums_ref,
    turned_ref, mixed_ref, *lists,
):
    chan, dests = left_ref.shape[:2]

    def turn(n, carry):
        for k in range(2):
            for b in range(dests):
                right_t_ref[2 * n + k, b] = right_ref[2 * n + k, b].T
        return carry

    lax.fori_loop(0, chan // 2, turn, 0)
    image_ref[...] = jnp.zeros_like(image_ref)
    steps = list_pairs(rel_ref, 0, dests, *lists)
    add_pairs(steps, lists, kron_ref, x_ref, left_ref, right_t_ref, image_ref, turned_ref, mixed_ref)

    def sums(b, r, start, carry):
        x = x_ref[b, r, :].astype(F32)
        return carry[0] + fold(x * image_ref[b, r, :]), carry[1] + fold(x * x)

    totals = row_loop(dests, x_ref.shape[1], sums, 2)
    sums_ref[...] = jnp.zeros_like(sums_ref)
    put_sums(sums_ref, totals)


def local_sources(
    rel_ref, kron_ref, x_ref, left_ref, right_t_ref,
    acc_ref,
    turned_ref, mixed_ref, *lists,
):
    acc_ref[...] = jnp.zeros_like(acc_ref)
    steps = list_pairs(rel_ref, 0, left_ref.shape[1], *lists)
    add_pairs(steps, lists, kron_ref, x_ref, left_ref, right_t_ref, acc_ref, turned_ref, mixed_ref)


def first_remote(
    rel_ref, kron_ref, other_ref, left_ref, right_t_ref, before_ref, local_sums_ref,
    acc_ref, sums_ref,
    turned_ref, mixed_ref, *lists,
):
    dests = left_ref.shape[1]
    sums_ref[...] = local_sums_ref[...]
    steps = list_pairs(rel_ref, dests, dests + 1, *lists)
    add_pairs(steps, lists, kron_ref, other_ref, left_ref, right_t_ref, acc_ref, turned_ref, mixed_ref)


def more_remote(
    rel_ref, kron_ref, other_ref, left_ref, right_t_ref, before_ref,
    acc_ref,
    turned_ref, mixed_ref, *lists,
):
    dests = left_ref.shape[1]
    steps = list_pairs(rel_ref, dests + 1, 2 * dests, *lists)
    add_pairs(steps, lists, kron_ref, other_ref, left_ref, right_t_ref, acc_ref, turned_ref, mixed_ref)


def first_finish(
    dest, rel_ref, kron_ref, other_ref, left_ref, right_t_ref, before_ref, x_ref, mine_ref,
    theirs_ref, *refs,
):
    dests = left_ref.shape[1]
    last = dest == dests - 1
    if last:
        earlier_ref, acc_ref, head_ref, tail_ref, all_ref = refs[:5]
        all_ref[0:dest] = earlier_ref[...]
    else:
        acc_ref, guess_ref = refs[:2]
    turned_ref, mixed_ref = refs[-6:-4]
    lists = refs[-4:]
    rows = x_ref.shape[1]
    begin = rows - other_ref.shape[1]
    steps = list_pairs(rel_ref, dests + 1, 2 * dests, *lists, only=(dest,))
    add_pairs(
        steps, lists, kron_ref, other_ref, left_ref, right_t_ref, acc_ref, turned_ref, mixed_ref, begin
    )
    shift = common_shift(mine_ref, theirs_ref)
    keep_state = jnp.tile(1.0 + STEP_SIZE * shift, (1, x_ref.shape[2] // LANES))

    def update(b, r, start, carry):
        x = x_ref[b, r, :].astype(F32)
        guess = (keep_state * x - STEP_SIZE * acc_ref[b, r, :]).astype(BF16)
        if last:
            all_ref[b, r, :] = guess
        else:
            guess_ref[0, r, :] = guess
        return carry

    row_loop(1, rows, update, 0, first=dest)
    if last:
        head_ref[0] = all_ref[dest, 0:begin]
        tail_ref[0] = all_ref[dest, begin:rows]


def second_remote(
    rel_ref, rank_ref, kron_ref, other_ref, left_ref, right_t_ref, before_ref, x_ref, image_ref,
    guess_ref,
    acc_ref, sums_ref,
    turned_ref, mixed_ref, *lists,
):
    dests, rows, _ = x_ref.shape
    steps = list_pairs(rel_ref, dests, dests + 1, *lists)
    add_pairs(steps, lists, kron_ref, other_ref, left_ref, right_t_ref, acc_ref, turned_ref, mixed_ref)

    def sums(b, r, start, carry):
        x = x_ref[b, r, :].astype(F32)
        guess = guess_ref[b, r, :].astype(F32)
        image = image_ref[b, r, :]
        keep = kept_rows(rank_ref[b], start)
        xx, xg, gg = fold(x * x), fold(x * guess), fold(guess * guess)
        new = (fold(x * image), xx, fold(guess * image), xg, gg, keep * gg, keep * xx, keep * xg)
        return tuple(total + value for total, value in zip(carry, new))

    put_sums(sums_ref, row_loop(dests, rows, sums, 8))


def second_finish(
    rel_ref, rank_ref, kron_ref, other_ref, left_ref, right_t_ref, before_ref, x_ref, guess_ref,
    mine_ref, theirs_ref, early_ref,
    kept_ref, sums_ref,
    turned_ref, mixed_ref, *lists,
):
    dests, rows, width = x_ref.shape
    steps = list_pairs(rel_ref, dests + 1, 2 * dests, *lists)
    add_pairs(
        steps, lists, kron_ref, other_ref, left_ref, right_t_ref, kept_ref, turned_ref, mixed_ref,
        rows - other_ref.shape[1],
    )
    shift = common_shift(mine_ref, theirs_ref)
    keep_guess = jnp.tile(1.0 + STEP_SIZE * shift, (1, width // LANES))

    def sums(b, r, start, carry):
        x = x_ref[b, r, :].astype(F32)
        guess = guess_ref[b, r, :].astype(F32)
        kept = keep_guess * guess - STEP_SIZE * kept_ref[b, r, :]
        kept_ref[b, r, :] = kept
        keep = kept_rows(rank_ref[b], start)
        kg, kx = fold(kept * guess), fold(kept * x)
        new = (kg, kx, keep * kg, keep * kx, keep * fold(kept * kept))
        return tuple(total + value for total, value in zip(carry, new))

    totals = row_loop(dests, rows, sums, 5)
    sums_ref[0:8, :] = early_ref[...]
    put_sums(sums_ref, totals, first=8)
    sums_ref[13:16, :] = jnp.zeros((3, LANES), F32)


def normalize(
    cells, rank_ref, kept_ref, guess_ref, x_ref, mine_ref, theirs_ref, my_sums_ref, their_sums_ref,
    state_ref, turned_ref,
):
    both = my_sums_ref[...] + their_sums_ref[...]
    xv, xx, gv, xg, gg, gg_kept, xx_kept, xg_kept, kg, kx, kg_kept, kx_kept, kk_kept = (
        both[n : n + 1] for n in range(13)
    )
    shift = common_shift(mine_ref, theirs_ref)
    delta = STEP_SIZE * (xv / xx - shift)
    scale = (1.0 + STEP_SIZE * shift) / STEP_SIZE
    gw, xw = scale * gg - kg / STEP_SIZE, scale * xg - kx / STEP_SIZE
    num = gw + delta * (xw + gv + delta * xv)
    den = gg + delta * (2.0 * xg + delta * xx)
    beta = STEP_SIZE * (num / den - shift)
    of_guess, of_state = beta + delta, beta * delta
    norm = (
        kk_kept
        + of_guess * (2.0 * kg_kept + of_guess * gg_kept)
        + of_state * (2.0 * kx_kept + of_state * xx_kept + 2.0 * of_guess * xg_kept)
    )
    gain = jnp.sqrt(cells / (jnp.maximum(norm, 0.0) + EPSILON))
    blocks, rows, width = kept_ref.shape
    group = 8 * LANES
    per = width // group
    row = lax.broadcasted_iota(jnp.int32, (rows, LANES), 0)

    def one(n, carry):
        b = n // per
        factor = jnp.where(row < rank_ref[b], gain, 0.0)
        for p in range(8):
            cols = pl.ds(pl.multiple_of(lax.rem(n, per) * group + p * LANES, LANES), LANES)
            kept = (
                kept_ref[b, :, cols]
                + of_guess * guess_ref[b, :, cols].astype(F32)
                + of_state * x_ref[b, :, cols].astype(F32)
            )
            state = (kept * factor).astype(BF16)
            state_ref[b, :, cols] = state
            turned_ref[b, :, cols] = state.T
        return carry

    lax.fori_loop(0, blocks * per, one, 0)


def environments(first, count, scale, env_ref, inner_ref, outer_ref, out_ref, mid_ref):
    dests, rows, width = outer_ref.shape
    phys = width // LANES
    pairs = mid_ref.shape[0] // dests

    def step(n, carry):
        for j in range(pairs):
            k = first + 2 * (n * pairs + j)
            for b in range(dests):
                env = jnp.concatenate([env_ref[k, b], env_ref[k + 1, b]], axis=0)
                mid = dot(env, inner_ref[b]).astype(BF16)
                for p in range(phys):
                    for i in range(2):
                        mid_ref[
                            j * dests + b, p * rows : (p + 1) * rows, i * LANES : (i + 1) * LANES
                        ] = mid[i * rows : (i + 1) * rows, p * LANES : (p + 1) * LANES]
        for j in range(pairs):
            place = 2 * (n * pairs + j)
            for b in range(dests):
                out = (dot(outer_ref[b], mid_ref[j * dests + b]) * scale).astype(BF16)
                out_ref[place, b] = out[:, :LANES]
                out_ref[place + 1, b] = out[:, LANES:]
        return carry

    lax.fori_loop(0, count // (2 * pairs), step, 0)


def normalize_and_left(
    first, count, scale, cells,
    rank_ref, kept_ref, guess_ref, x_ref, mine_ref, theirs_ref, my_sums_ref, their_sums_ref, env_ref,
    new_ref, state_ref, turned_ref, out_ref,
    mid_ref, sem,
):
    normalize(
        cells, rank_ref, kept_ref, guess_ref, x_ref, mine_ref, theirs_ref, my_sums_ref,
        their_sums_ref, state_ref, turned_ref,
    )
    copy = pltpu.make_async_copy(state_ref, new_ref, sem)
    copy.start()
    environments(first, count, scale, env_ref, state_ref, turned_ref, out_ref, mid_ref)
    copy.wait()


def widen(places, *refs):
    pieces, (outs, wides, sems) = refs[: len(places)], (refs[-5:-3], refs[-3:-1], refs[-1])
    copies = []
    for piece, (side, begin) in zip(pieces, places):
        for n in range(0, piece.shape[0], 2):
            span = pl.ds(begin + n, 2)
            wides[side][begin + n : begin + n + 2] = piece[n : n + 2].astype(F32)
            copy = pltpu.make_async_copy(
                wides[side].at[span], outs[side].at[span], sems.at[len(copies)]
            )
            copy.start()
            copies.append(copy)
    for copy in copies:
        copy.wait()


def shards(state, left_env, right_env, site_ops, sector_map, ranks):
    dests, rows, width = state.shape[1:]
    chan, phys = site_ops.shape[1:3]
    groups = lax.axis_size("blk")
    total_blocks = groups * dests
    first_block = lax.axis_index("blk") * dests
    x, left, right, ops = state[0], left_env[0], right_env[0], site_ops[0]
    local_map = lax.dynamic_slice_in_dim(sector_map[0], first_block, dests, 1)
    rel = lax.rem(local_map - first_block + total_blocks, total_blocks)

    swap = [(g, groups - 1 - g) for g in range(groups)]

    def trade(value):
        return lax.ppermute(value, "blk", swap)

    def shape(dims, kind):
        return jax.ShapeDtypeStruct(dims, kind)

    wave = (dests, rows, width)
    wave_f32 = shape(wave, F32)
    wave_b16 = shape(wave, BF16)
    sums_kind = shape((8, LANES), F32)
    lists = [pltpu.SMEM((chan * dests + 2 * dests * dests + 1,), jnp.int32)] * 4
    pair_scratch = [
        pltpu.VMEM((2, rows // GROUP, phys * GROUP, LANES), BF16),
        pltpu.VMEM((2 * rows, width), BF16),
    ] + lists

    def call(body, specs, outs, scratch, *args, aliases={}):
        return pl.pallas_call(
            body,
            in_specs=specs,
            out_specs=jax.tree.map(lambda _: VMEM, outs),
            out_shape=outs,
            scratch_shapes=scratch,
            compiler_params=PARAMS,
            cost_estimate=COST,
            input_output_aliases=aliases,
        )(*args)

    places = pieces_of(dests, rows)
    kinds = tuple(shape((1, end - begin, width), BF16) for _, begin, end in places)
    own = call(cut, [VMEM], kinds, [], x)
    other = [trade(value) for value in own]
    kron = call(
        make_kron, [VMEM], shape((chan, phys * GROUP, phys * GROUP), BF16),
        [pltpu.VMEM((chan * phys, phys * GROUP), F32)], ops,
    )
    right_t, image, mine = call(
        first_local, [SMEM] + [VMEM] * 4,
        (shape(right.shape, BF16), wave_f32, sums_kind), pair_scratch,
        rel, kron, x, left, right,
    )
    image, mine = call(
        first_remote, [SMEM] + [VMEM] * 6, (wave_f32, sums_kind), pair_scratch,
        rel, kron, other[0], left, right_t, image, mine, aliases={5: 0},
    )
    theirs = trade(mine)
    image = call(
        more_remote, [SMEM] + [VMEM] * 5, wave_f32, pair_scratch,
        rel, kron, other[1], left, right_t, image, aliases={5: 0},
    )
    image, first_guess = call(
        functools.partial(first_finish, 0), [SMEM] + [VMEM] * 8,
        (wave_f32, kinds[0]), pair_scratch,
        rel, kron, other[2], left, right_t, image, x, mine, theirs, aliases={5: 0},
    )
    image, head, tail, guess = call(
        functools.partial(first_finish, 1), [SMEM] + [VMEM] * 9,
        (wave_f32, kinds[1], kinds[2], wave_b16), pair_scratch,
        rel, kron, other[2], left, right_t, image, x, mine, theirs, first_guess, aliases={5: 0},
    )
    other = [trade(first_guess), trade(head), trade(tail)]
    acc = call(
        local_sources, [SMEM] + [VMEM] * 4, wave_f32, pair_scratch,
        rel, kron, guess, left, right_t,
    )
    acc, early_sums = call(
        second_remote, [SMEM] * 2 + [VMEM] * 8, (wave_f32, sums_kind), pair_scratch,
        rel, ranks[0], kron, other[0], left, right_t, acc, x, image, guess, aliases={6: 0},
    )
    acc = call(
        more_remote, [SMEM] + [VMEM] * 5, wave_f32, pair_scratch,
        rel, kron, other[1], left, right_t, acc, aliases={5: 0},
    )
    kept, my_sums = call(
        second_finish, [SMEM] * 2 + [VMEM] * 10, (wave_f32, shape((16, LANES), F32)), pair_scratch,
        rel, ranks[0], kron, other[2], left, right_t, acc, x, guess, mine, theirs, early_sums,
        aliases={6: 0},
    )
    their_sums = trade(my_sums)

    env_scale = 1.0 / math.sqrt(phys * rows)
    cells = float(total_blocks * rows * width)
    early, later = 8, 8

    def mid(count):
        pairs = next(n for n in (2, 3, 1) if count % (2 * n) == 0)
        return [pltpu.VMEM((pairs * dests, width, 2 * LANES), BF16)]

    def sent(value, steps):
        count = lax.axis_size("seg")
        begin, end = max(0, -steps), min(count, count - steps)
        return lax.ppermute(value, "seg", [(s, s + steps) for s in range(begin, end)])

    def env_kind(count):
        return shape((count,) + left.shape[1:], BF16)

    def env_call(begin, count, env, inner, outer):
        return call(
            functools.partial(environments, begin, count, env_scale),
            [VMEM] * 3, env_kind(count), mid(count), env, inner, outer,
        )

    new_state, state_kept, turned, piece = pl.pallas_call(
        functools.partial(normalize_and_left, 0, early, env_scale, cells),
        in_specs=[SMEM] + [VMEM] * 8,
        out_specs=(HBM, VMEM, VMEM, VMEM),
        out_shape=(wave_b16, wave_b16, wave_b16, env_kind(early)),
        scratch_shapes=mid(early) + [pltpu.SemaphoreType.DMA],
        compiler_params=PARAMS,
        cost_estimate=COST,
    )(ranks[0], kept, guess, x, mine, theirs, my_sums, their_sums, left)
    pieces = [
        sent(piece, 1),
        sent(env_call(0, later, right, turned, state_kept), -1),
        sent(env_call(early, chan - early, left, state_kept, turned), 1),
        sent(env_call(later, chan - later, right, turned, state_kept), -1),
    ]
    env_f32 = shape(left.shape, F32)

    def widened(places, values, filled):
        count = len(values)
        return pl.pallas_call(
            functools.partial(widen, places),
            in_specs=[VMEM] * count + [HBM] * len(filled),
            out_specs=(HBM, HBM),
            out_shape=(env_f32, env_f32),
            input_output_aliases={count + n: n for n in range(len(filled))},
            scratch_shapes=[pltpu.VMEM(left.shape, F32)] * 2 + [pltpu.SemaphoreType.DMA((chan,))],
            compiler_params=PARAMS,
            cost_estimate=COST,
        )(*values, *filled)

    filled = widened(((0, 0),), pieces[:1], ())
    filled = widened(((1, 0),), pieces[1:2], filled)
    received_left, received_right = widened(((0, early), (1, later)), pieces[2:], filled)
    return (new_state[None], received_left[None], received_right[None])


def solution(mesh):
    placed = (
        P("seg", "blk", None, None),
        P("seg", None, "blk", None, None),
        P("seg", None, "blk", None, None),
        P("seg", None, None, None),
        P("seg", None, None),
        P("seg", "blk"),
    )
    return jax.shard_map(
        shards,
        mesh=mesh,
        in_specs=placed,
        out_specs=(
            P("seg", "blk", None, None),
            P("seg", None, "blk", None, None),
            P("seg", None, "blk", None, None),
        ),
        check_vma=False,
    )
```

```python
import functools
import math

import jax
import jax.numpy as jnp
from jax import lax
from jax.experimental import pallas as pl
from jax.experimental.pallas import tpu as pltpu
from jax.sharding import PartitionSpec as P

STEP_SIZE = 0.25
EPSILON = 1e-06
LANES = 128
GROUP = 8
CHUNK = 32
F32 = jnp.float32
BF16 = jnp.bfloat16
VMEM = pl.BlockSpec(memory_space=pltpu.VMEM)
HBM = pl.BlockSpec(memory_space=pltpu.HBM)
SMEM = pl.BlockSpec(memory_space=pltpu.SMEM)
COST = pl.CostEstimate(flops=1024, bytes_accessed=1024, transcendentals=0)
PARAMS = pltpu.CompilerParams(vmem_limit_bytes=32 * 1024 * 1024)


def dot(left, right):
    return lax.dot_general(
        left, right, (((1,), (0,)), ((), ())), preferred_element_type=F32
    )


def pieces_of(blocks, rows):
    last = rows - rows // 4
    whole = [(b, 0, rows) for b in range(blocks - 1)]
    return whole + [(blocks - 1, 0, last), (blocks - 1, last, rows)]


def make_kron(ops_ref, kron_ref, spread_ref):
    chan, phys, _ = ops_ref.shape
    wide = phys * GROUP
    columns = lax.broadcasted_iota(jnp.int32, (phys, wide), 1)
    spread = (columns // GROUP == lax.broadcasted_iota(jnp.int32, (phys, wide), 0)).astype(F32)
    spread_ref[...] = dot(ops_ref[...].reshape(chan * phys, phys), spread.astype(BF16))
    same = lax.broadcasted_iota(jnp.int32, (GROUP, wide), 1) % GROUP == lax.broadcasted_iota(
        jnp.int32, (GROUP, wide), 0
    )

    def one(k, carry):
        rows = spread_ref[pl.ds(pl.multiple_of(k * phys, phys), phys), :]
        full = [
            jnp.where(same, jnp.broadcast_to(rows[p : p + 1], (GROUP, wide)), 0.0)
            for p in range(phys)
        ]
        kron_ref[k] = jnp.concatenate(full, axis=0).astype(BF16)
        return carry

    lax.fori_loop(0, chan, one, 0)


def list_pairs(rel_ref, low, high, chan_list, src_list, live_list, dest_list, only=None):
    chan, dests = rel_ref.shape
    place = jnp.int32(0)
    for b in range(dests) if only is None else only:
        for source in range(low, high):
            for k in range(chan):
                chan_list[place] = k
                src_list[place] = source - low
                live_list[place] = 1
                dest_list[place] = b
                place = place + jnp.where(rel_ref[k, b] == source, 1, 0)
            chan_list[place] = 0
            src_list[place] = source - low
            live_list[place] = 0
            dest_list[place] = b
            place = place + lax.rem(place, 2)
    return place // 2


def add_pairs(
    steps, lists, kron_ref, x_ref, left_ref, right_t_ref, acc_ref, turned_ref, mixed_ref, start=0
):
    chan_list, src_list, live_list, dest_list = lists
    rows = x_ref.shape[1]
    phys = x_ref.shape[2] // LANES
    groups = rows // GROUP

    def lanes(n):
        return slice(n * LANES, (n + 1) * LANES)

    def act_right(s):
        source, dest = src_list[2 * s], dest_list[2 * s]
        tall = jnp.concatenate([x_ref[source, :, lanes(q)] for q in range(phys)], axis=0)
        second = right_t_ref[chan_list[2 * s + 1], dest]
        second = jnp.where(live_list[2 * s + 1] > 0, second, jnp.zeros_like(second))
        out = dot(tall, jnp.concatenate([right_t_ref[chan_list[2 * s], dest], second], axis=1))
        for i in range(2):
            for g in range(groups):
                turned_ref[i, g] = jnp.concatenate(
                    [
                        out[q * rows + g * GROUP : q * rows + (g + 1) * GROUP, lanes(i)]
                        for q in range(phys)
                    ],
                    axis=0,
                ).astype(BF16)

    def act_site(s):
        for i in range(2):
            kron = kron_ref[chan_list[2 * s + i]]
            for h in range(groups // 2):
                both = jnp.concatenate([turned_ref[i, 2 * h], turned_ref[i, 2 * h + 1]], axis=1)
                out = dot(kron, both)
                r0 = i * rows + 2 * h * GROUP
                for p in range(phys):
                    row = slice(p * GROUP, (p + 1) * GROUP)
                    mixed_ref[r0 : r0 + 2 * GROUP, lanes(p)] = jnp.concatenate(
                        [out[row, lanes(0)], out[row, lanes(1)]], axis=0
                    ).astype(BF16)

    def act_left(s):
        dest = dest_list[2 * s]
        left = jnp.concatenate(
            [left_ref[chan_list[2 * s + i], dest][:, start : start + rows] for i in range(2)], axis=1
        )
        acc_ref[dest] += dot(left, mixed_ref[0 : 2 * rows, :])

    def middle(s, carry):
        act_site(s)
        act_right(s + 1)
        act_left(s)
        return carry

    @pl.when(steps > 0)
    def _():
        act_right(0)
        lax.fori_loop(0, steps - 1, middle, 0)
        act_site(steps - 1)
        act_left(steps - 1)


def fold(values):
    total = values[:, :LANES]
    for p in range(1, values.shape[1] // LANES):
        total = total + values[:, p * LANES : (p + 1) * LANES]
    return total


def row_loop(blocks, rows, body, count, first=0):
    zeros = tuple(jnp.zeros((CHUNK, LANES), F32) for _ in range(count))
    per = rows // CHUNK

    def step(n, carry):
        start = pl.multiple_of(lax.rem(n, per) * CHUNK, CHUNK)
        return body(first + n // per, pl.ds(start, CHUNK), start, carry)

    return lax.fori_loop(0, blocks * per, step, zeros)


def kept_rows(rank, start):
    row = start + lax.broadcasted_iota(jnp.int32, (CHUNK, LANES), 0)
    return (row < rank).astype(F32)


def put_sums(out_ref, values, first=0):
    for n, value in enumerate(values):
        out_ref[first + n : first + n + 1, :] = jnp.full((1, LANES), 1.0, F32) * jnp.sum(value)


def common_shift(mine_ref, theirs_ref):
    num = mine_ref[0:1, :] + theirs_ref[0:1, :]
    den = mine_ref[1:2, :] + theirs_ref[1:2, :]
    return jnp.where(den > 0, num / jnp.where(den > 0, den, 1.0), 0.0)


def cut(first, x_ref, *out_refs):
    for (b, begin, end), out_ref in zip(pieces_of(*x_ref.shape[:2])[first:], out_refs):
        out_ref[0] = x_ref[b, begin:end]


def first_local(
    rel_ref, ops_ref, x_ref, left_ref, right_ref,
    kron_ref, right_t_ref, image_ref, sums_ref,
    turned_ref, mixed_ref, *scratch,
):
    lists, spread_ref = scratch[:-1], scratch[-1]
    make_kron(ops_ref, kron_ref, spread_ref)
    chan, dests = left_ref.shape[:2]

    def turn(n, carry):
        for k in range(2):
            for b in range(dests):
                right_t_ref[2 * n + k, b] = right_ref[2 * n + k, b].T
        return carry

    lax.fori_loop(0, chan // 2, turn, 0)
    image_ref[...] = jnp.zeros_like(image_ref)
    steps = list_pairs(rel_ref, 0, dests, *lists)
    add_pairs(steps, lists, kron_ref, x_ref, left_ref, right_t_ref, image_ref, turned_ref, mixed_ref)

    def sums(b, r, start, carry):
        x = x_ref[b, r, :].astype(F32)
        return carry[0] + fold(x * image_ref[b, r, :]), carry[1] + fold(x * x)

    totals = row_loop(dests, x_ref.shape[1], sums, 2)
    sums_ref[...] = jnp.zeros_like(sums_ref)
    put_sums(sums_ref, totals)


def more_remote(
    block, rel_ref, kron_ref, other_ref, left_ref, right_t_ref, before_ref,
    acc_ref,
    turned_ref, mixed_ref, *lists,
):
    low = left_ref.shape[1] + block
    steps = list_pairs(rel_ref, low, low + 1, *lists)
    add_pairs(steps, lists, kron_ref, other_ref, left_ref, right_t_ref, acc_ref, turned_ref, mixed_ref)


def first_remote(
    rel_ref, kron_ref, other_ref, left_ref, right_t_ref, before_ref, local_sums_ref,
    acc_ref, sums_ref, *scratch,
):
    sums_ref[...] = local_sums_ref[...]
    more_remote(
        left_ref.shape[1] - 1, rel_ref, kron_ref, other_ref, left_ref, right_t_ref, before_ref,
        acc_ref, *scratch,
    )


def first_finish(
    dest, rel_ref, kron_ref, other_ref, left_ref, right_t_ref, before_ref, x_ref, mine_ref,
    theirs_ref, *refs,
):
    dests = left_ref.shape[1]
    last = dest == dests - 1
    if last:
        earlier_ref, acc_ref, head_ref, tail_ref, all_ref = refs[:5]
        all_ref[0:dest] = earlier_ref[...]
    else:
        acc_ref, guess_ref = refs[:2]
    turned_ref, mixed_ref = refs[-6:-4]
    lists = refs[-4:]
    rows = x_ref.shape[1]
    begin = rows - other_ref.shape[1]
    steps = list_pairs(rel_ref, dests + 1, 2 * dests, *lists, only=(dest,))
    add_pairs(
        steps, lists, kron_ref, other_ref, left_ref, right_t_ref, acc_ref, turned_ref, mixed_ref, begin
    )
    shift = common_shift(mine_ref, theirs_ref)
    keep_state = jnp.tile(1.0 + STEP_SIZE * shift, (1, x_ref.shape[2] // LANES))

    def update(b, r, start, carry):
        x = x_ref[b, r, :].astype(F32)
        guess = (keep_state * x - STEP_SIZE * acc_ref[b, r, :]).astype(BF16)
        if last:
            all_ref[b, r, :] = guess
        else:
            guess_ref[0, r, :] = guess
        return carry

    row_loop(1, rows, update, 0, first=dest)
    if last:
        head_ref[0] = all_ref[dest, 0:begin]
        tail_ref[0] = all_ref[dest, begin:rows]


def second_local(
    rel_ref, rank_ref, kron_ref, guess_ref, left_ref, right_t_ref, x_ref, image_ref,
    acc_ref, sums_ref,
    turned_ref, mixed_ref, *lists,
):
    dests, rows, _ = x_ref.shape
    acc_ref[...] = jnp.zeros_like(acc_ref)
    steps = list_pairs(rel_ref, 0, dests, *lists)
    add_pairs(steps, lists, kron_ref, guess_ref, left_ref, right_t_ref, acc_ref, turned_ref, mixed_ref)

    def sums(b, r, start, carry):
        x = x_ref[b, r, :].astype(F32)
        guess = guess_ref[b, r, :].astype(F32)
        image = image_ref[b, r, :]
        keep = kept_rows(rank_ref[b], start)
        xx, xg, gg = fold(x * x), fold(x * guess), fold(guess * guess)
        new = (fold(x * image), xx, fold(guess * image), xg, gg, keep * gg, keep * xx, keep * xg)
        return tuple(total + value for total, value in zip(carry, new))

    put_sums(sums_ref, row_loop(dests, rows, sums, 8))


def second_finish(
    rel_ref, rank_ref, kron_ref, other_ref, left_ref, right_t_ref, before_ref, x_ref, guess_ref,
    mine_ref, theirs_ref, early_ref,
    kept_ref, sums_ref,
    turned_ref, mixed_ref, *lists,
):
    dests, rows, width = x_ref.shape
    steps = list_pairs(rel_ref, dests + 1, 2 * dests, *lists)
    add_pairs(
        steps, lists, kron_ref, other_ref, left_ref, right_t_ref, kept_ref, turned_ref, mixed_ref,
        rows - other_ref.shape[1],
    )
    shift = common_shift(mine_ref, theirs_ref)
    keep_guess = jnp.tile(1.0 + STEP_SIZE * shift, (1, width // LANES))

    def sums(b, r, start, carry):
        x = x_ref[b, r, :].astype(F32)
        guess = guess_ref[b, r, :].astype(F32)
        kept = keep_guess * guess - STEP_SIZE * kept_ref[b, r, :]
        kept_ref[b, r, :] = kept
        keep = kept_rows(rank_ref[b], start)
        kg, kx = fold(kept * guess), fold(kept * x)
        new = (kg, kx, keep * kg, keep * kx, keep * fold(kept * kept))
        return tuple(total + value for total, value in zip(carry, new))

    totals = row_loop(dests, rows, sums, 5)
    sums_ref[0:8, :] = early_ref[...]
    put_sums(sums_ref, totals, first=8)
    sums_ref[13:16, :] = jnp.zeros((3, LANES), F32)


def normalize(
    cells, rank_ref, kept_ref, guess_ref, x_ref, mine_ref, theirs_ref, my_sums_ref, their_sums_ref,
    state_ref, turned_ref,
):
    both = my_sums_ref[...] + their_sums_ref[...]
    xv, xx, gv, xg, gg, gg_kept, xx_kept, xg_kept, kg, kx, kg_kept, kx_kept, kk_kept = (
        both[n : n + 1] for n in range(13)
    )
    shift = common_shift(mine_ref, theirs_ref)
    delta = STEP_SIZE * (xv / xx - shift)
    scale = (1.0 + STEP_SIZE * shift) / STEP_SIZE
    gw, xw = scale * gg - kg / STEP_SIZE, scale * xg - kx / STEP_SIZE
    num = gw + delta * (xw + gv + delta * xv)
    den = gg + delta * (2.0 * xg + delta * xx)
    beta = STEP_SIZE * (num / den - shift)
    of_guess, of_state = beta + delta, beta * delta
    norm = (
        kk_kept
        + of_guess * (2.0 * kg_kept + of_guess * gg_kept)
        + of_state * (2.0 * kx_kept + of_state * xx_kept + 2.0 * of_guess * xg_kept)
    )
    gain = jnp.sqrt(cells / (jnp.maximum(norm, 0.0) + EPSILON))
    blocks, rows, width = kept_ref.shape
    group = 8 * LANES
    per = width // group
    row = lax.broadcasted_iota(jnp.int32, (rows, LANES), 0)

    def one(n, carry):
        b = n // per
        factor = jnp.where(row < rank_ref[b], gain, 0.0)
        for p in range(8):
            cols = pl.ds(pl.multiple_of(lax.rem(n, per) * group + p * LANES, LANES), LANES)
            kept = (
                kept_ref[b, :, cols]
                + of_guess * guess_ref[b, :, cols].astype(F32)
                + of_state * x_ref[b, :, cols].astype(F32)
            )
            state = (kept * factor).astype(BF16)
            state_ref[b, :, cols] = state
            turned_ref[b, :, cols] = state.T
        return carry

    lax.fori_loop(0, blocks * per, one, 0)


def environments(first, count, scale, env_ref, inner_ref, outer_ref, out_ref, mid_ref):
    dests, rows, width = outer_ref.shape
    phys = width // LANES
    pairs = mid_ref.shape[0] // dests

    def step(n, carry):
        for j in range(pairs):
            k = first + 2 * (n * pairs + j)
            for b in range(dests):
                env = jnp.concatenate([env_ref[k, b], env_ref[k + 1, b]], axis=0)
                mid = dot(env, inner_ref[b]).astype(BF16)
                for p in range(phys):
                    for i in range(2):
                        mid_ref[
                            j * dests + b, p * rows : (p + 1) * rows, i * LANES : (i + 1) * LANES
                        ] = mid[i * rows : (i + 1) * rows, p * LANES : (p + 1) * LANES]
        for j in range(pairs):
            place = 2 * (n * pairs + j)
            for b in range(dests):
                out = (dot(outer_ref[b], mid_ref[j * dests + b]) * scale).astype(BF16)
                out_ref[place, b] = out[:, :LANES]
                out_ref[place + 1, b] = out[:, LANES:]
        return carry

    lax.fori_loop(0, count // (2 * pairs), step, 0)


def normalize_and_left(
    first, count, scale, cells,
    rank_ref, kept_ref, guess_ref, x_ref, mine_ref, theirs_ref, my_sums_ref, their_sums_ref, env_ref,
    new_ref, state_ref, turned_ref, out_ref,
    mid_ref, sem,
):
    normalize(
        cells, rank_ref, kept_ref, guess_ref, x_ref, mine_ref, theirs_ref, my_sums_ref,
        their_sums_ref, state_ref, turned_ref,
    )
    copy = pltpu.make_async_copy(state_ref, new_ref, sem)
    copy.start()
    environments(first, count, scale, env_ref, state_ref, turned_ref, out_ref, mid_ref)
    copy.wait()


def widen(places, *refs):
    pieces, (outs, wides, sems) = refs[: len(places)], (refs[-5:-3], refs[-3:-1], refs[-1])
    copies = []
    for piece, (side, begin) in zip(pieces, places):
        for n in range(0, piece.shape[0], 2):
            span = pl.ds(begin + n, 2)
            wides[side][begin + n : begin + n + 2] = piece[n : n + 2].astype(F32)
            copy = pltpu.make_async_copy(
                wides[side].at[span], outs[side].at[span], sems.at[len(copies)]
            )
            copy.start()
            copies.append(copy)
    for copy in copies:
        copy.wait()


def shards(state, left_env, right_env, site_ops, sector_map, ranks):
    dests, rows, width = state.shape[1:]
    chan, phys = site_ops.shape[1:3]
    groups = lax.axis_size("blk")
    total_blocks = groups * dests
    first_block = lax.axis_index("blk") * dests
    x, left, right, ops = state[0], left_env[0], right_env[0], site_ops[0]
    local_map = lax.dynamic_slice_in_dim(sector_map[0], first_block, dests, 1)
    rel = lax.rem(local_map - first_block + total_blocks, total_blocks)

    swap = [(g, groups - 1 - g) for g in range(groups)]

    def trade(value):
        return lax.ppermute(value, "blk", swap)

    def shape(dims, kind):
        return jax.ShapeDtypeStruct(dims, kind)

    wave = (dests, rows, width)
    wave_f32 = shape(wave, F32)
    wave_b16 = shape(wave, BF16)
    sums_kind = shape((8, LANES), F32)
    lists = [pltpu.SMEM((chan * dests + 2 * dests * dests + 1,), jnp.int32)] * 4
    pair_scratch = [
        pltpu.VMEM((2, rows // GROUP, phys * GROUP, LANES), BF16),
        pltpu.VMEM((2 * rows, width), BF16),
    ] + lists

    def call(body, specs, outs, scratch, *args, aliases={}):
        return pl.pallas_call(
            body,
            in_specs=specs,
            out_specs=jax.tree.map(lambda _: VMEM, outs),
            out_shape=outs,
            scratch_shapes=scratch,
            compiler_params=PARAMS,
            cost_estimate=COST,
            input_output_aliases=aliases,
        )(*args)

    places = pieces_of(dests, rows)
    kinds = tuple(shape((1, end - begin, width), BF16) for _, begin, end in places)
    own = [
        call(functools.partial(cut, 0), [VMEM], kinds[0], [], x),
        *call(functools.partial(cut, 1), [VMEM], kinds[1:], [], x),
    ]
    other = [trade(value) for value in own]
    kron, right_t, image, mine = call(
        first_local, [SMEM] + [VMEM] * 4,
        (
            shape((chan, phys * GROUP, phys * GROUP), BF16), shape(right.shape, BF16), wave_f32,
            sums_kind,
        ),
        pair_scratch + [pltpu.VMEM((chan * phys, phys * GROUP), F32)],
        rel, ops, x, left, right,
    )
    image = call(
        functools.partial(more_remote, 0), [SMEM] + [VMEM] * 5, wave_f32, pair_scratch,
        rel, kron, other[0], left, right_t, image, aliases={5: 0},
    )
    image, mine = call(
        first_remote, [SMEM] + [VMEM] * 6, (wave_f32, sums_kind), pair_scratch,
        rel, kron, other[1], left, right_t, image, mine, aliases={5: 0},
    )
    theirs = trade(mine)
    image, first_guess = call(
        functools.partial(first_finish, 0), [SMEM] + [VMEM] * 8,
        (wave_f32, kinds[0]), pair_scratch,
        rel, kron, other[2], left, right_t, image, x, mine, theirs, aliases={5: 0},
    )
    image, head, tail, guess = call(
        functools.partial(first_finish, 1), [SMEM] + [VMEM] * 9,
        (wave_f32, kinds[1], kinds[2], wave_b16), pair_scratch,
        rel, kron, other[2], left, right_t, image, x, mine, theirs, first_guess, aliases={5: 0},
    )
    other = [trade(first_guess), trade(head), trade(tail)]
    acc, early_sums = call(
        second_local, [SMEM] * 2 + [VMEM] * 6, (wave_f32, sums_kind), pair_scratch,
        rel, ranks[0], kron, guess, left, right_t, x, image,
    )
    acc = call(
        functools.partial(more_remote, 0), [SMEM] + [VMEM] * 5, wave_f32, pair_scratch,
        rel, kron, other[0], left, right_t, acc, aliases={5: 0},
    )
    acc = call(
        functools.partial(more_remote, 1), [SMEM] + [VMEM] * 5, wave_f32, pair_scratch,
        rel, kron, other[1], left, right_t, acc, aliases={5: 0},
    )
    kept, my_sums = call(
        second_finish, [SMEM] * 2 + [VMEM] * 10, (wave_f32, shape((16, LANES), F32)), pair_scratch,
        rel, ranks[0], kron, other[2], left, right_t, acc, x, guess, mine, theirs, early_sums,
        aliases={6: 0},
    )
    their_sums = trade(my_sums)

    env_scale = 1.0 / math.sqrt(phys * rows)
    cells = float(total_blocks * rows * width)
    early, later = 8, 8

    def mid(count):
        pairs = next(n for n in (2, 3, 1) if count % (2 * n) == 0)
        return [pltpu.VMEM((pairs * dests, width, 2 * LANES), BF16)]

    def sent(value, steps):
        count = lax.axis_size("seg")
        begin, end = max(0, -steps), min(count, count - steps)
        return lax.ppermute(value, "seg", [(s, s + steps) for s in range(begin, end)])

    def env_kind(count):
        return shape((count,) + left.shape[1:], BF16)

    def env_call(begin, count, env, inner, outer):
        return call(
            functools.partial(environments, begin, count, env_scale),
            [VMEM] * 3, env_kind(count), mid(count), env, inner, outer,
        )

    new_state, state_kept, turned, piece = pl.pallas_call(
        functools.partial(normalize_and_left, 0, early, env_scale, cells),
        in_specs=[SMEM] + [VMEM] * 8,
        out_specs=(HBM, VMEM, VMEM, VMEM),
        out_shape=(wave_b16, wave_b16, wave_b16, env_kind(early)),
        scratch_shapes=mid(early) + [pltpu.SemaphoreType.DMA],
        compiler_params=PARAMS,
        cost_estimate=COST,
    )(ranks[0], kept, guess, x, mine, theirs, my_sums, their_sums, left)
    pieces = [
        sent(piece, 1),
        sent(env_call(0, later, right, turned, state_kept), -1),
        sent(env_call(early, chan - early, left, state_kept, turned), 1),
        sent(env_call(later, chan - later, right, turned, state_kept), -1),
    ]
    env_f32 = shape(left.shape, F32)

    def widened(places, values, filled):
        count = len(values)
        return pl.pallas_call(
            functools.partial(widen, places),
            in_specs=[VMEM] * count + [HBM] * len(filled),
            out_specs=(HBM, HBM),
            out_shape=(env_f32, env_f32),
            input_output_aliases={count + n: n for n in range(len(filled))},
            scratch_shapes=[pltpu.VMEM(left.shape, F32)] * 2 + [pltpu.SemaphoreType.DMA((chan,))],
            compiler_params=PARAMS,
            cost_estimate=COST,
        )(*values, *filled)

    filled = widened(((0, 0),), pieces[:1], ())
    filled = widened(((1, 0),), pieces[1:2], filled)
    received_left, received_right = widened(((0, early), (1, later)), pieces[2:], filled)
    return (new_state[None], received_left[None], received_right[None])


def solution(mesh):
    placed = (
        P("seg", "blk", None, None),
        P("seg", None, "blk", None, None),
        P("seg", None, "blk", None, None),
        P("seg", None, None, None),
        P("seg", None, None),
        P("seg", "blk"),
    )
    return jax.shard_map(
        shards,
        mesh=mesh,
        in_specs=placed,
        out_specs=(
            P("seg", "blk", None, None),
            P("seg", None, "blk", None, None),
            P("seg", None, "blk", None, None),
        ),
        check_vma=False,
    )
```

```python
import functools
import math

import jax
import jax.numpy as jnp
from jax import lax
from jax.experimental import pallas as pl
from jax.experimental.pallas import tpu as pltpu
from jax.sharding import PartitionSpec as P

STEP_SIZE = 0.25
EPSILON = 1e-06
LANES = 128
GROUP = 8
CHUNK = 32
F32 = jnp.float32
BF16 = jnp.bfloat16
VMEM = pl.BlockSpec(memory_space=pltpu.VMEM)
HBM = pl.BlockSpec(memory_space=pltpu.HBM)
SMEM = pl.BlockSpec(memory_space=pltpu.SMEM)
COST = pl.CostEstimate(flops=1024, bytes_accessed=1024, transcendentals=0)
PARAMS = pltpu.CompilerParams(vmem_limit_bytes=32 * 1024 * 1024)


def dot(left, right):
    return lax.dot_general(
        left, right, (((1,), (0,)), ((), ())), preferred_element_type=F32
    )


def make_kron(ops_ref, kron_ref, spread_ref):
    chan, phys, _ = ops_ref.shape
    wide = phys * GROUP
    columns = lax.broadcasted_iota(jnp.int32, (phys, wide), 1)
    spread = (columns // GROUP == lax.broadcasted_iota(jnp.int32, (phys, wide), 0)).astype(F32)
    spread_ref[...] = dot(ops_ref[...].reshape(chan * phys, phys), spread.astype(BF16))
    same = lax.broadcasted_iota(jnp.int32, (GROUP, wide), 1) % GROUP == lax.broadcasted_iota(
        jnp.int32, (GROUP, wide), 0
    )

    def one(k, carry):
        rows = spread_ref[pl.ds(pl.multiple_of(k * phys, phys), phys), :]
        full = [
            jnp.where(same, jnp.broadcast_to(rows[p : p + 1], (GROUP, wide)), 0.0)
            for p in range(phys)
        ]
        kron_ref[k] = jnp.concatenate(full, axis=0).astype(BF16)
        return carry

    lax.fori_loop(0, chan, one, 0)


def list_pairs(rel_ref, low, high, chan_list, src_list, live_list, dest_list, only=None):
    chan, dests = rel_ref.shape
    place = jnp.int32(0)
    for b in range(dests) if only is None else only:
        for source in range(low, high):
            for k in range(chan):
                chan_list[place] = k
                src_list[place] = source - low
                live_list[place] = 1
                dest_list[place] = b
                place = place + jnp.where(rel_ref[k, b] == source, 1, 0)
            chan_list[place] = 0
            src_list[place] = source - low
            live_list[place] = 0
            dest_list[place] = b
            place = place + lax.rem(place, 2)
    return place // 2


def add_pairs(
    steps, lists, kron_ref, x_ref, left_ref, right_t_ref, acc_ref, turned_ref, mixed_ref, start=0
):
    chan_list, src_list, live_list, dest_list = lists
    rows = x_ref.shape[1]
    phys = x_ref.shape[2] // LANES
    groups = rows // GROUP

    def lanes(n):
        return slice(n * LANES, (n + 1) * LANES)

    def act_right(s):
        source, dest = src_list[2 * s], dest_list[2 * s]
        tall = jnp.concatenate([x_ref[source, :, lanes(q)] for q in range(phys)], axis=0)
        second = right_t_ref[chan_list[2 * s + 1], dest]
        second = jnp.where(live_list[2 * s + 1] > 0, second, jnp.zeros_like(second))
        out = dot(tall, jnp.concatenate([right_t_ref[chan_list[2 * s], dest], second], axis=1))
        for i in range(2):
            for g in range(groups):
                turned_ref[i, g] = jnp.concatenate(
                    [
                        out[q * rows + g * GROUP : q * rows + (g + 1) * GROUP, lanes(i)]
                        for q in range(phys)
                    ],
                    axis=0,
                ).astype(BF16)

    def act_site(s):
        for i in range(2):
            kron = kron_ref[chan_list[2 * s + i]]
            for h in range(groups // 2):
                both = jnp.concatenate([turned_ref[i, 2 * h], turned_ref[i, 2 * h + 1]], axis=1)
                out = dot(kron, both)
                r0 = i * rows + 2 * h * GROUP
                for p in range(phys):
                    row = slice(p * GROUP, (p + 1) * GROUP)
                    mixed_ref[r0 : r0 + 2 * GROUP, lanes(p)] = jnp.concatenate(
                        [out[row, lanes(0)], out[row, lanes(1)]], axis=0
                    ).astype(BF16)

    def act_left(s):
        dest = dest_list[2 * s]
        left = jnp.concatenate(
            [left_ref[chan_list[2 * s + i], dest][:, start : start + rows] for i in range(2)], axis=1
        )
        acc_ref[dest] += dot(left, mixed_ref[0 : 2 * rows, :])

    def middle(s, carry):
        act_site(s)
        act_right(s + 1)
        act_left(s)
        return carry

    @pl.when(steps > 0)
    def _():
        act_right(0)
        lax.fori_loop(0, steps - 1, middle, 0)
        act_site(steps - 1)
        act_left(steps - 1)


def fold(values):
    total = values[:, :LANES]
    for p in range(1, values.shape[1] // LANES):
        total = total + values[:, p * LANES : (p + 1) * LANES]
    return total


def row_loop(blocks, rows, body, count, first=0):
    zeros = tuple(jnp.zeros((CHUNK, LANES), F32) for _ in range(count))
    per = rows // CHUNK

    def step(n, carry):
        start = pl.multiple_of(lax.rem(n, per) * CHUNK, CHUNK)
        return body(first + n // per, pl.ds(start, CHUNK), start, carry)

    return lax.fori_loop(0, blocks * per, step, zeros)


def kept_rows(rank, start):
    row = start + lax.broadcasted_iota(jnp.int32, (CHUNK, LANES), 0)
    return (row < rank).astype(F32)


def put_sums(out_ref, values, first=0):
    for n, value in enumerate(values):
        out_ref[first + n : first + n + 1, :] = jnp.full((1, LANES), 1.0, F32) * jnp.sum(value)


def common_shift(mine_ref, theirs_ref):
    num = mine_ref[0:1, :] + theirs_ref[0:1, :]
    den = mine_ref[1:2, :] + theirs_ref[1:2, :]
    return jnp.where(den > 0, num / jnp.where(den > 0, den, 1.0), 0.0)


def cut(x_ref, *out_refs):
    for b, out_ref in enumerate(out_refs):
        out_ref[0] = x_ref[b]


def first_local(
    rel_ref, kron_ref, x_ref, left_ref, right_ref,
    right_t_ref, image_ref, sums_ref,
    turned_ref, mixed_ref, *lists,
):
    chan, dests = left_ref.shape[:2]

    def turn(n, carry):
        for k in range(2):
            for b in range(dests):
                right_t_ref[2 * n + k, b] = right_ref[2 * n + k, b].T
        return carry

    lax.fori_loop(0, chan // 2, turn, 0)
    image_ref[...] = jnp.zeros_like(image_ref)
    steps = list_pairs(rel_ref, 0, dests, *lists)
    add_pairs(steps, lists, kron_ref, x_ref, left_ref, right_t_ref, image_ref, turned_ref, mixed_ref)

    def sums(b, r, start, carry):
        x = x_ref[b, r, :].astype(F32)
        return carry[0] + fold(x * image_ref[b, r, :]), carry[1] + fold(x * x)

    totals = row_loop(dests, x_ref.shape[1], sums, 2)
    sums_ref[...] = jnp.zeros_like(sums_ref)
    put_sums(sums_ref, totals)


def more_remote(
    block, rel_ref, kron_ref, other_ref, left_ref, right_t_ref, before_ref,
    acc_ref,
    turned_ref, mixed_ref, *lists,
):
    low = left_ref.shape[1] + block
    steps = list_pairs(rel_ref, low, low + 1, *lists)
    add_pairs(steps, lists, kron_ref, other_ref, left_ref, right_t_ref, acc_ref, turned_ref, mixed_ref)


def first_remote(
    rel_ref, kron_ref, other_ref, left_ref, right_t_ref, before_ref, local_sums_ref,
    acc_ref, sums_ref, *scratch,
):
    sums_ref[...] = local_sums_ref[...]
    more_remote(
        0, rel_ref, kron_ref, other_ref, left_ref, right_t_ref, before_ref,
        acc_ref, *scratch,
    )


def first_finish(
    dest, rel_ref, kron_ref, other_ref, left_ref, right_t_ref, before_ref, x_ref, mine_ref,
    theirs_ref, *refs,
):
    dests = left_ref.shape[1]
    last = dest == dests - 1
    if last:
        earlier_ref, acc_ref, head_ref, tail_ref, all_ref = refs[:5]
        all_ref[0:dest] = earlier_ref[...]
    else:
        acc_ref, guess_ref = refs[:2]
    turned_ref, mixed_ref = refs[-6:-4]
    lists = refs[-4:]
    rows = x_ref.shape[1]
    begin = rows - other_ref.shape[1]
    steps = list_pairs(rel_ref, dests + 1, 2 * dests, *lists, only=(dest,))
    add_pairs(
        steps, lists, kron_ref, other_ref, left_ref, right_t_ref, acc_ref, turned_ref, mixed_ref, begin
    )
    shift = common_shift(mine_ref, theirs_ref)
    keep_state = jnp.tile(1.0 + STEP_SIZE * shift, (1, x_ref.shape[2] // LANES))

    def update(b, r, start, carry):
        x = x_ref[b, r, :].astype(F32)
        guess = (keep_state * x - STEP_SIZE * acc_ref[b, r, :]).astype(BF16)
        if last:
            all_ref[b, r, :] = guess
        else:
            guess_ref[0, r, :] = guess
        return carry

    row_loop(1, rows, update, 0, first=dest)
    if last:
        cut_row = head_ref.shape[1]
        head_ref[0] = all_ref[dest, 0:cut_row]
        tail_ref[0] = all_ref[dest, cut_row:rows]


def second_local(
    rel_ref, rank_ref, kron_ref, guess_ref, left_ref, right_t_ref, x_ref, image_ref,
    acc_ref, sums_ref,
    turned_ref, mixed_ref, *lists,
):
    dests, rows, _ = x_ref.shape
    acc_ref[...] = jnp.zeros_like(acc_ref)
    steps = list_pairs(rel_ref, 0, dests, *lists)
    add_pairs(steps, lists, kron_ref, guess_ref, left_ref, right_t_ref, acc_ref, turned_ref, mixed_ref)

    def sums(b, r, start, carry):
        x = x_ref[b, r, :].astype(F32)
        guess = guess_ref[b, r, :].astype(F32)
        image = image_ref[b, r, :]
        keep = kept_rows(rank_ref[b], start)
        xx, xg, gg = fold(x * x), fold(x * guess), fold(guess * guess)
        new = (fold(x * image), xx, fold(guess * image), xg, gg, keep * gg, keep * xx, keep * xg)
        return tuple(total + value for total, value in zip(carry, new))

    put_sums(sums_ref, row_loop(dests, rows, sums, 8))


def second_finish(
    rel_ref, rank_ref, kron_ref, other_ref, left_ref, right_t_ref, before_ref, x_ref, guess_ref,
    mine_ref, theirs_ref, early_ref,
    kept_ref, sums_ref,
    turned_ref, mixed_ref, *lists,
):
    dests, rows, width = x_ref.shape
    steps = list_pairs(rel_ref, dests + 1, 2 * dests, *lists)
    add_pairs(
        steps, lists, kron_ref, other_ref, left_ref, right_t_ref, kept_ref, turned_ref, mixed_ref,
        rows - other_ref.shape[1],
    )
    shift = common_shift(mine_ref, theirs_ref)
    keep_guess = jnp.tile(1.0 + STEP_SIZE * shift, (1, width // LANES))

    def sums(b, r, start, carry):
        x = x_ref[b, r, :].astype(F32)
        guess = guess_ref[b, r, :].astype(F32)
        kept = keep_guess * guess - STEP_SIZE * kept_ref[b, r, :]
        kept_ref[b, r, :] = kept
        keep = kept_rows(rank_ref[b], start)
        kg, kx = fold(kept * guess), fold(kept * x)
        new = (kg, kx, keep * kg, keep * kx, keep * fold(kept * kept))
        return tuple(total + value for total, value in zip(carry, new))

    totals = row_loop(dests, rows, sums, 5)
    sums_ref[0:8, :] = early_ref[...]
    put_sums(sums_ref, totals, first=8)
    sums_ref[13:16, :] = jnp.zeros((3, LANES), F32)


def normalize(
    cells, rank_ref, kept_ref, guess_ref, x_ref, mine_ref, theirs_ref, my_sums_ref, their_sums_ref,
    state_ref, turned_ref,
):
    both = my_sums_ref[...] + their_sums_ref[...]
    xv, xx, gv, xg, gg, gg_kept, xx_kept, xg_kept, kg, kx, kg_kept, kx_kept, kk_kept = (
        both[n : n + 1] for n in range(13)
    )
    shift = common_shift(mine_ref, theirs_ref)
    delta = STEP_SIZE * (xv / xx - shift)
    scale = (1.0 + STEP_SIZE * shift) / STEP_SIZE
    gw, xw = scale * gg - kg / STEP_SIZE, scale * xg - kx / STEP_SIZE
    num = gw + delta * (xw + gv + delta * xv)
    den = gg + delta * (2.0 * xg + delta * xx)
    beta = STEP_SIZE * (num / den - shift)
    of_guess, of_state = beta + delta, beta * delta
    norm = (
        kk_kept
        + of_guess * (2.0 * kg_kept + of_guess * gg_kept)
        + of_state * (2.0 * kx_kept + of_state * xx_kept + 2.0 * of_guess * xg_kept)
    )
    gain = jnp.sqrt(cells / (jnp.maximum(norm, 0.0) + EPSILON))
    blocks, rows, width = kept_ref.shape
    group = 8 * LANES
    per = width // group
    row = lax.broadcasted_iota(jnp.int32, (rows, LANES), 0)

    def one(n, carry):
        b = n // per
        factor = jnp.where(row < rank_ref[b], gain, 0.0)
        for p in range(8):
            cols = pl.ds(pl.multiple_of(lax.rem(n, per) * group + p * LANES, LANES), LANES)
            kept = (
                kept_ref[b, :, cols]
                + of_guess * guess_ref[b, :, cols].astype(F32)
                + of_state * x_ref[b, :, cols].astype(F32)
            )
            state = (kept * factor).astype(BF16)
            state_ref[b, :, cols] = state
            turned_ref[b, :, cols] = state.T
        return carry

    lax.fori_loop(0, blocks * per, one, 0)


def environments(first, count, scale, env_ref, inner_ref, outer_ref, out_ref, mid_ref):
    dests, rows, width = outer_ref.shape
    phys = width // LANES
    pairs = mid_ref.shape[0] // dests

    def step(n, carry):
        for j in range(pairs):
            k = first + 2 * (n * pairs + j)
            for b in range(dests):
                env = jnp.concatenate([env_ref[k, b], env_ref[k + 1, b]], axis=0)
                mid = dot(env, inner_ref[b]).astype(BF16)
                for p in range(phys):
                    for i in range(2):
                        mid_ref[
                            j * dests + b, p * rows : (p + 1) * rows, i * LANES : (i + 1) * LANES
                        ] = mid[i * rows : (i + 1) * rows, p * LANES : (p + 1) * LANES]
        for j in range(pairs):
            place = 2 * (n * pairs + j)
            for b in range(dests):
                out = (dot(outer_ref[b], mid_ref[j * dests + b]) * scale).astype(BF16)
                out_ref[place, b] = out[:, :LANES]
                out_ref[place + 1, b] = out[:, LANES:]
        return carry

    lax.fori_loop(0, count // (2 * pairs), step, 0)


def normalize_and_left(
    first, count, scale, cells,
    rank_ref, kept_ref, guess_ref, x_ref, mine_ref, theirs_ref, my_sums_ref, their_sums_ref, env_ref,
    new_ref, state_ref, turned_ref, out_ref,
    mid_ref, sem,
):
    normalize(
        cells, rank_ref, kept_ref, guess_ref, x_ref, mine_ref, theirs_ref, my_sums_ref,
        their_sums_ref, state_ref, turned_ref,
    )
    copy = pltpu.make_async_copy(state_ref, new_ref, sem)
    copy.start()
    environments(first, count, scale, env_ref, state_ref, turned_ref, out_ref, mid_ref)
    copy.wait()


def widen(places, *refs):
    pieces, (outs, wides, sems) = refs[: len(places)], (refs[-5:-3], refs[-3:-1], refs[-1])
    copies = []
    for piece, (side, begin) in zip(pieces, places):
        for n in range(0, piece.shape[0], 2):
            span = pl.ds(begin + n, 2)
            wides[side][begin + n : begin + n + 2] = piece[n : n + 2].astype(F32)
            copy = pltpu.make_async_copy(
                wides[side].at[span], outs[side].at[span], sems.at[len(copies)]
            )
            copy.start()
            copies.append(copy)
    for copy in copies:
        copy.wait()


def shards(state, left_env, right_env, site_ops, sector_map, ranks):
    dests, rows, width = state.shape[1:]
    chan, phys = site_ops.shape[1:3]
    groups = lax.axis_size("blk")
    total_blocks = groups * dests
    first_block = lax.axis_index("blk") * dests
    x, left, right, ops = state[0], left_env[0], right_env[0], site_ops[0]
    local_map = lax.dynamic_slice_in_dim(sector_map[0], first_block, dests, 1)
    rel = lax.rem(local_map - first_block + total_blocks, total_blocks)

    swap = [(g, groups - 1 - g) for g in range(groups)]

    def trade(value):
        return lax.ppermute(value, "blk", swap)

    def shape(dims, kind):
        return jax.ShapeDtypeStruct(dims, kind)

    wave = (dests, rows, width)
    wave_f32 = shape(wave, F32)
    wave_b16 = shape(wave, BF16)
    sums_kind = shape((8, LANES), F32)
    lists = [pltpu.SMEM((chan * dests + 2 * dests * dests + 1,), jnp.int32)] * 4
    pair_scratch = [
        pltpu.VMEM((2, rows // GROUP, phys * GROUP, LANES), BF16),
        pltpu.VMEM((2 * rows, width), BF16),
    ] + lists

    def call(body, specs, outs, scratch, *args, aliases={}):
        return pl.pallas_call(
            body,
            in_specs=specs,
            out_specs=jax.tree.map(lambda _: VMEM, outs),
            out_shape=outs,
            scratch_shapes=scratch,
            compiler_params=PARAMS,
            cost_estimate=COST,
            input_output_aliases=aliases,
        )(*args)

    block = shape((1, rows, width), BF16)
    own = call(cut, [VMEM], (block,) * dests, [], x)
    other = [trade(value) for value in own]
    kron = call(
        make_kron, [VMEM], shape((chan, phys * GROUP, phys * GROUP), BF16),
        [pltpu.VMEM((chan * phys, phys * GROUP), F32)], ops,
    )
    right_t, image, mine = call(
        first_local, [SMEM] + [VMEM] * 4,
        (shape(right.shape, BF16), wave_f32, sums_kind), pair_scratch,
        rel, kron, x, left, right,
    )
    image, mine = call(
        first_remote, [SMEM] + [VMEM] * 6, (wave_f32, sums_kind), pair_scratch,
        rel, kron, other[0], left, right_t, image, mine, aliases={5: 0},
    )
    theirs = trade(mine)
    image, first_guess = call(
        functools.partial(first_finish, 0), [SMEM] + [VMEM] * 8,
        (wave_f32, block), pair_scratch,
        rel, kron, other[1], left, right_t, image, x, mine, theirs, aliases={5: 0},
    )
    tail_rows = rows // 4
    image, head, tail, guess = call(
        functools.partial(first_finish, 1), [SMEM] + [VMEM] * 9,
        (
            wave_f32, shape((1, rows - tail_rows, width), BF16), shape((1, tail_rows, width), BF16),
            wave_b16,
        ),
        pair_scratch,
        rel, kron, other[1], left, right_t, image, x, mine, theirs, first_guess, aliases={5: 0},
    )
    other = [trade(first_guess), trade(head), trade(tail)]
    acc, early_sums = call(
        second_local, [SMEM] * 2 + [VMEM] * 6, (wave_f32, sums_kind), pair_scratch,
        rel, ranks[0], kron, guess, left, right_t, x, image,
    )
    for n in range(2):
        acc = call(
            functools.partial(more_remote, n), [SMEM] + [VMEM] * 5, wave_f32, pair_scratch,
            rel, kron, other[n], left, right_t, acc, aliases={5: 0},
        )
    kept, my_sums = call(
        second_finish, [SMEM] * 2 + [VMEM] * 10, (wave_f32, shape((16, LANES), F32)), pair_scratch,
        rel, ranks[0], kron, other[2], left, right_t, acc, x, guess, mine, theirs, early_sums,
        aliases={6: 0},
    )
    their_sums = trade(my_sums)

    env_scale = 1.0 / math.sqrt(phys * rows)
    cells = float(total_blocks * rows * width)
    early, later = 8, 8

    def mid(count):
        pairs = next(n for n in (2, 3, 1) if count % (2 * n) == 0)
        return [pltpu.VMEM((pairs * dests, width, 2 * LANES), BF16)]

    def sent(value, steps):
        count = lax.axis_size("seg")
        begin, end = max(0, -steps), min(count, count - steps)
        return lax.ppermute(value, "seg", [(s, s + steps) for s in range(begin, end)])

    def env_kind(count):
        return shape((count,) + left.shape[1:], BF16)

    def env_call(begin, count, env, inner, outer):
        return call(
            functools.partial(environments, begin, count, env_scale),
            [VMEM] * 3, env_kind(count), mid(count), env, inner, outer,
        )

    new_state, state_kept, turned, piece = pl.pallas_call(
        functools.partial(normalize_and_left, 0, early, env_scale, cells),
        in_specs=[SMEM] + [VMEM] * 8,
        out_specs=(HBM, VMEM, VMEM, VMEM),
        out_shape=(wave_b16, wave_b16, wave_b16, env_kind(early)),
        scratch_shapes=mid(early) + [pltpu.SemaphoreType.DMA],
        compiler_params=PARAMS,
        cost_estimate=COST,
    )(ranks[0], kept, guess, x, mine, theirs, my_sums, their_sums, left)
    pieces = [
        sent(piece, 1),
        sent(env_call(0, later, right, turned, state_kept), -1),
        sent(env_call(early, chan - early, left, state_kept, turned), 1),
        sent(env_call(later, chan - later, right, turned, state_kept), -1),
    ]
    env_f32 = shape(left.shape, F32)

    def widened(places, values, filled):
        count = len(values)
        return pl.pallas_call(
            functools.partial(widen, places),
            in_specs=[VMEM] * count + [HBM] * len(filled),
            out_specs=(HBM, HBM),
            out_shape=(env_f32, env_f32),
            input_output_aliases={count + n: n for n in range(len(filled))},
            scratch_shapes=[pltpu.VMEM(left.shape, F32)] * 2 + [pltpu.SemaphoreType.DMA((chan,))],
            compiler_params=PARAMS,
            cost_estimate=COST,
        )(*values, *filled)

    filled = widened(((0, 0),), pieces[:1], ())
    filled = widened(((1, 0),), pieces[1:2], filled)
    received_left, received_right = widened(((0, early), (1, later)), pieces[2:], filled)
    return (new_state[None], received_left[None], received_right[None])


def solution(mesh):
    placed = (
        P("seg", "blk", None, None),
        P("seg", None, "blk", None, None),
        P("seg", None, "blk", None, None),
        P("seg", None, None, None),
        P("seg", None, None),
        P("seg", "blk"),
    )
    return jax.shard_map(
        shards,
        mesh=mesh,
        in_specs=placed,
        out_specs=(
            P("seg", "blk", None, None),
            P("seg", None, "blk", None, None),
            P("seg", None, "blk", None, None),
        ),
        check_vma=False,
    )
```

```python
import functools
import math

import jax
import jax.numpy as jnp
from jax import lax
from jax.experimental import pallas as pl
from jax.experimental.pallas import tpu as pltpu
from jax.sharding import PartitionSpec as P

STEP_SIZE = 0.25
EPSILON = 1e-06
LANES = 128
GROUP = 8
CHUNK = 32
F32 = jnp.float32
BF16 = jnp.bfloat16
VMEM = pl.BlockSpec(memory_space=pltpu.VMEM)
HBM = pl.BlockSpec(memory_space=pltpu.HBM)
SMEM = pl.BlockSpec(memory_space=pltpu.SMEM)
COST = pl.CostEstimate(flops=1024, bytes_accessed=1024, transcendentals=0)
PARAMS = pltpu.CompilerParams(vmem_limit_bytes=32 * 1024 * 1024)


def dot(left, right):
    return lax.dot_general(
        left, right, (((1,), (0,)), ((), ())), preferred_element_type=F32
    )


def make_kron(ops_ref, kron_ref, spread_ref):
    chan, phys, _ = ops_ref.shape
    wide = phys * GROUP
    columns = lax.broadcasted_iota(jnp.int32, (phys, wide), 1)
    spread = (columns // GROUP == lax.broadcasted_iota(jnp.int32, (phys, wide), 0)).astype(F32)
    spread_ref[...] = dot(ops_ref[...].reshape(chan * phys, phys), spread.astype(BF16))
    same = lax.broadcasted_iota(jnp.int32, (GROUP, wide), 1) % GROUP == lax.broadcasted_iota(
        jnp.int32, (GROUP, wide), 0
    )

    def one(k, carry):
        rows = spread_ref[pl.ds(pl.multiple_of(k * phys, phys), phys), :]
        full = [
            jnp.where(same, jnp.broadcast_to(rows[p : p + 1], (GROUP, wide)), 0.0)
            for p in range(phys)
        ]
        kron_ref[k] = jnp.concatenate(full, axis=0).astype(BF16)
        return carry

    lax.fori_loop(0, chan, one, 0)


def list_pairs(rel_ref, low, high, chan_list, src_list, live_list, dest_list, only=None):
    chan, dests = rel_ref.shape
    place = jnp.int32(0)
    for b in range(dests) if only is None else only:
        for source in range(low, high):
            for k in range(chan):
                chan_list[place] = k
                src_list[place] = source - low
                live_list[place] = 1
                dest_list[place] = b
                place = place + jnp.where(rel_ref[k, b] == source, 1, 0)
            chan_list[place] = 0
            src_list[place] = source - low
            live_list[place] = 0
            dest_list[place] = b
            place = place + lax.rem(place, 2)
    return place // 2


def add_pairs(steps, lists, kron_ref, x_ref, left_ref, right_t_ref, acc_ref, turned_ref, mixed_ref):
    chan_list, src_list, live_list, dest_list = lists
    rows = x_ref.shape[1]
    phys = x_ref.shape[2] // LANES
    groups = rows // GROUP

    def lanes(n):
        return slice(n * LANES, (n + 1) * LANES)

    def act_right(s):
        source, dest = src_list[2 * s], dest_list[2 * s]
        tall = jnp.concatenate([x_ref[source, :, lanes(q)] for q in range(phys)], axis=0)
        second = right_t_ref[chan_list[2 * s + 1], dest]
        second = jnp.where(live_list[2 * s + 1] > 0, second, jnp.zeros_like(second))
        out = dot(tall, jnp.concatenate([right_t_ref[chan_list[2 * s], dest], second], axis=1))
        for i in range(2):
            for g in range(groups):
                turned_ref[i, g] = jnp.concatenate(
                    [
                        out[q * rows + g * GROUP : q * rows + (g + 1) * GROUP, lanes(i)]
                        for q in range(phys)
                    ],
                    axis=0,
                ).astype(BF16)

    def act_site(s):
        for i in range(2):
            kron = kron_ref[chan_list[2 * s + i]]
            for h in range(groups // 2):
                both = jnp.concatenate([turned_ref[i, 2 * h], turned_ref[i, 2 * h + 1]], axis=1)
                out = dot(kron, both)
                r0 = i * rows + 2 * h * GROUP
                for p in range(phys):
                    row = slice(p * GROUP, (p + 1) * GROUP)
                    mixed_ref[r0 : r0 + 2 * GROUP, lanes(p)] = jnp.concatenate(
                        [out[row, lanes(0)], out[row, lanes(1)]], axis=0
                    ).astype(BF16)

    def act_left(s):
        dest = dest_list[2 * s]
        left = jnp.concatenate(
            [left_ref[chan_list[2 * s], dest], left_ref[chan_list[2 * s + 1], dest]], axis=1
        )
        acc_ref[dest] += dot(left, mixed_ref[...])

    def middle(s, carry):
        act_site(s)
        act_right(s + 1)
        act_left(s)
        return carry

    @pl.when(steps > 0)
    def _():
        act_right(0)
        lax.fori_loop(0, steps - 1, middle, 0)
        act_site(steps - 1)
        act_left(steps - 1)


def fold(values):
    total = values[:, :LANES]
    for p in range(1, values.shape[1] // LANES):
        total = total + values[:, p * LANES : (p + 1) * LANES]
    return total


def row_loop(blocks, rows, body, count, first=0):
    zeros = tuple(jnp.zeros((CHUNK, LANES), F32) for _ in range(count))
    per = rows // CHUNK

    def step(n, carry):
        start = pl.multiple_of(lax.rem(n, per) * CHUNK, CHUNK)
        return body(first + n // per, pl.ds(start, CHUNK), start, carry)

    return lax.fori_loop(0, blocks * per, step, zeros)


def kept_rows(rank, start):
    row = start + lax.broadcasted_iota(jnp.int32, (CHUNK, LANES), 0)
    return (row < rank).astype(F32)


def put_sums(out_ref, values, first=0):
    for n, value in enumerate(values):
        out_ref[first + n : first + n + 1, :] = jnp.full((1, LANES), 1.0, F32) * jnp.sum(value)


def common_shift(mine_ref, theirs_ref):
    num = mine_ref[0:1, :] + theirs_ref[0:1, :]
    den = mine_ref[1:2, :] + theirs_ref[1:2, :]
    return jnp.where(den > 0, num / jnp.where(den > 0, den, 1.0), 0.0)


def choose_order(map_ref, rel_ref, arrived_ref, order_ref):
    chan, dests = rel_ref.shape
    for k in range(chan):
        for b in range(dests):
            rel_ref[k, b] = map_ref[k, b]

    def uses(first, source):
        total = jnp.int32(0)
        for k in range(chan):
            for b in range(first, first + dests):
                total = total + jnp.where(map_ref[k, b] == source, 1, 0)
        return total

    swap_mine = uses(dests, 0) < uses(dests, 1)
    swap_theirs = uses(0, dests) < uses(0, dests + 1)
    order_ref[0] = jnp.where(swap_mine, 1, 0)
    order_ref[1] = jnp.where(swap_mine, 0, 1)
    for k in range(chan):
        for b in range(dests):
            source = rel_ref[k, b]
            other = 2 * dests + 1 - source
            arrived_ref[k, b] = jnp.where(swap_theirs & (source >= dests), other, source)


def cut(b, x_ref, out_ref):
    out_ref[0] = x_ref[b]


def first_local(
    map_ref, kron_ref, x_ref, left_ref, right_ref,
    right_t_ref, image_ref, sums_ref, rel_ref, arrived_ref, order_ref,
    turned_ref, mixed_ref, *lists,
):
    choose_order(map_ref, rel_ref, arrived_ref, order_ref)
    chan, dests = left_ref.shape[:2]

    def turn(n, carry):
        for k in range(2):
            for b in range(dests):
                right_t_ref[2 * n + k, b] = right_ref[2 * n + k, b].T
        return carry

    lax.fori_loop(0, chan // 2, turn, 0)
    image_ref[...] = jnp.zeros_like(image_ref)
    steps = list_pairs(rel_ref, 0, dests, *lists)
    add_pairs(steps, lists, kron_ref, x_ref, left_ref, right_t_ref, image_ref, turned_ref, mixed_ref)

    def sums(b, r, start, carry):
        x = x_ref[b, r, :].astype(F32)
        return carry[0] + fold(x * image_ref[b, r, :]), carry[1] + fold(x * x)

    totals = row_loop(dests, x_ref.shape[1], sums, 2)
    sums_ref[...] = jnp.zeros_like(sums_ref)
    put_sums(sums_ref, totals)


def remote_sources(
    rel_ref, kron_ref, other_ref, left_ref, right_t_ref, before_ref,
    acc_ref,
    turned_ref, mixed_ref, *lists,
):
    dests = left_ref.shape[1]
    steps = list_pairs(rel_ref, dests, dests + 1, *lists)
    add_pairs(steps, lists, kron_ref, other_ref, left_ref, right_t_ref, acc_ref, turned_ref, mixed_ref)


def first_remote(
    rel_ref, kron_ref, other_ref, left_ref, right_t_ref, before_ref, local_sums_ref,
    acc_ref, sums_ref,
    turned_ref, mixed_ref, *lists,
):
    dests = left_ref.shape[1]
    sums_ref[...] = local_sums_ref[...]
    steps = list_pairs(rel_ref, dests, dests + 1, *lists)
    add_pairs(steps, lists, kron_ref, other_ref, left_ref, right_t_ref, acc_ref, turned_ref, mixed_ref)


def first_finish(
    turn, rel_ref, order_ref, kron_ref, other_ref, left_ref, right_t_ref, before_ref, x_ref,
    mine_ref, theirs_ref, *refs,
):
    dests, rows = x_ref.shape[:2]
    dest = order_ref[turn]
    last = turn == dests - 1
    if last:
        earlier_ref, acc_ref, guess_ref, all_ref = refs[:4]
        all_ref[order_ref[0]] = earlier_ref[0]
    else:
        acc_ref, guess_ref = refs[:2]
    turned_ref, mixed_ref = refs[-6:-4]
    lists = refs[-4:]
    steps = list_pairs(rel_ref, dests + 1, 2 * dests, *lists, only=(dest,))
    add_pairs(steps, lists, kron_ref, other_ref, left_ref, right_t_ref, acc_ref, turned_ref, mixed_ref)
    shift = common_shift(mine_ref, theirs_ref)
    keep_state = jnp.tile(1.0 + STEP_SIZE * shift, (1, x_ref.shape[2] // LANES))

    def update(b, r, start, carry):
        x = x_ref[b, r, :].astype(F32)
        guess = (keep_state * x - STEP_SIZE * acc_ref[b, r, :]).astype(BF16)
        guess_ref[0, r, :] = guess
        if last:
            all_ref[b, r, :] = guess
        return carry

    row_loop(1, rows, update, 0, first=dest)


def second_local(
    rel_ref, rank_ref, kron_ref, guess_ref, left_ref, right_t_ref, x_ref, image_ref,
    acc_ref, sums_ref,
    turned_ref, mixed_ref, *lists,
):
    dests, rows, _ = x_ref.shape
    acc_ref[...] = jnp.zeros_like(acc_ref)
    steps = list_pairs(rel_ref, 0, dests, *lists)
    add_pairs(steps, lists, kron_ref, guess_ref, left_ref, right_t_ref, acc_ref, turned_ref, mixed_ref)

    def sums(b, r, start, carry):
        x = x_ref[b, r, :].astype(F32)
        guess = guess_ref[b, r, :].astype(F32)
        image = image_ref[b, r, :]
        keep = kept_rows(rank_ref[b], start)
        xx, xg, gg = fold(x * x), fold(x * guess), fold(guess * guess)
        new = (fold(x * image), xx, fold(guess * image), xg, gg, keep * gg, keep * xx, keep * xg)
        return tuple(total + value for total, value in zip(carry, new))

    put_sums(sums_ref, row_loop(dests, rows, sums, 8))


def second_finish(
    rel_ref, rank_ref, kron_ref, other_ref, left_ref, right_t_ref, before_ref, x_ref, guess_ref,
    mine_ref, theirs_ref, early_ref,
    kept_ref, sums_ref,
    turned_ref, mixed_ref, *lists,
):
    dests, rows, width = x_ref.shape
    steps = list_pairs(rel_ref, dests + 1, 2 * dests, *lists)
    add_pairs(steps, lists, kron_ref, other_ref, left_ref, right_t_ref, kept_ref, turned_ref, mixed_ref)
    shift = common_shift(mine_ref, theirs_ref)
    keep_guess = jnp.tile(1.0 + STEP_SIZE * shift, (1, width // LANES))

    def sums(b, r, start, carry):
        x = x_ref[b, r, :].astype(F32)
        guess = guess_ref[b, r, :].astype(F32)
        kept = keep_guess * guess - STEP_SIZE * kept_ref[b, r, :]
        kept_ref[b, r, :] = kept
        keep = kept_rows(rank_ref[b], start)
        kg, kx = fold(kept * guess), fold(kept * x)
        new = (kg, kx, keep * kg, keep * kx, keep * fold(kept * kept))
        return tuple(total + value for total, value in zip(carry, new))

    totals = row_loop(dests, rows, sums, 5)
    sums_ref[0:8, :] = early_ref[...]
    put_sums(sums_ref, totals, first=8)
    sums_ref[13:16, :] = jnp.zeros((3, LANES), F32)


def normalize(
    cells, rank_ref, kept_ref, guess_ref, x_ref, mine_ref, theirs_ref, my_sums_ref, their_sums_ref,
    state_ref,
):
    both = my_sums_ref[...] + their_sums_ref[...]
    xv, xx, gv, xg, gg, gg_kept, xx_kept, xg_kept, kg, kx, kg_kept, kx_kept, kk_kept = (
        both[n : n + 1] for n in range(13)
    )
    shift = common_shift(mine_ref, theirs_ref)
    delta = STEP_SIZE * (xv / xx - shift)
    scale = (1.0 + STEP_SIZE * shift) / STEP_SIZE
    gw, xw = scale * gg - kg / STEP_SIZE, scale * xg - kx / STEP_SIZE
    num = gw + delta * (xw + gv + delta * xv)
    den = gg + delta * (2.0 * xg + delta * xx)
    beta = STEP_SIZE * (num / den - shift)
    of_guess, of_state = beta + delta, beta * delta
    norm = (
        kk_kept
        + of_guess * (2.0 * kg_kept + of_guess * gg_kept)
        + of_state * (2.0 * kx_kept + of_state * xx_kept + 2.0 * of_guess * xg_kept)
    )
    gain = jnp.sqrt(cells / (jnp.maximum(norm, 0.0) + EPSILON))
    blocks, rows, width = kept_ref.shape
    group = 8 * LANES
    per = width // group
    row = lax.broadcasted_iota(jnp.int32, (rows, LANES), 0)

    def one(n, carry):
        b = n // per
        factor = jnp.where(row < rank_ref[b], gain, 0.0)
        for p in range(8):
            cols = pl.ds(pl.multiple_of(lax.rem(n, per) * group + p * LANES, LANES), LANES)
            kept = (
                kept_ref[b, :, cols]
                + of_guess * guess_ref[b, :, cols].astype(F32)
                + of_state * x_ref[b, :, cols].astype(F32)
            )
            state_ref[b, :, cols] = (kept * factor).astype(BF16)
        return carry

    lax.fori_loop(0, blocks * per, one, 0)


def env_middle(k, b, env_ref, inner_ref, mid_ref, place):
    rows, width = inner_ref.shape[1:]
    env = jnp.concatenate([env_ref[k, b], env_ref[k + 1, b]], axis=0)
    mid = dot(env, inner_ref[b]).astype(BF16)
    for p in range(width // LANES):
        for i in range(2):
            mid_ref[place, p * rows : (p + 1) * rows, i * LANES : (i + 1) * LANES] = mid[
                i * rows : (i + 1) * rows, p * LANES : (p + 1) * LANES
            ]


def env_result(k, b, scale, outer_ref, mid_ref, place, out_ref):
    out = (dot(outer_ref[b], mid_ref[place]) * scale).astype(BF16)
    out_ref[k, b] = out[:, :LANES]
    out_ref[k + 1, b] = out[:, LANES:]


def environments(first, count, scale, env_ref, inner_ref, outer_ref, out_ref, mid_ref):
    dests = outer_ref.shape[0]
    pairs = mid_ref.shape[0] // dests

    def step(n, carry):
        for j in range(pairs):
            for b in range(dests):
                env_middle(first + 2 * (n * pairs + j), b, env_ref, inner_ref, mid_ref, j * dests + b)
        for j in range(pairs):
            for b in range(dests):
                env_result(2 * (n * pairs + j), b, scale, outer_ref, mid_ref, j * dests + b, out_ref)
        return carry

    lax.fori_loop(0, count // (2 * pairs), step, 0)


def left_beside_turn(count, scale, env_ref, state_ref, turned_ref, out_ref, mid_ref):
    dests, _, width = state_ref.shape
    phys = width // LANES
    rounds = count // 4
    tiles = dests * phys // rounds

    def before(n, carry):
        for t in range(tiles):
            tile = n * tiles + t
            cols = pl.ds(pl.multiple_of(lax.rem(tile, phys) * LANES, LANES), LANES)
            turned_ref[tile // phys, :, cols] = state_ref[tile // phys, :, cols].T
        for j in range(2):
            for b in range(dests):
                place = (2 * n + j) * dests + b
                env_middle(2 * (2 * n + j), b, env_ref, state_ref, mid_ref, place)
        return carry

    def after(n, carry):
        for j in range(2):
            for b in range(dests):
                place = (2 * n + j) * dests + b
                env_result(2 * (2 * n + j), b, scale, turned_ref, mid_ref, place, out_ref)
        return carry

    lax.fori_loop(0, rounds, before, 0)
    lax.fori_loop(0, rounds, after, 0)


def normalize_and_left(
    count, scale, cells,
    rank_ref, kept_ref, guess_ref, x_ref, mine_ref, theirs_ref, my_sums_ref, their_sums_ref, env_ref,
    new_ref, state_ref, turned_ref, out_ref,
    mid_ref, sem,
):
    normalize(
        cells, rank_ref, kept_ref, guess_ref, x_ref, mine_ref, theirs_ref, my_sums_ref,
        their_sums_ref, state_ref,
    )
    copy = pltpu.make_async_copy(state_ref, new_ref, sem)
    copy.start()
    left_beside_turn(count, scale, env_ref, state_ref, turned_ref, out_ref, mid_ref)
    copy.wait()


def widen(places, *refs):
    pieces, (outs, wides, sems) = refs[: len(places)], (refs[-5:-3], refs[-3:-1], refs[-1])
    copies = []
    for piece, (side, begin) in zip(pieces, places):
        for n in range(0, piece.shape[0], 2):
            span = pl.ds(begin + n, 2)
            wides[side][begin + n : begin + n + 2] = piece[n : n + 2].astype(F32)
            copy = pltpu.make_async_copy(
                wides[side].at[span], outs[side].at[span], sems.at[len(copies)]
            )
            copy.start()
            copies.append(copy)
    for copy in copies:
        copy.wait()


def shards(state, left_env, right_env, site_ops, sector_map, ranks):
    dests, rows, width = state.shape[1:]
    chan, phys = site_ops.shape[1:3]
    groups = lax.axis_size("blk")
    total_blocks = groups * dests
    first_block = lax.axis_index("blk") * dests
    x, left, right, ops = state[0], left_env[0], right_env[0], site_ops[0]

    twice = jnp.concatenate([sector_map[0]] * 2, axis=1)
    turned_map = lax.dynamic_slice_in_dim(twice, first_block, total_blocks, 1)
    turned_map = lax.rem(turned_map - first_block + total_blocks, total_blocks)

    swap = [(g, groups - 1 - g) for g in range(groups)]

    def trade(value):
        return lax.ppermute(value, "blk", swap)

    def shape(dims, kind):
        return jax.ShapeDtypeStruct(dims, kind)

    wave = (dests, rows, width)
    wave_f32 = shape(wave, F32)
    wave_b16 = shape(wave, BF16)
    sums_kind = shape((8, LANES), F32)
    lists = [pltpu.SMEM((chan * dests + 2 * dests * dests + 1,), jnp.int32)] * 4
    pair_scratch = [
        pltpu.VMEM((2, rows // GROUP, phys * GROUP, LANES), BF16),
        pltpu.VMEM((2 * rows, width), BF16),
    ] + lists

    def call(body, specs, outs, scratch, *args, aliases={}, out_specs=None):
        return pl.pallas_call(
            body,
            in_specs=specs,
            out_specs=out_specs or jax.tree.map(lambda _: VMEM, outs),
            out_shape=outs,
            scratch_shapes=scratch,
            compiler_params=PARAMS,
            cost_estimate=COST,
            input_output_aliases=aliases,
        )(*args)

    block = shape((1, rows, width), BF16)
    own = [call(functools.partial(cut, b), [VMEM], block, [], x) for b in range(dests)]
    other = [trade(value) for value in own]
    kron = call(
        make_kron, [VMEM], shape((chan, phys * GROUP, phys * GROUP), BF16),
        [pltpu.VMEM((chan * phys, phys * GROUP), F32)], ops,
    )
    rel_kind = shape((chan, dests), jnp.int32)
    right_t, image, mine, rel, arrived, order = call(
        first_local, [SMEM] + [VMEM] * 4,
        (
            shape(right.shape, BF16), wave_f32, sums_kind, rel_kind, rel_kind,
            shape((dests,), jnp.int32),
        ),
        pair_scratch, turned_map, kron, x, left, right, out_specs=(VMEM,) * 3 + (SMEM,) * 3,
    )
    image, mine = call(
        first_remote, [SMEM] + [VMEM] * 6, (wave_f32, sums_kind), pair_scratch,
        rel, kron, other[0], left, right_t, image, mine, aliases={5: 0},
    )
    theirs = trade(mine)
    image, first_guess = call(
        functools.partial(first_finish, 0), [SMEM] * 2 + [VMEM] * 8,
        (wave_f32, block), pair_scratch,
        rel, order, kron, other[1], left, right_t, image, x, mine, theirs, aliases={6: 0},
    )
    image, last_guess, guess = call(
        functools.partial(first_finish, 1), [SMEM] * 2 + [VMEM] * 9,
        (wave_f32, block, wave_b16), pair_scratch,
        rel, order, kron, other[1], left, right_t, image, x, mine, theirs, first_guess,
        aliases={6: 0},
    )
    other = [trade(first_guess), trade(last_guess)]
    acc, early_sums = call(
        second_local, [SMEM] * 2 + [VMEM] * 6, (wave_f32, sums_kind), pair_scratch,
        arrived, ranks[0], kron, guess, left, right_t, x, image,
    )
    acc = call(
        remote_sources, [SMEM] + [VMEM] * 5, wave_f32, pair_scratch,
        arrived, kron, other[0], left, right_t, acc, aliases={5: 0},
    )
    kept, my_sums = call(
        second_finish, [SMEM] * 2 + [VMEM] * 10, (wave_f32, shape((16, LANES), F32)), pair_scratch,
        arrived, ranks[0], kron, other[1], left, right_t, acc, x, guess, mine, theirs, early_sums,
        aliases={6: 0},
    )
    their_sums = trade(my_sums)

    env_scale = 1.0 / math.sqrt(phys * rows)
    cells = float(total_blocks * rows * width)
    early, later = 8, 8

    def mid(count):
        pairs = next(n for n in (2, 3, 1) if count % (2 * n) == 0)
        return [pltpu.VMEM((pairs * dests, width, 2 * LANES), BF16)]

    def sent(value, steps):
        count = lax.axis_size("seg")
        begin, end = max(0, -steps), min(count, count - steps)
        return lax.ppermute(value, "seg", [(s, s + steps) for s in range(begin, end)])

    def env_kind(count):
        return shape((count,) + left.shape[1:], BF16)

    def env_call(begin, count, env, inner, outer):
        return call(
            functools.partial(environments, begin, count, env_scale),
            [VMEM] * 3, env_kind(count), mid(count), env, inner, outer,
        )

    new_state, state_kept, turned, piece = pl.pallas_call(
        functools.partial(normalize_and_left, early, env_scale, cells),
        in_specs=[SMEM] + [VMEM] * 8,
        out_specs=(HBM, VMEM, VMEM, VMEM),
        out_shape=(wave_b16, wave_b16, wave_b16, env_kind(early)),
        scratch_shapes=[pltpu.VMEM((early // 2 * dests, width, 2 * LANES), BF16)] + [pltpu.SemaphoreType.DMA],
        compiler_params=PARAMS,
        cost_estimate=COST,
    )(ranks[0], kept, guess, x, mine, theirs, my_sums, their_sums, left)
    pieces = [
        sent(piece, 1),
        sent(env_call(0, later, right, turned, state_kept), -1),
        sent(env_call(early, chan - early, left, state_kept, turned), 1),
        sent(env_call(later, chan - later, right, turned, state_kept), -1),
    ]
    env_f32 = shape(left.shape, F32)

    def widened(places, values, filled):
        count = len(values)
        return pl.pallas_call(
            functools.partial(widen, places),
            in_specs=[VMEM] * count + [HBM] * len(filled),
            out_specs=(HBM, HBM),
            out_shape=(env_f32, env_f32),
            input_output_aliases={count + n: n for n in range(len(filled))},
            scratch_shapes=[pltpu.VMEM(left.shape, F32)] * 2 + [pltpu.SemaphoreType.DMA((chan,))],
            compiler_params=PARAMS,
            cost_estimate=COST,
        )(*values, *filled)

    filled = widened(((0, 0),), pieces[:1], ())
    filled = widened(((1, 0),), pieces[1:2], filled)
    received_left, received_right = widened(((0, early), (1, later)), pieces[2:], filled)
    return (new_state[None], received_left[None], received_right[None])


def solution(mesh):
    placed = (
        P("seg", "blk", None, None),
        P("seg", None, "blk", None, None),
        P("seg", None, "blk", None, None),
        P("seg", None, None, None),
        P("seg", None, None),
        P("seg", "blk"),
    )
    return jax.shard_map(
        shards,
        mesh=mesh,
        in_specs=placed,
        out_specs=(
            P("seg", "blk", None, None),
            P("seg", None, "blk", None, None),
            P("seg", None, "blk", None, None),
        ),
        check_vma=False,
    )
```

```python
import functools
import math

import jax
import jax.numpy as jnp
from jax import lax
from jax.experimental import pallas as pl
from jax.experimental.pallas import tpu as pltpu
from jax.sharding import PartitionSpec as P

STEP_SIZE = 0.25
EPSILON = 1e-06
LANES = 128
GROUP = 8
CHUNK = 32
F32 = jnp.float32
BF16 = jnp.bfloat16
VMEM = pl.BlockSpec(memory_space=pltpu.VMEM)
HBM = pl.BlockSpec(memory_space=pltpu.HBM)
SMEM = pl.BlockSpec(memory_space=pltpu.SMEM)
COST = pl.CostEstimate(flops=1024, bytes_accessed=1024, transcendentals=0)
PARAMS = pltpu.CompilerParams(vmem_limit_bytes=32 * 1024 * 1024)


def dot(left, right):
    return lax.dot_general(
        left, right, (((1,), (0,)), ((), ())), preferred_element_type=F32
    )


def make_kron(ops_ref, kron_ref, spread_ref):
    chan, phys, _ = ops_ref.shape
    wide = phys * GROUP
    columns = lax.broadcasted_iota(jnp.int32, (phys, wide), 1)
    spread = (columns // GROUP == lax.broadcasted_iota(jnp.int32, (phys, wide), 0)).astype(F32)
    spread_ref[...] = dot(ops_ref[...].reshape(chan * phys, phys), spread.astype(BF16))
    same = lax.broadcasted_iota(jnp.int32, (GROUP, wide), 1) % GROUP == lax.broadcasted_iota(
        jnp.int32, (GROUP, wide), 0
    )

    def one(k, carry):
        rows = spread_ref[pl.ds(pl.multiple_of(k * phys, phys), phys), :]
        full = [
            jnp.where(same, jnp.broadcast_to(rows[p : p + 1], (GROUP, wide)), 0.0)
            for p in range(phys)
        ]
        kron_ref[k] = jnp.concatenate(full, axis=0).astype(BF16)
        return carry

    lax.fori_loop(0, chan, one, 0)


def list_pairs(rel_ref, low, high, chan_list, src_list, live_list, dest_list, only=None):
    chan, dests = rel_ref.shape
    place = jnp.int32(0)
    for b in range(dests) if only is None else only:
        for source in range(low, high):
            for k in range(chan):
                chan_list[place] = k
                src_list[place] = source - low
                live_list[place] = 1
                dest_list[place] = b
                place = place + jnp.where(rel_ref[k, b] == source, 1, 0)
            chan_list[place] = 0
            src_list[place] = source - low
            live_list[place] = 0
            dest_list[place] = b
            place = place + lax.rem(place, 2)
    return place // 2


def add_pairs(steps, lists, kron_ref, x_ref, left_ref, right_t_ref, acc_ref, turned_ref, mixed_ref):
    chan_list, src_list, live_list, dest_list = lists
    rows = x_ref.shape[1]
    phys = x_ref.shape[2] // LANES
    groups = rows // GROUP

    def lanes(n):
        return slice(n * LANES, (n + 1) * LANES)

    def act_right(s):
        source, dest = src_list[2 * s], dest_list[2 * s]
        tall = jnp.concatenate([x_ref[source, :, lanes(q)] for q in range(phys)], axis=0)
        second = right_t_ref[chan_list[2 * s + 1], dest]
        second = jnp.where(live_list[2 * s + 1] > 0, second, jnp.zeros_like(second))
        out = dot(tall, jnp.concatenate([right_t_ref[chan_list[2 * s], dest], second], axis=1))
        for i in range(2):
            for g in range(groups):
                turned_ref[i, g] = jnp.concatenate(
                    [
                        out[q * rows + g * GROUP : q * rows + (g + 1) * GROUP, lanes(i)]
                        for q in range(phys)
                    ],
                    axis=0,
                ).astype(BF16)

    def act_site(s):
        for i in range(2):
            kron = kron_ref[chan_list[2 * s + i]]
            for h in range(groups // 2):
                both = jnp.concatenate([turned_ref[i, 2 * h], turned_ref[i, 2 * h + 1]], axis=1)
                out = dot(kron, both)
                r0 = i * rows + 2 * h * GROUP
                for p in range(phys):
                    row = slice(p * GROUP, (p + 1) * GROUP)
                    mixed_ref[r0 : r0 + 2 * GROUP, lanes(p)] = jnp.concatenate(
                        [out[row, lanes(0)], out[row, lanes(1)]], axis=0
                    ).astype(BF16)

    def act_left(s):
        dest = dest_list[2 * s]
        left = jnp.concatenate(
            [left_ref[chan_list[2 * s], dest], left_ref[chan_list[2 * s + 1], dest]], axis=1
        )
        acc_ref[dest] += dot(left, mixed_ref[...])

    def middle(s, carry):
        act_site(s)
        act_right(s + 1)
        act_left(s)
        return carry

    @pl.when(steps > 0)
    def _():
        act_right(0)
        lax.fori_loop(0, steps - 1, middle, 0)
        act_site(steps - 1)
        act_left(steps - 1)


def fold(values):
    total = values[:, :LANES]
    for p in range(1, values.shape[1] // LANES):
        total = total + values[:, p * LANES : (p + 1) * LANES]
    return total


def row_loop(blocks, rows, body, count, first=0):
    zeros = tuple(jnp.zeros((CHUNK, LANES), F32) for _ in range(count))
    per = rows // CHUNK

    def step(n, carry):
        start = pl.multiple_of(lax.rem(n, per) * CHUNK, CHUNK)
        return body(first + n // per, pl.ds(start, CHUNK), start, carry)

    return lax.fori_loop(0, blocks * per, step, zeros)


def kept_rows(rank, start):
    row = start + lax.broadcasted_iota(jnp.int32, (CHUNK, LANES), 0)
    return (row < rank).astype(F32)


def put_sums(out_ref, values, first=0):
    for n, value in enumerate(values):
        out_ref[first + n : first + n + 1, :] = jnp.full((1, LANES), 1.0, F32) * jnp.sum(value)


def common_shift(mine_ref, theirs_ref):
    num = mine_ref[0:1, :] + theirs_ref[0:1, :]
    den = mine_ref[1:2, :] + theirs_ref[1:2, :]
    return jnp.where(den > 0, num / jnp.where(den > 0, den, 1.0), 0.0)


def choose_order(map_ref, rel_ref, arrived_ref, order_ref):
    chan, dests = rel_ref.shape
    for k in range(chan):
        for b in range(dests):
            rel_ref[k, b] = map_ref[k, b]

    def uses(first, source):
        total = jnp.int32(0)
        for k in range(chan):
            for b in range(first, first + dests):
                total = total + jnp.where(map_ref[k, b] == source, 1, 0)
        return total

    swap_mine = uses(dests, 0) < uses(dests, 1)
    swap_theirs = uses(0, dests) < uses(0, dests + 1)
    order_ref[0] = jnp.where(swap_mine, 1, 0)
    order_ref[1] = jnp.where(swap_mine, 0, 1)
    for k in range(chan):
        for b in range(dests):
            source = rel_ref[k, b]
            other = 2 * dests + 1 - source
            arrived_ref[k, b] = jnp.where(swap_theirs & (source >= dests), other, source)


def cut(b, x_ref, out_ref):
    out_ref[0] = x_ref[b]


def first_local(
    map_ref, kron_ref, x_ref, left_ref, right_ref,
    right_t_ref, image_ref, sums_ref, rel_ref, arrived_ref, order_ref,
    turned_ref, mixed_ref, *lists,
):
    choose_order(map_ref, rel_ref, arrived_ref, order_ref)
    chan, dests = left_ref.shape[:2]

    def turn(n, carry):
        for k in range(2):
            for b in range(dests):
                right_t_ref[2 * n + k, b] = right_ref[2 * n + k, b].T
        return carry

    lax.fori_loop(0, chan // 2, turn, 0)
    image_ref[...] = jnp.zeros_like(image_ref)
    steps = list_pairs(rel_ref, 0, dests, *lists)
    add_pairs(steps, lists, kron_ref, x_ref, left_ref, right_t_ref, image_ref, turned_ref, mixed_ref)

    def sums(b, r, start, carry):
        x = x_ref[b, r, :].astype(F32)
        return carry[0] + fold(x * image_ref[b, r, :]), carry[1] + fold(x * x)

    totals = row_loop(dests, x_ref.shape[1], sums, 2)
    sums_ref[...] = jnp.zeros_like(sums_ref)
    put_sums(sums_ref, totals)


def remote_sources(
    rel_ref, kron_ref, other_ref, left_ref, right_t_ref, before_ref,
    acc_ref,
    turned_ref, mixed_ref, *lists,
):
    dests = left_ref.shape[1]
    steps = list_pairs(rel_ref, dests, dests + 1, *lists)
    add_pairs(steps, lists, kron_ref, other_ref, left_ref, right_t_ref, acc_ref, turned_ref, mixed_ref)


def first_remote(
    rel_ref, kron_ref, other_ref, left_ref, right_t_ref, before_ref, local_sums_ref,
    acc_ref, sums_ref,
    turned_ref, mixed_ref, *lists,
):
    dests = left_ref.shape[1]
    sums_ref[...] = local_sums_ref[...]
    steps = list_pairs(rel_ref, dests, dests + 1, *lists)
    add_pairs(steps, lists, kron_ref, other_ref, left_ref, right_t_ref, acc_ref, turned_ref, mixed_ref)


def first_finish(
    turn, rel_ref, order_ref, kron_ref, other_ref, left_ref, right_t_ref, before_ref, x_ref,
    mine_ref, theirs_ref, *refs,
):
    dests, rows = x_ref.shape[:2]
    dest = order_ref[turn]
    last = turn == dests - 1
    if last:
        earlier_ref, acc_ref, guess_ref, all_ref = refs[:4]
        all_ref[order_ref[0]] = earlier_ref[0]
    else:
        acc_ref, guess_ref = refs[:2]
    turned_ref, mixed_ref = refs[-6:-4]
    lists = refs[-4:]
    steps = list_pairs(rel_ref, dests + 1, 2 * dests, *lists, only=(dest,))
    add_pairs(steps, lists, kron_ref, other_ref, left_ref, right_t_ref, acc_ref, turned_ref, mixed_ref)
    shift = common_shift(mine_ref, theirs_ref)
    keep_state = jnp.tile(1.0 + STEP_SIZE * shift, (1, x_ref.shape[2] // LANES))

    def update(b, r, start, carry):
        x = x_ref[b, r, :].astype(F32)
        guess = (keep_state * x - STEP_SIZE * acc_ref[b, r, :]).astype(BF16)
        guess_ref[0, r, :] = guess
        if last:
            all_ref[b, r, :] = guess
        return carry

    row_loop(1, rows, update, 0, first=dest)


def second_local(
    rel_ref, rank_ref, kron_ref, guess_ref, left_ref, right_t_ref, x_ref, image_ref,
    acc_ref, sums_ref,
    turned_ref, mixed_ref, *lists,
):
    dests, rows, _ = x_ref.shape
    acc_ref[...] = jnp.zeros_like(acc_ref)
    steps = list_pairs(rel_ref, 0, dests, *lists)
    add_pairs(steps, lists, kron_ref, guess_ref, left_ref, right_t_ref, acc_ref, turned_ref, mixed_ref)

    def sums(b, r, start, carry):
        x = x_ref[b, r, :].astype(F32)
        guess = guess_ref[b, r, :].astype(F32)
        image = image_ref[b, r, :]
        keep = kept_rows(rank_ref[b], start)
        xx, xg, gg = fold(x * x), fold(x * guess), fold(guess * guess)
        new = (fold(x * image), xx, fold(guess * image), xg, gg, keep * gg, keep * xx, keep * xg)
        return tuple(total + value for total, value in zip(carry, new))

    put_sums(sums_ref, row_loop(dests, rows, sums, 8))


def second_finish(
    rel_ref, rank_ref, kron_ref, other_ref, left_ref, right_t_ref, before_ref, x_ref, guess_ref,
    mine_ref, theirs_ref, early_ref,
    kept_ref, sums_ref,
    turned_ref, mixed_ref, *lists,
):
    dests, rows, width = x_ref.shape
    steps = list_pairs(rel_ref, dests + 1, 2 * dests, *lists)
    add_pairs(steps, lists, kron_ref, other_ref, left_ref, right_t_ref, kept_ref, turned_ref, mixed_ref)
    shift = common_shift(mine_ref, theirs_ref)
    keep_guess = jnp.tile(1.0 + STEP_SIZE * shift, (1, width // LANES))

    def sums(b, r, start, carry):
        x = x_ref[b, r, :].astype(F32)
        guess = guess_ref[b, r, :].astype(F32)
        kept = keep_guess * guess - STEP_SIZE * kept_ref[b, r, :]
        kept_ref[b, r, :] = kept
        keep = kept_rows(rank_ref[b], start)
        kg, kx = fold(kept * guess), fold(kept * x)
        new = (kg, kx, keep * kg, keep * kx, keep * fold(kept * kept))
        return tuple(total + value for total, value in zip(carry, new))

    totals = row_loop(dests, rows, sums, 5)
    sums_ref[0:8, :] = early_ref[...]
    put_sums(sums_ref, totals, first=8)
    sums_ref[13:16, :] = jnp.zeros((3, LANES), F32)


def normalize(
    cells, rank_ref, kept_ref, guess_ref, x_ref, mine_ref, theirs_ref, my_sums_ref, their_sums_ref,
    both_ref,
):
    both = my_sums_ref[...] + their_sums_ref[...]
    xv, xx, gv, xg, gg, gg_kept, xx_kept, xg_kept, kg, kx, kg_kept, kx_kept, kk_kept = (
        both[n : n + 1] for n in range(13)
    )
    shift = common_shift(mine_ref, theirs_ref)
    delta = STEP_SIZE * (xv / xx - shift)
    scale = (1.0 + STEP_SIZE * shift) / STEP_SIZE
    gw, xw = scale * gg - kg / STEP_SIZE, scale * xg - kx / STEP_SIZE
    num = gw + delta * (xw + gv + delta * xv)
    den = gg + delta * (2.0 * xg + delta * xx)
    beta = STEP_SIZE * (num / den - shift)
    of_guess, of_state = beta + delta, beta * delta
    norm = (
        kk_kept
        + of_guess * (2.0 * kg_kept + of_guess * gg_kept)
        + of_state * (2.0 * kx_kept + of_state * xx_kept + 2.0 * of_guess * xg_kept)
    )
    gain = jnp.sqrt(cells / (jnp.maximum(norm, 0.0) + EPSILON))
    blocks, rows, width = kept_ref.shape
    group = 8 * LANES
    per = width // group
    row = lax.broadcasted_iota(jnp.int32, (rows, LANES), 0)

    def one(n, carry):
        b = n // per
        factor = jnp.where(row < rank_ref[b], gain, 0.0)
        for p in range(8):
            cols = pl.ds(pl.multiple_of(lax.rem(n, per) * group + p * LANES, LANES), LANES)
            kept = (
                kept_ref[b, :, cols]
                + of_guess * guess_ref[b, :, cols].astype(F32)
                + of_state * x_ref[b, :, cols].astype(F32)
            )
            state = (kept * factor).astype(BF16)
            both_ref[0, b, :, cols] = state
            both_ref[1, b, :, cols] = state.T
        return carry

    lax.fori_loop(0, blocks * per, one, 0)


def environments(
    first, counts, scale, use_left, left_ref, right_ref, both_ref, out_ref, mid_ref
):
    _, dests, rows, width = both_ref.shape
    phys = width // LANES
    inner = jnp.where(use_left, 0, 1)

    def step(begin, pairs):
        for j in range(pairs):
            k = first + begin + 2 * j
            for b in range(dests):
                env = jnp.concatenate(
                    [
                        jnp.where(use_left, left_ref[k + i, b], right_ref[k + i, b])
                        for i in range(2)
                    ],
                    axis=0,
                )
                mid = dot(env, both_ref[inner, b]).astype(BF16)
                for p in range(phys):
                    for i in range(2):
                        mid_ref[
                            j * dests + b, p * rows : (p + 1) * rows, i * LANES : (i + 1) * LANES
                        ] = mid[i * rows : (i + 1) * rows, p * LANES : (p + 1) * LANES]
        for j in range(pairs):
            k = begin + 2 * j
            for b in range(dests):
                out = (dot(both_ref[1 - inner, b], mid_ref[j * dests + b]) * scale).astype(BF16)
                out_ref[k, b] = out[:, :LANES]
                out_ref[k + 1, b] = out[:, LANES:]

    begin = 0
    for pairs, passes in counts:

        def one(n, carry, begin=begin, pairs=pairs):
            step(begin + 2 * pairs * n, pairs)
            return carry

        lax.fori_loop(0, passes, one, 0)
        begin += 2 * pairs * passes


def normalize_and_cross(
    counts, scale, cells,
    odd_ref, rank_ref, kept_ref, guess_ref, x_ref, mine_ref, theirs_ref, my_sums_ref,
    their_sums_ref, left_ref, right_ref,
    new_ref, both_ref, out_ref,
    mid_ref, sem,
):
    normalize(
        cells, rank_ref, kept_ref, guess_ref, x_ref, mine_ref, theirs_ref, my_sums_ref,
        their_sums_ref, both_ref,
    )
    copy = pltpu.make_async_copy(both_ref.at[0], new_ref, sem)
    copy.start()
    environments(
        0, counts, scale, odd_ref[0] == 1, left_ref, right_ref, both_ref, out_ref, mid_ref
    )
    copy.wait()


def cross(first, counts, scale, odd_ref, left_ref, right_ref, both_ref, out_ref, mid_ref):
    environments(
        first, counts, scale, odd_ref[0] == 1, left_ref, right_ref, both_ref, out_ref, mid_ref
    )


def within(counts, scale, odd_ref, left_ref, right_ref, both_ref, *refs):
    outs, all_ref, mid_ref = refs[:-2], refs[-2], refs[-1]
    environments(
        0, counts, scale, odd_ref[0] == 0, left_ref, right_ref, both_ref, all_ref, mid_ref
    )
    begin = 0
    for out_ref in outs:
        count = out_ref.shape[0]
        out_ref[...] = all_ref[begin : begin + count]
        begin += count


def widen(begins, crossed, odd_ref, *refs):
    pieces, (outs, wide_ref, sems) = refs[: len(begins)], (refs[-4:-2], refs[-2], refs[-1])
    to_right = odd_ref[0] == (1 if crossed else 0)
    copies = []
    for piece, begin in zip(pieces, begins):
        for n in range(piece.shape[0]):
            place = begin + n
            wide_ref[place] = piece[n].astype(F32)
            pair = [
                pltpu.make_async_copy(wide_ref.at[place], out.at[place], sems.at[place])
                for out in outs
            ]
            pl.when(jnp.logical_not(to_right))(pair[0].start)
            pl.when(to_right)(pair[1].start)
            copies.append(pair)
    for pair in copies:
        pl.when(jnp.logical_not(to_right))(pair[0].wait)
        pl.when(to_right)(pair[1].wait)


def shards(state, left_env, right_env, site_ops, sector_map, ranks):
    dests, rows, width = state.shape[1:]
    chan, phys = site_ops.shape[1:3]
    groups = lax.axis_size("blk")
    total_blocks = groups * dests
    first_block = lax.axis_index("blk") * dests
    x, left, right, ops = state[0], left_env[0], right_env[0], site_ops[0]

    twice = jnp.concatenate([sector_map[0]] * 2, axis=1)
    turned_map = lax.dynamic_slice_in_dim(twice, first_block, total_blocks, 1)
    turned_map = lax.rem(turned_map - first_block + total_blocks, total_blocks)

    swap = [(g, groups - 1 - g) for g in range(groups)]

    def trade(value):
        return lax.ppermute(value, "blk", swap)

    def shape(dims, kind):
        return jax.ShapeDtypeStruct(dims, kind)

    wave = (dests, rows, width)
    wave_f32 = shape(wave, F32)
    wave_b16 = shape(wave, BF16)
    sums_kind = shape((8, LANES), F32)
    lists = [pltpu.SMEM((chan * dests + 2 * dests * dests + 1,), jnp.int32)] * 4
    pair_scratch = [
        pltpu.VMEM((2, rows // GROUP, phys * GROUP, LANES), BF16),
        pltpu.VMEM((2 * rows, width), BF16),
    ] + lists

    def call(body, specs, outs, scratch, *args, aliases={}, out_specs=None):
        return pl.pallas_call(
            body,
            in_specs=specs,
            out_specs=out_specs or jax.tree.map(lambda _: VMEM, outs),
            out_shape=outs,
            scratch_shapes=scratch,
            compiler_params=PARAMS,
            cost_estimate=COST,
            input_output_aliases=aliases,
        )(*args)

    block = shape((1, rows, width), BF16)
    own = [call(functools.partial(cut, b), [VMEM], block, [], x) for b in range(dests)]
    other = [trade(value) for value in own]
    kron = call(
        make_kron, [VMEM], shape((chan, phys * GROUP, phys * GROUP), BF16),
        [pltpu.VMEM((chan * phys, phys * GROUP), F32)], ops,
    )
    rel_kind = shape((chan, dests), jnp.int32)
    right_t, image, mine, rel, arrived, order = call(
        first_local, [SMEM] + [VMEM] * 4,
        (
            shape(right.shape, BF16), wave_f32, sums_kind, rel_kind, rel_kind,
            shape((dests,), jnp.int32),
        ),
        pair_scratch, turned_map, kron, x, left, right, out_specs=(VMEM,) * 3 + (SMEM,) * 3,
    )
    image, mine = call(
        first_remote, [SMEM] + [VMEM] * 6, (wave_f32, sums_kind), pair_scratch,
        rel, kron, other[0], left, right_t, image, mine, aliases={5: 0},
    )
    theirs = trade(mine)
    image, first_guess = call(
        functools.partial(first_finish, 0), [SMEM] * 2 + [VMEM] * 8,
        (wave_f32, block), pair_scratch,
        rel, order, kron, other[1], left, right_t, image, x, mine, theirs, aliases={6: 0},
    )
    image, last_guess, guess = call(
        functools.partial(first_finish, 1), [SMEM] * 2 + [VMEM] * 9,
        (wave_f32, block, wave_b16), pair_scratch,
        rel, order, kron, other[1], left, right_t, image, x, mine, theirs, first_guess,
        aliases={6: 0},
    )
    other = [trade(first_guess), trade(last_guess)]
    acc, early_sums = call(
        second_local, [SMEM] * 2 + [VMEM] * 6, (wave_f32, sums_kind), pair_scratch,
        arrived, ranks[0], kron, guess, left, right_t, x, image,
    )
    acc = call(
        remote_sources, [SMEM] + [VMEM] * 5, wave_f32, pair_scratch,
        arrived, kron, other[0], left, right_t, acc, aliases={5: 0},
    )
    kept, my_sums = call(
        second_finish, [SMEM] * 2 + [VMEM] * 10, (wave_f32, shape((16, LANES), F32)), pair_scratch,
        arrived, ranks[0], kron, other[1], left, right_t, acc, x, guess, mine, theirs, early_sums,
        aliases={6: 0},
    )
    their_sums = trade(my_sums)

    env_scale = 1.0 / math.sqrt(phys * rows)
    cells = float(total_blocks * rows * width)
    early = 8
    count = lax.axis_size("seg")
    odd = jnp.full((1,), lax.rem(lax.axis_index("seg"), 2), jnp.int32)

    def swapped(value, low):
        pairs = [(s, s + 1) for s in range(low, count - 1, 2)]
        return lax.ppermute(value, "seg", pairs + [(t, s) for s, t in pairs])

    def env_kind(number):
        return shape((number,) + left.shape[1:], BF16)

    def mid(pairs):
        return [pltpu.VMEM((pairs * dests, width, 2 * LANES), BF16)]

    new_state, both, piece = call(
        functools.partial(normalize_and_cross, ((2, 2),), env_scale, cells),
        [SMEM] * 2 + [VMEM] * 9, (wave_b16, shape((2,) + wave, BF16), env_kind(early)),
        mid(2) + [pltpu.SemaphoreType.DMA],
        odd, ranks[0], kept, guess, x, mine, theirs, my_sums, their_sums, left, right,
        out_specs=(HBM, VMEM, VMEM),
    )
    rest = call(
        functools.partial(cross, early, ((3, 1),), env_scale),
        [SMEM] + [VMEM] * 3, env_kind(chan - early), mid(3), odd, left, right, both,
    )
    sizes = (5, 5, 4)
    inside = call(
        functools.partial(within, ((2, 3), (1, 1)), env_scale),
        [SMEM] + [VMEM] * 3, tuple(env_kind(size) for size in sizes),
        [pltpu.VMEM(left.shape, BF16)] + mid(2), odd, left, right, both,
    )
    piece, rest = swapped(piece, 1), swapped(rest, 1)
    inside = [swapped(value, 0) for value in inside]
    env_f32 = shape(left.shape, F32)

    def widened(begins, crossed, values, filled):
        number = 1 + len(values)
        return call(
            functools.partial(widen, begins, crossed),
            [SMEM] + [VMEM] * len(values) + [HBM] * len(filled), (env_f32, env_f32),
            [pltpu.VMEM(left.shape, F32), pltpu.SemaphoreType.DMA((chan,))],
            odd, *values, *filled,
            aliases={number + n: n for n in range(len(filled))}, out_specs=(HBM, HBM),
        )

    filled = widened((0,), True, [piece], ())
    filled = widened((0, sizes[0], sizes[0] + sizes[1]), False, inside, filled)
    received_left, received_right = widened((early,), True, [rest], filled)
    return (new_state[None], received_left[None], received_right[None])


def solution(mesh):
    placed = (
        P("seg", "blk", None, None),
        P("seg", None, "blk", None, None),
        P("seg", None, "blk", None, None),
        P("seg", None, None, None),
        P("seg", None, None),
        P("seg", "blk"),
    )
    return jax.shard_map(
        shards,
        mesh=mesh,
        in_specs=placed,
        out_specs=(
            P("seg", "blk", None, None),
            P("seg", None, "blk", None, None),
            P("seg", None, "blk", None, None),
        ),
        check_vma=False,
    )
```

```python
import functools
import math

import jax
import jax.numpy as jnp
from jax import lax
from jax.experimental import pallas as pl
from jax.experimental.pallas import tpu as pltpu
from jax.sharding import PartitionSpec as P

STEP_SIZE = 0.25
EPSILON = 1e-06
LANES = 128
GROUP = 8
CHUNK = 32
F32 = jnp.float32
BF16 = jnp.bfloat16
VMEM = pl.BlockSpec(memory_space=pltpu.VMEM)
HBM = pl.BlockSpec(memory_space=pltpu.HBM)
SMEM = pl.BlockSpec(memory_space=pltpu.SMEM)
COST = pl.CostEstimate(flops=1024, bytes_accessed=1024, transcendentals=0)
PARAMS = pltpu.CompilerParams(vmem_limit_bytes=20 * 1024 * 1024)


def dot(left, right):
    return lax.dot_general(
        left, right, (((1,), (0,)), ((), ())), preferred_element_type=F32
    )


def make_kron(ops_ref, kron_ref, spread_ref):
    chan, phys, _ = ops_ref.shape
    wide = phys * GROUP
    columns = lax.broadcasted_iota(jnp.int32, (phys, wide), 1)
    spread = (columns // GROUP == lax.broadcasted_iota(jnp.int32, (phys, wide), 0)).astype(F32)
    spread_ref[...] = dot(ops_ref[...].reshape(chan * phys, phys), spread.astype(BF16))
    same = lax.broadcasted_iota(jnp.int32, (GROUP, wide), 1) % GROUP == lax.broadcasted_iota(
        jnp.int32, (GROUP, wide), 0
    )

    def one(k, carry):
        rows = spread_ref[pl.ds(pl.multiple_of(k * phys, phys), phys), :]
        full = [
            jnp.where(same, jnp.broadcast_to(rows[p : p + 1], (GROUP, wide)), 0.0)
            for p in range(phys)
        ]
        kron_ref[k] = jnp.concatenate(full, axis=0).astype(BF16)
        return carry

    lax.fori_loop(0, chan, one, 0)


def list_pairs(rel_ref, low, high, chan_list, src_list, live_list, dest_list, only=None):
    chan, dests = rel_ref.shape
    place = jnp.int32(0)
    for b in range(dests) if only is None else only:
        for source in range(low, high):
            for k in range(chan):
                chan_list[place] = k
                src_list[place] = source - low
                live_list[place] = 1
                dest_list[place] = b
                place = place + jnp.where(rel_ref[k, b] == source, 1, 0)
            chan_list[place] = 0
            src_list[place] = source - low
            live_list[place] = 0
            dest_list[place] = b
            place = place + lax.rem(place, 2)
    return place // 2


def add_pairs(steps, lists, kron_ref, x_ref, left_ref, right_t_ref, acc_ref, turned_ref, mixed_ref):
    chan_list, src_list, live_list, dest_list = lists
    rows = x_ref.shape[1]
    phys = x_ref.shape[2] // LANES
    groups = rows // GROUP

    def lanes(n):
        return slice(n * LANES, (n + 1) * LANES)

    def act_right(s):
        source, dest = src_list[2 * s], dest_list[2 * s]
        tall = jnp.concatenate([x_ref[source, :, lanes(q)] for q in range(phys)], axis=0)
        second = right_t_ref[chan_list[2 * s + 1], dest]
        second = jnp.where(live_list[2 * s + 1] > 0, second, jnp.zeros_like(second))
        out = dot(tall, jnp.concatenate([right_t_ref[chan_list[2 * s], dest], second], axis=1))
        for i in range(2):
            for g in range(groups):
                turned_ref[i, g] = jnp.concatenate(
                    [
                        out[q * rows + g * GROUP : q * rows + (g + 1) * GROUP, lanes(i)]
                        for q in range(phys)
                    ],
                    axis=0,
                ).astype(BF16)

    def act_site(s):
        for i in range(2):
            kron = kron_ref[chan_list[2 * s + i]]
            for h in range(groups // 2):
                both = jnp.concatenate([turned_ref[i, 2 * h], turned_ref[i, 2 * h + 1]], axis=1)
                out = dot(kron, both)
                r0 = i * rows + 2 * h * GROUP
                for p in range(phys):
                    row = slice(p * GROUP, (p + 1) * GROUP)
                    mixed_ref[r0 : r0 + 2 * GROUP, lanes(p)] = jnp.concatenate(
                        [out[row, lanes(0)], out[row, lanes(1)]], axis=0
                    ).astype(BF16)

    def act_left(s):
        dest = dest_list[2 * s]
        left = jnp.concatenate(
            [left_ref[chan_list[2 * s], dest], left_ref[chan_list[2 * s + 1], dest]], axis=1
        )
        acc_ref[dest] += dot(left, mixed_ref[...])

    def middle(s, carry):
        act_site(s)
        act_right(s + 1)
        act_left(s)
        return carry

    @pl.when(steps > 0)
    def _():
        act_right(0)
        lax.fori_loop(0, steps - 1, middle, 0)
        act_site(steps - 1)
        act_left(steps - 1)


def fold(values):
    total = values[:, :LANES]
    for p in range(1, values.shape[1] // LANES):
        total = total + values[:, p * LANES : (p + 1) * LANES]
    return total


def row_loop(blocks, rows, body, count, first=0):
    zeros = tuple(jnp.zeros((CHUNK, LANES), F32) for _ in range(count))
    per = rows // CHUNK

    def step(n, carry):
        start = pl.multiple_of(lax.rem(n, per) * CHUNK, CHUNK)
        return body(first + n // per, pl.ds(start, CHUNK), start, carry)

    return lax.fori_loop(0, blocks * per, step, zeros)


def kept_rows(rank, start):
    row = start + lax.broadcasted_iota(jnp.int32, (CHUNK, LANES), 0)
    return (row < rank).astype(F32)


def put_sums(out_ref, values, first=0):
    for n, value in enumerate(values):
        out_ref[first + n : first + n + 1, :] = jnp.full((1, LANES), 1.0, F32) * jnp.sum(value)


def common_shift(mine_ref, theirs_ref):
    num = mine_ref[0:1, :] + theirs_ref[0:1, :]
    den = mine_ref[1:2, :] + theirs_ref[1:2, :]
    return jnp.where(den > 0, num / jnp.where(den > 0, den, 1.0), 0.0)


def choose_order(map_ref, rel_ref, arrived_ref, order_ref):
    chan, dests = rel_ref.shape
    for k in range(chan):
        for b in range(dests):
            rel_ref[k, b] = map_ref[k, b]

    def uses(first, source):
        total = jnp.int32(0)
        for k in range(chan):
            for b in range(first, first + dests):
                total = total + jnp.where(map_ref[k, b] == source, 1, 0)
        return total

    swap_mine = uses(dests, 0) < uses(dests, 1)
    swap_theirs = uses(0, dests) < uses(0, dests + 1)
    order_ref[0] = jnp.where(swap_mine, 1, 0)
    order_ref[1] = jnp.where(swap_mine, 0, 1)
    for k in range(chan):
        for b in range(dests):
            source = rel_ref[k, b]
            other = 2 * dests + 1 - source
            arrived_ref[k, b] = jnp.where(swap_theirs & (source >= dests), other, source)


def cut(b, x_ref, out_ref):
    out_ref[0] = x_ref[b]


def first_local(
    map_ref, kron_ref, x_ref, left_ref, right_ref,
    right_t_ref, image_ref, sums_ref, rel_ref, arrived_ref, order_ref,
    turned_ref, mixed_ref, *lists,
):
    choose_order(map_ref, rel_ref, arrived_ref, order_ref)
    chan, dests = left_ref.shape[:2]

    def turn(n, carry):
        for k in range(2):
            for b in range(dests):
                right_t_ref[2 * n + k, b] = right_ref[2 * n + k, b].T
        return carry

    lax.fori_loop(0, chan // 2, turn, 0)
    image_ref[...] = jnp.zeros_like(image_ref)
    steps = list_pairs(rel_ref, 0, dests, *lists)
    add_pairs(steps, lists, kron_ref, x_ref, left_ref, right_t_ref, image_ref, turned_ref, mixed_ref)

    def sums(b, r, start, carry):
        x = x_ref[b, r, :].astype(F32)
        return carry[0] + fold(x * image_ref[b, r, :]), carry[1] + fold(x * x)

    totals = row_loop(dests, x_ref.shape[1], sums, 2)
    sums_ref[...] = jnp.zeros_like(sums_ref)
    put_sums(sums_ref, totals)


def remote_sources(
    rel_ref, kron_ref, other_ref, left_ref, right_t_ref, before_ref,
    acc_ref,
    turned_ref, mixed_ref, *lists,
):
    dests = left_ref.shape[1]
    steps = list_pairs(rel_ref, dests, dests + 1, *lists)
    add_pairs(steps, lists, kron_ref, other_ref, left_ref, right_t_ref, acc_ref, turned_ref, mixed_ref)


def first_remote(
    rel_ref, kron_ref, other_ref, left_ref, right_t_ref, before_ref, local_sums_ref,
    acc_ref, sums_ref,
    turned_ref, mixed_ref, *lists,
):
    dests = left_ref.shape[1]
    sums_ref[...] = local_sums_ref[...]
    steps = list_pairs(rel_ref, dests, dests + 1, *lists)
    add_pairs(steps, lists, kron_ref, other_ref, left_ref, right_t_ref, acc_ref, turned_ref, mixed_ref)


def first_finish(
    turn, rel_ref, order_ref, kron_ref, other_ref, left_ref, right_t_ref, before_ref, x_ref,
    mine_ref, theirs_ref, *refs,
):
    dests, rows = x_ref.shape[:2]
    dest = order_ref[turn]
    last = turn == dests - 1
    if last:
        earlier_ref, acc_ref, guess_ref, all_ref = refs[:4]
        all_ref[order_ref[0]] = earlier_ref[0]
    else:
        acc_ref, guess_ref = refs[:2]
    turned_ref, mixed_ref = refs[-6:-4]
    lists = refs[-4:]
    steps = list_pairs(rel_ref, dests + 1, 2 * dests, *lists, only=(dest,))
    add_pairs(steps, lists, kron_ref, other_ref, left_ref, right_t_ref, acc_ref, turned_ref, mixed_ref)
    shift = common_shift(mine_ref, theirs_ref)
    keep_state = jnp.tile(1.0 + STEP_SIZE * shift, (1, x_ref.shape[2] // LANES))

    def update(b, r, start, carry):
        x = x_ref[b, r, :].astype(F32)
        guess = (keep_state * x - STEP_SIZE * acc_ref[b, r, :]).astype(BF16)
        guess_ref[0, r, :] = guess
        if last:
            all_ref[b, r, :] = guess
        return carry

    row_loop(1, rows, update, 0, first=dest)


def second_local(
    rel_ref, rank_ref, kron_ref, guess_ref, left_ref, right_t_ref, x_ref, image_ref,
    acc_ref, sums_ref,
    turned_ref, mixed_ref, *lists,
):
    dests, rows, _ = x_ref.shape
    acc_ref[...] = jnp.zeros_like(acc_ref)
    steps = list_pairs(rel_ref, 0, dests, *lists)
    add_pairs(steps, lists, kron_ref, guess_ref, left_ref, right_t_ref, acc_ref, turned_ref, mixed_ref)

    def sums(b, r, start, carry):
        x = x_ref[b, r, :].astype(F32)
        guess = guess_ref[b, r, :].astype(F32)
        image = image_ref[b, r, :]
        keep = kept_rows(rank_ref[b], start)
        xx, xg, gg = fold(x * x), fold(x * guess), fold(guess * guess)
        new = (fold(x * image), xx, fold(guess * image), xg, gg, keep * gg, keep * xx, keep * xg)
        return tuple(total + value for total, value in zip(carry, new))

    put_sums(sums_ref, row_loop(dests, rows, sums, 8))


def second_finish(
    rel_ref, rank_ref, kron_ref, other_ref, left_ref, right_t_ref, before_ref, x_ref, guess_ref,
    mine_ref, theirs_ref, early_ref,
    kept_ref, sums_ref,
    turned_ref, mixed_ref, *lists,
):
    dests, rows, width = x_ref.shape
    steps = list_pairs(rel_ref, dests + 1, 2 * dests, *lists)
    add_pairs(steps, lists, kron_ref, other_ref, left_ref, right_t_ref, kept_ref, turned_ref, mixed_ref)
    shift = common_shift(mine_ref, theirs_ref)
    keep_guess = jnp.tile(1.0 + STEP_SIZE * shift, (1, width // LANES))

    def sums(b, r, start, carry):
        x = x_ref[b, r, :].astype(F32)
        guess = guess_ref[b, r, :].astype(F32)
        kept = keep_guess * guess - STEP_SIZE * kept_ref[b, r, :]
        kept_ref[b, r, :] = kept
        keep = kept_rows(rank_ref[b], start)
        kg, kx = fold(kept * guess), fold(kept * x)
        new = (kg, kx, keep * kg, keep * kx, keep * fold(kept * kept))
        return tuple(total + value for total, value in zip(carry, new))

    totals = row_loop(dests, rows, sums, 5)
    sums_ref[0:8, :] = early_ref[...]
    put_sums(sums_ref, totals, first=8)
    sums_ref[13:16, :] = jnp.zeros((3, LANES), F32)


def normalize(
    cells, rank_ref, kept_ref, guess_ref, x_ref, mine_ref, theirs_ref, my_sums_ref, their_sums_ref,
    both_ref,
):
    both = my_sums_ref[...] + their_sums_ref[...]
    xv, xx, gv, xg, gg, gg_kept, xx_kept, xg_kept, kg, kx, kg_kept, kx_kept, kk_kept = (
        both[n : n + 1] for n in range(13)
    )
    shift = common_shift(mine_ref, theirs_ref)
    delta = STEP_SIZE * (xv / xx - shift)
    scale = (1.0 + STEP_SIZE * shift) / STEP_SIZE
    gw, xw = scale * gg - kg / STEP_SIZE, scale * xg - kx / STEP_SIZE
    num = gw + delta * (xw + gv + delta * xv)
    den = gg + delta * (2.0 * xg + delta * xx)
    beta = STEP_SIZE * (num / den - shift)
    of_guess, of_state = beta + delta, beta * delta
    norm = (
        kk_kept
        + of_guess * (2.0 * kg_kept + of_guess * gg_kept)
        + of_state * (2.0 * kx_kept + of_state * xx_kept + 2.0 * of_guess * xg_kept)
    )
    gain = jnp.sqrt(cells / (jnp.maximum(norm, 0.0) + EPSILON))
    blocks, rows, width = kept_ref.shape
    group = 8 * LANES
    per = width // group
    row = lax.broadcasted_iota(jnp.int32, (rows, LANES), 0)

    def one(n, carry):
        b = n // per
        factor = jnp.where(row < rank_ref[b], gain, 0.0)
        for p in range(8):
            cols = pl.ds(pl.multiple_of(lax.rem(n, per) * group + p * LANES, LANES), LANES)
            kept = (
                kept_ref[b, :, cols]
                + of_guess * guess_ref[b, :, cols].astype(F32)
                + of_state * x_ref[b, :, cols].astype(F32)
            )
            state = (kept * factor).astype(BF16)
            both_ref[0, b, :, cols] = state
            both_ref[1, b, :, cols] = state.T
        return carry

    lax.fori_loop(0, blocks * per, one, 0)


def environments(
    first, counts, scale, use_left, left_ref, right_ref, both_ref, out_ref, mid_ref
):
    _, dests, rows, width = both_ref.shape
    phys = width // LANES
    inner = jnp.where(use_left, 0, 1)

    def step(begin, pairs):
        for j in range(pairs):
            k = first + begin + 2 * j
            for b in range(dests):
                env = jnp.concatenate(
                    [
                        jnp.where(use_left, left_ref[k + i, b], right_ref[k + i, b])
                        for i in range(2)
                    ],
                    axis=0,
                )
                mid = dot(env, both_ref[inner, b]).astype(BF16)
                for p in range(phys):
                    for i in range(2):
                        mid_ref[
                            j * dests + b, p * rows : (p + 1) * rows, i * LANES : (i + 1) * LANES
                        ] = mid[i * rows : (i + 1) * rows, p * LANES : (p + 1) * LANES]
        for j in range(pairs):
            k = begin + 2 * j
            for b in range(dests):
                out = (dot(both_ref[1 - inner, b], mid_ref[j * dests + b]) * scale).astype(BF16)
                out_ref[k, b] = out[:, :LANES]
                out_ref[k + 1, b] = out[:, LANES:]

    begin = 0
    for pairs, passes in counts:

        def one(n, carry, begin=begin, pairs=pairs):
            step(begin + 2 * pairs * n, pairs)
            return carry

        lax.fori_loop(0, passes, one, 0)
        begin += 2 * pairs * passes


def normalize_and_cross(
    counts, scale, cells,
    odd_ref, rank_ref, kept_ref, guess_ref, x_ref, mine_ref, theirs_ref, my_sums_ref,
    their_sums_ref, left_ref, right_ref,
    new_ref, both_ref, out_ref,
    mid_ref, sem,
):
    normalize(
        cells, rank_ref, kept_ref, guess_ref, x_ref, mine_ref, theirs_ref, my_sums_ref,
        their_sums_ref, both_ref,
    )
    copy = pltpu.make_async_copy(both_ref.at[0], new_ref, sem)
    copy.start()
    environments(
        0, counts, scale, odd_ref[0] == 1, left_ref, right_ref, both_ref, out_ref, mid_ref
    )
    copy.wait()


def cross(first, counts, scale, odd_ref, left_ref, right_ref, both_ref, out_ref, mid_ref):
    environments(
        first, counts, scale, odd_ref[0] == 1, left_ref, right_ref, both_ref, out_ref, mid_ref
    )


def within(counts, scale, odd_ref, left_ref, right_ref, both_ref, *refs):
    outs, all_ref, mid_ref = refs[:-2], refs[-2], refs[-1]
    environments(
        0, counts, scale, odd_ref[0] == 0, left_ref, right_ref, both_ref, all_ref, mid_ref
    )
    begin = 0
    for out_ref in outs:
        count = out_ref.shape[0]
        out_ref[...] = all_ref[begin : begin + count]
        begin += count


def widen(begins, crossed, odd_ref, *refs):
    pieces, (outs, wide_ref, sems) = refs[: len(begins)], (refs[-4:-2], refs[-2], refs[-1])
    to_right = odd_ref[0] == (1 if crossed else 0)
    copies = []
    for piece, begin in zip(pieces, begins):
        for n in range(piece.shape[0]):
            place = begin + n
            wide_ref[place] = piece[n].astype(F32)
            pair = [
                pltpu.make_async_copy(wide_ref.at[place], out.at[place], sems.at[place])
                for out in outs
            ]
            pl.when(jnp.logical_not(to_right))(pair[0].start)
            pl.when(to_right)(pair[1].start)
            copies.append(pair)
    for pair in copies:
        pl.when(jnp.logical_not(to_right))(pair[0].wait)
        pl.when(to_right)(pair[1].wait)


def shards(state, left_env, right_env, site_ops, sector_map, ranks):
    dests, rows, width = state.shape[1:]
    chan, phys = site_ops.shape[1:3]
    groups = lax.axis_size("blk")
    total_blocks = groups * dests
    first_block = lax.axis_index("blk") * dests
    x, left, right, ops = state[0], left_env[0], right_env[0], site_ops[0]

    twice = jnp.concatenate([sector_map[0]] * 2, axis=1)
    turned_map = lax.dynamic_slice_in_dim(twice, first_block, total_blocks, 1)
    turned_map = lax.rem(turned_map - first_block + total_blocks, total_blocks)

    swap = [(g, groups - 1 - g) for g in range(groups)]

    def trade(value):
        return lax.ppermute(value, "blk", swap)

    def shape(dims, kind):
        return jax.ShapeDtypeStruct(dims, kind)

    wave = (dests, rows, width)
    wave_f32 = shape(wave, F32)
    wave_b16 = shape(wave, BF16)
    sums_kind = shape((8, LANES), F32)
    lists = [pltpu.SMEM((chan * dests + 2 * dests * dests + 1,), jnp.int32)] * 4
    pair_scratch = [
        pltpu.VMEM((2, rows // GROUP, phys * GROUP, LANES), BF16),
        pltpu.VMEM((2 * rows, width), BF16),
    ] + lists

    def call(body, specs, outs, scratch, *args, aliases={}, out_specs=None):
        return pl.pallas_call(
            body,
            in_specs=specs,
            out_specs=out_specs or jax.tree.map(lambda _: VMEM, outs),
            out_shape=outs,
            scratch_shapes=scratch,
            compiler_params=PARAMS,
            cost_estimate=COST,
            input_output_aliases=aliases,
        )(*args)

    block = shape((1, rows, width), BF16)
    own = [call(functools.partial(cut, b), [VMEM], block, [], x) for b in range(dests)]
    other = [trade(value) for value in own]
    kron = call(
        make_kron, [VMEM], shape((chan, phys * GROUP, phys * GROUP), BF16),
        [pltpu.VMEM((chan * phys, phys * GROUP), F32)], ops,
    )
    rel_kind = shape((chan, dests), jnp.int32)
    right_t, image, mine, rel, arrived, order = call(
        first_local, [SMEM] + [VMEM] * 4,
        (
            shape(right.shape, BF16), wave_f32, sums_kind, rel_kind, rel_kind,
            shape((dests,), jnp.int32),
        ),
        pair_scratch, turned_map, kron, x, left, right, out_specs=(VMEM,) * 3 + (SMEM,) * 3,
    )
    image, mine = call(
        first_remote, [SMEM] + [VMEM] * 6, (wave_f32, sums_kind), pair_scratch,
        rel, kron, other[0], left, right_t, image, mine, aliases={5: 0},
    )
    theirs = trade(mine)
    image, first_guess = call(
        functools.partial(first_finish, 0), [SMEM] * 2 + [VMEM] * 8,
        (wave_f32, block), pair_scratch,
        rel, order, kron, other[1], left, right_t, image, x, mine, theirs, aliases={6: 0},
    )
    image, last_guess, guess = call(
        functools.partial(first_finish, 1), [SMEM] * 2 + [VMEM] * 9,
        (wave_f32, block, wave_b16), pair_scratch,
        rel, order, kron, other[1], left, right_t, image, x, mine, theirs, first_guess,
        aliases={6: 0},
    )
    other = [trade(first_guess), trade(last_guess)]
    acc, early_sums = call(
        second_local, [SMEM] * 2 + [VMEM] * 6, (wave_f32, sums_kind), pair_scratch,
        arrived, ranks[0], kron, guess, left, right_t, x, image,
    )
    acc = call(
        remote_sources, [SMEM] + [VMEM] * 5, wave_f32, pair_scratch,
        arrived, kron, other[0], left, right_t, acc, aliases={5: 0},
    )
    kept, my_sums = call(
        second_finish, [SMEM] * 2 + [VMEM] * 10, (wave_f32, shape((16, LANES), F32)), pair_scratch,
        arrived, ranks[0], kron, other[1], left, right_t, acc, x, guess, mine, theirs, early_sums,
        aliases={6: 0},
    )
    their_sums = trade(my_sums)

    env_scale = 1.0 / math.sqrt(phys * rows)
    cells = float(total_blocks * rows * width)
    early = 8
    count = lax.axis_size("seg")
    odd = jnp.full((1,), lax.rem(lax.axis_index("seg"), 2), jnp.int32)

    def swapped(value, low):
        pairs = [(s, s + 1) for s in range(low, count - 1, 2)]
        return lax.ppermute(value, "seg", pairs + [(t, s) for s, t in pairs])

    def env_kind(number):
        return shape((number,) + left.shape[1:], BF16)

    def mid(pairs):
        return [pltpu.VMEM((pairs * dests, width, 2 * LANES), BF16)]

    new_state, both, piece = call(
        functools.partial(normalize_and_cross, ((2, 2),), env_scale, cells),
        [SMEM] * 2 + [VMEM] * 9, (wave_b16, shape((2,) + wave, BF16), env_kind(early)),
        mid(2) + [pltpu.SemaphoreType.DMA],
        odd, ranks[0], kept, guess, x, mine, theirs, my_sums, their_sums, left, right,
        out_specs=(HBM, VMEM, VMEM),
    )
    rest = call(
        functools.partial(cross, early, ((3, 1),), env_scale),
        [SMEM] + [VMEM] * 3, env_kind(chan - early), mid(3), odd, left, right, both,
    )
    sizes = (5, 5, 4)
    inside = call(
        functools.partial(within, ((2, 3), (1, 1)), env_scale),
        [SMEM] + [VMEM] * 3, tuple(env_kind(size) for size in sizes),
        [pltpu.VMEM(left.shape, BF16)] + mid(2), odd, left, right, both,
    )
    piece, rest = swapped(piece, 1), swapped(rest, 1)
    inside = [swapped(value, 0) for value in inside]
    env_f32 = shape(left.shape, F32)

    def widened(begins, crossed, values, filled):
        number = 1 + len(values)
        return call(
            functools.partial(widen, begins, crossed),
            [SMEM] + [VMEM] * len(values) + [HBM] * len(filled), (env_f32, env_f32),
            [pltpu.VMEM(left.shape, F32), pltpu.SemaphoreType.DMA((chan,))],
            odd, *values, *filled,
            aliases={number + n: n for n in range(len(filled))}, out_specs=(HBM, HBM),
        )

    filled = widened((0,), True, [piece], ())
    filled = widened((0, sizes[0], sizes[0] + sizes[1]), False, inside, filled)
    received_left, received_right = widened((early,), True, [rest], filled)
    return (new_state[None], received_left[None], received_right[None])


def solution(mesh):
    placed = (
        P("seg", "blk", None, None),
        P("seg", None, "blk", None, None),
        P("seg", None, "blk", None, None),
        P("seg", None, None, None),
        P("seg", None, None),
        P("seg", "blk"),
    )
    return jax.shard_map(
        shards,
        mesh=mesh,
        in_specs=placed,
        out_specs=(
            P("seg", "blk", None, None),
            P("seg", None, "blk", None, None),
            P("seg", None, "blk", None, None),
        ),
        check_vma=False,
    )
```

```python
import functools
import math

import jax
import jax.numpy as jnp
from jax import lax
from jax.experimental import pallas as pl
from jax.experimental.pallas import tpu as pltpu
from jax.sharding import PartitionSpec as P

STEP_SIZE = 0.25
EPSILON = 1e-06
LANES = 128
GROUP = 8
CHUNK = 32
F32 = jnp.float32
BF16 = jnp.bfloat16
VMEM = pl.BlockSpec(memory_space=pltpu.VMEM)
HBM = pl.BlockSpec(memory_space=pltpu.HBM)
SMEM = pl.BlockSpec(memory_space=pltpu.SMEM)
COST = pl.CostEstimate(flops=1024, bytes_accessed=1024, transcendentals=0)
PARAMS = pltpu.CompilerParams(vmem_limit_bytes=20 * 1024 * 1024)


def dot(left, right):
    return lax.dot_general(
        left, right, (((1,), (0,)), ((), ())), preferred_element_type=F32
    )


def make_kron(ops_ref, kron_ref, spread_ref):
    chan, phys, _ = ops_ref.shape
    wide = phys * GROUP
    columns = lax.broadcasted_iota(jnp.int32, (phys, wide), 1)
    spread = (columns // GROUP == lax.broadcasted_iota(jnp.int32, (phys, wide), 0)).astype(F32)
    spread_ref[...] = dot(ops_ref[...].reshape(chan * phys, phys), spread.astype(BF16))
    same = lax.broadcasted_iota(jnp.int32, (GROUP, wide), 1) % GROUP == lax.broadcasted_iota(
        jnp.int32, (GROUP, wide), 0
    )

    def one(k, carry):
        rows = spread_ref[pl.ds(pl.multiple_of(k * phys, phys), phys), :]
        full = [
            jnp.where(same, jnp.broadcast_to(rows[p : p + 1], (GROUP, wide)), 0.0)
            for p in range(phys)
        ]
        kron_ref[k] = jnp.concatenate(full, axis=0).astype(BF16)
        return carry

    lax.fori_loop(0, chan, one, 0)


def list_pairs(rel_ref, low, high, chan_list, src_list, live_list, dest_list, only=None):
    chan, dests = rel_ref.shape
    place = jnp.int32(0)
    for b in range(dests) if only is None else only:
        for source in range(low, high):
            for k in range(chan):
                chan_list[place] = k
                src_list[place] = source - low
                live_list[place] = 1
                dest_list[place] = b
                place = place + jnp.where(rel_ref[k, b] == source, 1, 0)
            chan_list[place] = 0
            src_list[place] = source - low
            live_list[place] = 0
            dest_list[place] = b
            place = place + lax.rem(place, 2)
    return place // 2


def add_pairs(steps, lists, kron_ref, x_ref, left_ref, right_t_ref, acc_ref, turned_ref, mixed_ref):
    chan_list, src_list, live_list, dest_list = lists
    rows = x_ref.shape[1]
    phys = x_ref.shape[2] // LANES
    groups = rows // GROUP

    def lanes(n):
        return slice(n * LANES, (n + 1) * LANES)

    def act_right(s):
        source, dest = src_list[2 * s], dest_list[2 * s]
        tall = jnp.concatenate([x_ref[source, :, lanes(q)] for q in range(phys)], axis=0)
        second = right_t_ref[chan_list[2 * s + 1], dest]
        second = jnp.where(live_list[2 * s + 1] > 0, second, jnp.zeros_like(second))
        out = dot(tall, jnp.concatenate([right_t_ref[chan_list[2 * s], dest], second], axis=1))
        for i in range(2):
            for g in range(groups):
                turned_ref[i, g] = jnp.concatenate(
                    [
                        out[q * rows + g * GROUP : q * rows + (g + 1) * GROUP, lanes(i)]
                        for q in range(phys)
                    ],
                    axis=0,
                ).astype(BF16)

    def act_site(s):
        for i in range(2):
            kron = kron_ref[chan_list[2 * s + i]]
            for h in range(groups // 2):
                both = jnp.concatenate([turned_ref[i, 2 * h], turned_ref[i, 2 * h + 1]], axis=1)
                out = dot(kron, both)
                r0 = i * rows + 2 * h * GROUP
                for p in range(phys):
                    row = slice(p * GROUP, (p + 1) * GROUP)
                    mixed_ref[r0 : r0 + 2 * GROUP, lanes(p)] = jnp.concatenate(
                        [out[row, lanes(0)], out[row, lanes(1)]], axis=0
                    ).astype(BF16)

    def act_left(s):
        dest = dest_list[2 * s]
        left = jnp.concatenate(
            [left_ref[chan_list[2 * s], dest], left_ref[chan_list[2 * s + 1], dest]], axis=1
        )
        acc_ref[dest] += dot(left, mixed_ref[...])

    def middle(s, carry):
        act_site(s)
        act_right(s + 1)
        act_left(s)
        return carry

    @pl.when(steps > 0)
    def _():
        act_right(0)
        lax.fori_loop(0, steps - 1, middle, 0)
        act_site(steps - 1)
        act_left(steps - 1)


def fold(values):
    total = values[:, :LANES]
    for p in range(1, values.shape[1] // LANES):
        total = total + values[:, p * LANES : (p + 1) * LANES]
    return total


def row_loop(blocks, rows, body, count, first=0):
    zeros = tuple(jnp.zeros((CHUNK, LANES), F32) for _ in range(count))
    per = rows // CHUNK

    def step(n, carry):
        start = pl.multiple_of(lax.rem(n, per) * CHUNK, CHUNK)
        return body(first + n // per, pl.ds(start, CHUNK), start, carry)

    return lax.fori_loop(0, blocks * per, step, zeros)


def kept_rows(rank, start):
    row = start + lax.broadcasted_iota(jnp.int32, (CHUNK, LANES), 0)
    return (row < rank).astype(F32)


def put_sums(out_ref, values, first=0):
    for n, value in enumerate(values):
        out_ref[first + n : first + n + 1, :] = jnp.full((1, LANES), 1.0, F32) * jnp.sum(value)


def common_shift(mine_ref, theirs_ref):
    num = mine_ref[0:1, :] + theirs_ref[0:1, :]
    den = mine_ref[1:2, :] + theirs_ref[1:2, :]
    return jnp.where(den > 0, num / jnp.where(den > 0, den, 1.0), 0.0)


def choose_order(map_ref, rel_ref, arrived_ref, order_ref):
    chan, dests = rel_ref.shape
    for k in range(chan):
        for b in range(dests):
            rel_ref[k, b] = map_ref[k, b]

    def uses(first, source):
        total = jnp.int32(0)
        for k in range(chan):
            for b in range(first, first + dests):
                total = total + jnp.where(map_ref[k, b] == source, 1, 0)
        return total

    swap_mine = uses(dests, 0) < uses(dests, 1)
    swap_theirs = uses(0, dests) < uses(0, dests + 1)
    order_ref[0] = jnp.where(swap_mine, 1, 0)
    order_ref[1] = jnp.where(swap_mine, 0, 1)
    for k in range(chan):
        for b in range(dests):
            source = rel_ref[k, b]
            other = 2 * dests + 1 - source
            arrived_ref[k, b] = jnp.where(swap_theirs & (source >= dests), other, source)


def cut(b, x_ref, out_ref):
    out_ref[0] = x_ref[b]


def first_local(
    map_ref, odd_ref, kron_ref, x_ref, left_ref, right_ref,
    right_t_ref, image_ref, sums_ref, crossing_ref, inside_ref, rel_ref, arrived_ref, order_ref,
    turned_ref, mixed_ref, *lists,
):
    choose_order(map_ref, rel_ref, arrived_ref, order_ref)
    chan, dests = left_ref.shape[:2]

    def turn(n, carry):
        for k in range(2):
            for b in range(dests):
                one_left, one_right = left_ref[2 * n + k, b], right_ref[2 * n + k, b]
                right_t_ref[2 * n + k, b] = one_right.T
                crossing_ref[2 * n + k, b] = jnp.where(odd_ref[0] == 1, one_left, one_right)
                inside_ref[2 * n + k, b] = jnp.where(odd_ref[0] == 1, one_right, one_left)
        return carry

    lax.fori_loop(0, chan // 2, turn, 0)
    image_ref[...] = jnp.zeros_like(image_ref)
    steps = list_pairs(rel_ref, 0, dests, *lists)
    add_pairs(steps, lists, kron_ref, x_ref, left_ref, right_t_ref, image_ref, turned_ref, mixed_ref)

    def sums(b, r, start, carry):
        x = x_ref[b, r, :].astype(F32)
        return carry[0] + fold(x * image_ref[b, r, :]), carry[1] + fold(x * x)

    totals = row_loop(dests, x_ref.shape[1], sums, 2)
    sums_ref[...] = jnp.zeros_like(sums_ref)
    put_sums(sums_ref, totals)


def remote_sources(
    rel_ref, kron_ref, other_ref, left_ref, right_t_ref, before_ref,
    acc_ref,
    turned_ref, mixed_ref, *lists,
):
    dests = left_ref.shape[1]
    steps = list_pairs(rel_ref, dests, dests + 1, *lists)
    add_pairs(steps, lists, kron_ref, other_ref, left_ref, right_t_ref, acc_ref, turned_ref, mixed_ref)


def first_remote(
    rel_ref, kron_ref, other_ref, left_ref, right_t_ref, before_ref, local_sums_ref,
    acc_ref, sums_ref,
    turned_ref, mixed_ref, *lists,
):
    dests = left_ref.shape[1]
    sums_ref[...] = local_sums_ref[...]
    steps = list_pairs(rel_ref, dests, dests + 1, *lists)
    add_pairs(steps, lists, kron_ref, other_ref, left_ref, right_t_ref, acc_ref, turned_ref, mixed_ref)


def first_finish(
    turn, rel_ref, order_ref, kron_ref, other_ref, left_ref, right_t_ref, before_ref, x_ref,
    mine_ref, theirs_ref, *refs,
):
    dests, rows = x_ref.shape[:2]
    dest = order_ref[turn]
    last = turn == dests - 1
    if last:
        earlier_ref, acc_ref, guess_ref, all_ref = refs[:4]
        all_ref[order_ref[0]] = earlier_ref[0]
    else:
        acc_ref, guess_ref = refs[:2]
    turned_ref, mixed_ref = refs[-6:-4]
    lists = refs[-4:]
    steps = list_pairs(rel_ref, dests + 1, 2 * dests, *lists, only=(dest,))
    add_pairs(steps, lists, kron_ref, other_ref, left_ref, right_t_ref, acc_ref, turned_ref, mixed_ref)
    shift = common_shift(mine_ref, theirs_ref)
    keep_state = jnp.tile(1.0 + STEP_SIZE * shift, (1, x_ref.shape[2] // LANES))

    def update(b, r, start, carry):
        x = x_ref[b, r, :].astype(F32)
        guess = (keep_state * x - STEP_SIZE * acc_ref[b, r, :]).astype(BF16)
        guess_ref[0, r, :] = guess
        if last:
            all_ref[b, r, :] = guess
        return carry

    row_loop(1, rows, update, 0, first=dest)


def second_local(
    rel_ref, rank_ref, kron_ref, guess_ref, left_ref, right_t_ref, x_ref, image_ref,
    acc_ref, sums_ref,
    turned_ref, mixed_ref, *lists,
):
    dests, rows, _ = x_ref.shape
    acc_ref[...] = jnp.zeros_like(acc_ref)
    steps = list_pairs(rel_ref, 0, dests, *lists)
    add_pairs(steps, lists, kron_ref, guess_ref, left_ref, right_t_ref, acc_ref, turned_ref, mixed_ref)

    def sums(b, r, start, carry):
        x = x_ref[b, r, :].astype(F32)
        guess = guess_ref[b, r, :].astype(F32)
        image = image_ref[b, r, :]
        keep = kept_rows(rank_ref[b], start)
        xx, xg, gg = fold(x * x), fold(x * guess), fold(guess * guess)
        new = (fold(x * image), xx, fold(guess * image), xg, gg, keep * gg, keep * xx, keep * xg)
        return tuple(total + value for total, value in zip(carry, new))

    put_sums(sums_ref, row_loop(dests, rows, sums, 8))


def second_finish(
    rel_ref, rank_ref, kron_ref, other_ref, left_ref, right_t_ref, before_ref, x_ref, guess_ref,
    mine_ref, theirs_ref, early_ref,
    kept_ref, sums_ref,
    turned_ref, mixed_ref, *lists,
):
    dests, rows, width = x_ref.shape
    steps = list_pairs(rel_ref, dests + 1, 2 * dests, *lists)
    add_pairs(steps, lists, kron_ref, other_ref, left_ref, right_t_ref, kept_ref, turned_ref, mixed_ref)
    shift = common_shift(mine_ref, theirs_ref)
    keep_guess = jnp.tile(1.0 + STEP_SIZE * shift, (1, width // LANES))

    def sums(b, r, start, carry):
        x = x_ref[b, r, :].astype(F32)
        guess = guess_ref[b, r, :].astype(F32)
        kept = keep_guess * guess - STEP_SIZE * kept_ref[b, r, :]
        kept_ref[b, r, :] = kept
        keep = kept_rows(rank_ref[b], start)
        kg, kx = fold(kept * guess), fold(kept * x)
        new = (kg, kx, keep * kg, keep * kx, keep * fold(kept * kept))
        return tuple(total + value for total, value in zip(carry, new))

    totals = row_loop(dests, rows, sums, 5)
    sums_ref[0:8, :] = early_ref[...]
    put_sums(sums_ref, totals, first=8)
    sums_ref[13:16, :] = jnp.zeros((3, LANES), F32)


def normalize(
    cells, rank_ref, kept_ref, guess_ref, x_ref, mine_ref, theirs_ref, my_sums_ref, their_sums_ref,
    both_ref,
):
    both = my_sums_ref[...] + their_sums_ref[...]
    xv, xx, gv, xg, gg, gg_kept, xx_kept, xg_kept, kg, kx, kg_kept, kx_kept, kk_kept = (
        both[n : n + 1] for n in range(13)
    )
    shift = common_shift(mine_ref, theirs_ref)
    delta = STEP_SIZE * (xv / xx - shift)
    scale = (1.0 + STEP_SIZE * shift) / STEP_SIZE
    gw, xw = scale * gg - kg / STEP_SIZE, scale * xg - kx / STEP_SIZE
    num = gw + delta * (xw + gv + delta * xv)
    den = gg + delta * (2.0 * xg + delta * xx)
    beta = STEP_SIZE * (num / den - shift)
    of_guess, of_state = beta + delta, beta * delta
    norm = (
        kk_kept
        + of_guess * (2.0 * kg_kept + of_guess * gg_kept)
        + of_state * (2.0 * kx_kept + of_state * xx_kept + 2.0 * of_guess * xg_kept)
    )
    gain = jnp.sqrt(cells / (jnp.maximum(norm, 0.0) + EPSILON))
    blocks, rows, width = kept_ref.shape
    group = 8 * LANES
    per = width // group
    row = lax.broadcasted_iota(jnp.int32, (rows, LANES), 0)

    def one(n, carry):
        b = n // per
        factor = jnp.where(row < rank_ref[b], gain, 0.0)
        for p in range(8):
            cols = pl.ds(pl.multiple_of(lax.rem(n, per) * group + p * LANES, LANES), LANES)
            kept = (
                kept_ref[b, :, cols]
                + of_guess * guess_ref[b, :, cols].astype(F32)
                + of_state * x_ref[b, :, cols].astype(F32)
            )
            state = (kept * factor).astype(BF16)
            both_ref[0, b, :, cols] = state
            both_ref[1, b, :, cols] = state.T
        return carry

    lax.fori_loop(0, blocks * per, one, 0)


def environments(
    first, counts, scale, use_left, env_ref, both_ref, out_ref, mid_ref
):
    _, dests, rows, width = both_ref.shape
    phys = width // LANES
    inner = jnp.where(use_left, 0, 1)

    def step(begin, pairs):
        for j in range(pairs):
            k = first + begin + 2 * j
            for b in range(dests):
                env = jnp.concatenate([env_ref[k, b], env_ref[k + 1, b]], axis=0)
                mid = dot(env, both_ref[inner, b]).astype(BF16)
                for p in range(phys):
                    for i in range(2):
                        mid_ref[
                            j * dests + b, p * rows : (p + 1) * rows, i * LANES : (i + 1) * LANES
                        ] = mid[i * rows : (i + 1) * rows, p * LANES : (p + 1) * LANES]
        for j in range(pairs):
            k = begin + 2 * j
            for b in range(dests):
                out = (dot(both_ref[1 - inner, b], mid_ref[j * dests + b]) * scale).astype(BF16)
                out_ref[k, b] = out[:, :LANES]
                out_ref[k + 1, b] = out[:, LANES:]

    begin = 0
    for pairs, passes in counts:

        def one(n, carry, begin=begin, pairs=pairs):
            step(begin + 2 * pairs * n, pairs)
            return carry

        lax.fori_loop(0, passes, one, 0)
        begin += 2 * pairs * passes


def normalize_and_cross(
    counts, scale, cells,
    odd_ref, rank_ref, kept_ref, guess_ref, x_ref, mine_ref, theirs_ref, my_sums_ref,
    their_sums_ref, env_ref,
    new_ref, both_ref, out_ref,
    mid_ref, sem,
):
    normalize(
        cells, rank_ref, kept_ref, guess_ref, x_ref, mine_ref, theirs_ref, my_sums_ref,
        their_sums_ref, both_ref,
    )
    copy = pltpu.make_async_copy(both_ref.at[0], new_ref, sem)
    copy.start()
    environments(0, counts, scale, odd_ref[0] == 1, env_ref, both_ref, out_ref, mid_ref)
    copy.wait()


def cross(first, counts, scale, odd_ref, env_ref, both_ref, out_ref, mid_ref):
    environments(first, counts, scale, odd_ref[0] == 1, env_ref, both_ref, out_ref, mid_ref)


def within(counts, scale, odd_ref, env_ref, both_ref, *refs):
    outs, all_ref, mid_ref = refs[:-2], refs[-2], refs[-1]
    environments(0, counts, scale, odd_ref[0] == 0, env_ref, both_ref, all_ref, mid_ref)
    begin = 0
    for out_ref in outs:
        count = out_ref.shape[0]
        out_ref[...] = all_ref[begin : begin + count]
        begin += count


def widen(begins, crossed, odd_ref, *refs):
    pieces, (outs, wide_ref, sems) = refs[: len(begins)], (refs[-4:-2], refs[-2], refs[-1])
    to_right = odd_ref[0] == (1 if crossed else 0)
    copies = []
    for piece, begin in zip(pieces, begins):
        for n in range(piece.shape[0]):
            place = begin + n
            wide_ref[place] = piece[n].astype(F32)
            pair = [
                pltpu.make_async_copy(wide_ref.at[place], out.at[place], sems.at[place])
                for out in outs
            ]
            pl.when(jnp.logical_not(to_right))(pair[0].start)
            pl.when(to_right)(pair[1].start)
            copies.append(pair)
    for pair in copies:
        pl.when(jnp.logical_not(to_right))(pair[0].wait)
        pl.when(to_right)(pair[1].wait)


def shards(state, left_env, right_env, site_ops, sector_map, ranks):
    dests, rows, width = state.shape[1:]
    chan, phys = site_ops.shape[1:3]
    groups = lax.axis_size("blk")
    total_blocks = groups * dests
    first_block = lax.axis_index("blk") * dests
    x, left, right, ops = state[0], left_env[0], right_env[0], site_ops[0]

    twice = jnp.concatenate([sector_map[0]] * 2, axis=1)
    turned_map = lax.dynamic_slice_in_dim(twice, first_block, total_blocks, 1)
    turned_map = lax.rem(turned_map - first_block + total_blocks, total_blocks)

    swap = [(g, groups - 1 - g) for g in range(groups)]

    def trade(value):
        return lax.ppermute(value, "blk", swap)

    def shape(dims, kind):
        return jax.ShapeDtypeStruct(dims, kind)

    wave = (dests, rows, width)
    wave_f32 = shape(wave, F32)
    wave_b16 = shape(wave, BF16)
    sums_kind = shape((8, LANES), F32)
    lists = [pltpu.SMEM((chan * dests + 2 * dests * dests + 1,), jnp.int32)] * 4
    pair_scratch = [
        pltpu.VMEM((2, rows // GROUP, phys * GROUP, LANES), BF16),
        pltpu.VMEM((2 * rows, width), BF16),
    ] + lists

    def call(body, specs, outs, scratch, *args, aliases={}, out_specs=None):
        return pl.pallas_call(
            body,
            in_specs=specs,
            out_specs=out_specs or jax.tree.map(lambda _: VMEM, outs),
            out_shape=outs,
            scratch_shapes=scratch,
            compiler_params=PARAMS,
            cost_estimate=COST,
            input_output_aliases=aliases,
        )(*args)

    block = shape((1, rows, width), BF16)
    own = [call(functools.partial(cut, b), [VMEM], block, [], x) for b in range(dests)]
    other = [trade(value) for value in own]
    kron = call(
        make_kron, [VMEM], shape((chan, phys * GROUP, phys * GROUP), BF16),
        [pltpu.VMEM((chan * phys, phys * GROUP), F32)], ops,
    )
    rel_kind = shape((chan, dests), jnp.int32)
    odd = jnp.full((1,), lax.rem(lax.axis_index("seg"), 2), jnp.int32)
    envs = shape(right.shape, BF16)
    right_t, image, mine, crossing, inner, rel, arrived, order = call(
        first_local, [SMEM] * 2 + [VMEM] * 4,
        (envs, wave_f32, sums_kind, envs, envs, rel_kind, rel_kind, shape((dests,), jnp.int32)),
        pair_scratch, turned_map, odd, kron, x, left, right,
        out_specs=(VMEM,) * 5 + (SMEM,) * 3,
    )
    image, mine = call(
        first_remote, [SMEM] + [VMEM] * 6, (wave_f32, sums_kind), pair_scratch,
        rel, kron, other[0], left, right_t, image, mine, aliases={5: 0},
    )
    theirs = trade(mine)
    image, first_guess = call(
        functools.partial(first_finish, 0), [SMEM] * 2 + [VMEM] * 8,
        (wave_f32, block), pair_scratch,
        rel, order, kron, other[1], left, right_t, image, x, mine, theirs, aliases={6: 0},
    )
    image, last_guess, guess = call(
        functools.partial(first_finish, 1), [SMEM] * 2 + [VMEM] * 9,
        (wave_f32, block, wave_b16), pair_scratch,
        rel, order, kron, other[1], left, right_t, image, x, mine, theirs, first_guess,
        aliases={6: 0},
    )
    other = [trade(first_guess), trade(last_guess)]
    acc, early_sums = call(
        second_local, [SMEM] * 2 + [VMEM] * 6, (wave_f32, sums_kind), pair_scratch,
        arrived, ranks[0], kron, guess, left, right_t, x, image,
    )
    acc = call(
        remote_sources, [SMEM] + [VMEM] * 5, wave_f32, pair_scratch,
        arrived, kron, other[0], left, right_t, acc, aliases={5: 0},
    )
    kept, my_sums = call(
        second_finish, [SMEM] * 2 + [VMEM] * 10, (wave_f32, shape((16, LANES), F32)), pair_scratch,
        arrived, ranks[0], kron, other[1], left, right_t, acc, x, guess, mine, theirs, early_sums,
        aliases={6: 0},
    )
    their_sums = trade(my_sums)

    env_scale = 1.0 / math.sqrt(phys * rows)
    cells = float(total_blocks * rows * width)
    early = 8
    count = lax.axis_size("seg")

    def swapped(value, low):
        pairs = [(s, s + 1) for s in range(low, count - 1, 2)]
        return lax.ppermute(value, "seg", pairs + [(t, s) for s, t in pairs])

    def env_kind(number):
        return shape((number,) + left.shape[1:], BF16)

    def mid(pairs):
        return [pltpu.VMEM((pairs * dests, width, 2 * LANES), BF16)]

    new_state, both, piece = call(
        functools.partial(normalize_and_cross, ((2, 2),), env_scale, cells),
        [SMEM] * 2 + [VMEM] * 8, (wave_b16, shape((2,) + wave, BF16), env_kind(early)),
        mid(2) + [pltpu.SemaphoreType.DMA],
        odd, ranks[0], kept, guess, x, mine, theirs, my_sums, their_sums, crossing,
        out_specs=(HBM, VMEM, VMEM),
    )
    rest = call(
        functools.partial(cross, early, ((3, 1),), env_scale),
        [SMEM] + [VMEM] * 2, env_kind(chan - early), mid(3), odd, crossing, both,
    )
    sizes = (5, 5, 4)
    inside = call(
        functools.partial(within, ((2, 3), (1, 1)), env_scale),
        [SMEM] + [VMEM] * 2, tuple(env_kind(size) for size in sizes),
        [pltpu.VMEM(left.shape, BF16)] + mid(2), odd, inner, both,
    )
    piece, rest = swapped(piece, 1), swapped(rest, 1)
    inside = [swapped(value, 0) for value in inside]
    env_f32 = shape(left.shape, F32)

    def widened(begins, crossed, values, filled):
        number = 1 + len(values)
        return call(
            functools.partial(widen, begins, crossed),
            [SMEM] + [VMEM] * len(values) + [HBM] * len(filled), (env_f32, env_f32),
            [pltpu.VMEM(left.shape, F32), pltpu.SemaphoreType.DMA((chan,))],
            odd, *values, *filled,
            aliases={number + n: n for n in range(len(filled))}, out_specs=(HBM, HBM),
        )

    filled = widened((0,), True, [piece], ())
    filled = widened((0, sizes[0], sizes[0] + sizes[1]), False, inside, filled)
    received_left, received_right = widened((early,), True, [rest], filled)
    return (new_state[None], received_left[None], received_right[None])


def solution(mesh):
    placed = (
        P("seg", "blk", None, None),
        P("seg", None, "blk", None, None),
        P("seg", None, "blk", None, None),
        P("seg", None, None, None),
        P("seg", None, None),
        P("seg", "blk"),
    )
    return jax.shard_map(
        shards,
        mesh=mesh,
        in_specs=placed,
        out_specs=(
            P("seg", "blk", None, None),
            P("seg", None, "blk", None, None),
            P("seg", None, "blk", None, None),
        ),
        check_vma=False,
    )
```

```python
import functools
import math

import jax
import jax.numpy as jnp
from jax import lax
from jax.experimental import pallas as pl
from jax.experimental.pallas import tpu as pltpu
from jax.sharding import PartitionSpec as P

STEP_SIZE = 0.25
EPSILON = 1e-06
LANES = 128
GROUP = 8
CHUNK = 32
F32 = jnp.float32
BF16 = jnp.bfloat16
VMEM = pl.BlockSpec(memory_space=pltpu.VMEM)
HBM = pl.BlockSpec(memory_space=pltpu.HBM)
SMEM = pl.BlockSpec(memory_space=pltpu.SMEM)
COST = pl.CostEstimate(flops=1024, bytes_accessed=1024, transcendentals=0)
PARAMS = pltpu.CompilerParams(vmem_limit_bytes=20 * 1024 * 1024)


def dot(left, right):
    return lax.dot_general(
        left, right, (((1,), (0,)), ((), ())), preferred_element_type=F32
    )


def make_kron(ops_ref, kron_ref, spread_ref):
    chan, phys, _ = ops_ref.shape
    wide = phys * GROUP
    columns = lax.broadcasted_iota(jnp.int32, (phys, wide), 1)
    spread = (columns // GROUP == lax.broadcasted_iota(jnp.int32, (phys, wide), 0)).astype(F32)
    spread_ref[...] = dot(ops_ref[...].reshape(chan * phys, phys), spread.astype(BF16))
    same = lax.broadcasted_iota(jnp.int32, (GROUP, wide), 1) % GROUP == lax.broadcasted_iota(
        jnp.int32, (GROUP, wide), 0
    )

    def one(k, carry):
        rows = spread_ref[pl.ds(pl.multiple_of(k * phys, phys), phys), :]
        full = [
            jnp.where(same, jnp.broadcast_to(rows[p : p + 1], (GROUP, wide)), 0.0)
            for p in range(phys)
        ]
        kron_ref[k] = jnp.concatenate(full, axis=0).astype(BF16)
        return carry

    lax.fori_loop(0, chan, one, 0)


def list_pairs(rel_ref, low, high, chan_list, src_list, live_list, dest_list, only=None):
    chan, dests = rel_ref.shape
    place = jnp.int32(0)
    for b in range(dests) if only is None else only:
        for source in range(low, high):
            for k in range(chan):
                chan_list[place] = k
                src_list[place] = source - low
                live_list[place] = 1
                dest_list[place] = b
                place = place + jnp.where(rel_ref[k, b] == source, 1, 0)
            chan_list[place] = 0
            src_list[place] = source - low
            live_list[place] = 0
            dest_list[place] = b
            place = place + lax.rem(place, 2)
    return place // 2


def add_pairs(
    steps, lists, kron_ref, x_ref, left_ref, right_t_ref, acc_ref, turned_ref, mixed_ref, start=0
):
    chan_list, src_list, live_list, dest_list = lists
    rows = x_ref.shape[1]
    phys = x_ref.shape[2] // LANES
    groups = rows // GROUP

    def lanes(n):
        return slice(n * LANES, (n + 1) * LANES)

    def act_right(s):
        source, dest = src_list[2 * s], dest_list[2 * s]
        tall = jnp.concatenate([x_ref[source, :, lanes(q)] for q in range(phys)], axis=0)
        second = right_t_ref[chan_list[2 * s + 1], dest]
        second = jnp.where(live_list[2 * s + 1] > 0, second, jnp.zeros_like(second))
        out = dot(tall, jnp.concatenate([right_t_ref[chan_list[2 * s], dest], second], axis=1))
        for i in range(2):
            for g in range(groups):
                turned_ref[i, g] = jnp.concatenate(
                    [
                        out[q * rows + g * GROUP : q * rows + (g + 1) * GROUP, lanes(i)]
                        for q in range(phys)
                    ],
                    axis=0,
                ).astype(BF16)

    def act_site(s):
        for i in range(2):
            kron = kron_ref[chan_list[2 * s + i]]
            for h in range(groups // 2):
                both = jnp.concatenate([turned_ref[i, 2 * h], turned_ref[i, 2 * h + 1]], axis=1)
                out = dot(kron, both)
                r0 = i * rows + 2 * h * GROUP
                for p in range(phys):
                    row = slice(p * GROUP, (p + 1) * GROUP)
                    mixed_ref[r0 : r0 + 2 * GROUP, lanes(p)] = jnp.concatenate(
                        [out[row, lanes(0)], out[row, lanes(1)]], axis=0
                    ).astype(BF16)

    def act_left(s):
        dest = dest_list[2 * s]
        left = jnp.concatenate(
            [left_ref[chan_list[2 * s + i], dest][:, start : start + rows] for i in range(2)], axis=1
        )
        acc_ref[dest] += dot(left, mixed_ref[0 : 2 * rows, :])

    def middle(s, carry):
        act_site(s)
        act_right(s + 1)
        act_left(s)
        return carry

    @pl.when(steps > 0)
    def _():
        act_right(0)
        lax.fori_loop(0, steps - 1, middle, 0)
        act_site(steps - 1)
        act_left(steps - 1)


def fold(values):
    total = values[:, :LANES]
    for p in range(1, values.shape[1] // LANES):
        total = total + values[:, p * LANES : (p + 1) * LANES]
    return total


def row_loop(blocks, rows, body, count, first=0):
    zeros = tuple(jnp.zeros((CHUNK, LANES), F32) for _ in range(count))
    per = rows // CHUNK

    def step(n, carry):
        start = pl.multiple_of(lax.rem(n, per) * CHUNK, CHUNK)
        return body(first + n // per, pl.ds(start, CHUNK), start, carry)

    return lax.fori_loop(0, blocks * per, step, zeros)


def kept_rows(rank, start):
    row = start + lax.broadcasted_iota(jnp.int32, (CHUNK, LANES), 0)
    return (row < rank).astype(F32)


def put_sums(out_ref, values, first=0):
    for n, value in enumerate(values):
        out_ref[first + n : first + n + 1, :] = jnp.full((1, LANES), 1.0, F32) * jnp.sum(value)


def common_shift(mine_ref, theirs_ref):
    num = mine_ref[0:1, :] + theirs_ref[0:1, :]
    den = mine_ref[1:2, :] + theirs_ref[1:2, :]
    return jnp.where(den > 0, num / jnp.where(den > 0, den, 1.0), 0.0)


def choose_order(map_ref, rel_ref, arrived_ref, order_ref):
    chan, dests = rel_ref.shape
    for k in range(chan):
        for b in range(dests):
            rel_ref[k, b] = map_ref[k, b]

    def uses(first, source):
        total = jnp.int32(0)
        for k in range(chan):
            for b in range(first, first + dests):
                total = total + jnp.where(map_ref[k, b] == source, 1, 0)
        return total

    swap_mine = uses(dests, 0) < uses(dests, 1)
    swap_theirs = uses(0, dests) < uses(0, dests + 1)
    order_ref[0] = jnp.where(swap_mine, 1, 0)
    order_ref[1] = jnp.where(swap_mine, 0, 1)
    for k in range(chan):
        for b in range(dests):
            source = rel_ref[k, b]
            other = 2 * dests + 1 - source
            arrived_ref[k, b] = jnp.where(swap_theirs & (source >= dests), other, source)


def cut(b, x_ref, out_ref):
    out_ref[0] = x_ref[b]


def first_local(
    map_ref, odd_ref, kron_ref, x_ref, left_ref, right_ref,
    right_t_ref, image_ref, sums_ref, crossing_ref, inside_ref, rel_ref, arrived_ref, order_ref,
    turned_ref, mixed_ref, *lists,
):
    choose_order(map_ref, rel_ref, arrived_ref, order_ref)
    chan, dests = left_ref.shape[:2]

    def turn(n, carry):
        for k in range(2):
            for b in range(dests):
                one_left, one_right = left_ref[2 * n + k, b], right_ref[2 * n + k, b]
                right_t_ref[2 * n + k, b] = one_right.T
                crossing_ref[2 * n + k, b] = jnp.where(odd_ref[0] == 1, one_left, one_right)
                inside_ref[2 * n + k, b] = jnp.where(odd_ref[0] == 1, one_right, one_left)
        return carry

    lax.fori_loop(0, chan // 2, turn, 0)
    image_ref[...] = jnp.zeros_like(image_ref)
    steps = list_pairs(rel_ref, 0, dests, *lists)
    add_pairs(steps, lists, kron_ref, x_ref, left_ref, right_t_ref, image_ref, turned_ref, mixed_ref)

    def sums(b, r, start, carry):
        x = x_ref[b, r, :].astype(F32)
        return carry[0] + fold(x * image_ref[b, r, :]), carry[1] + fold(x * x)

    totals = row_loop(dests, x_ref.shape[1], sums, 2)
    sums_ref[...] = jnp.zeros_like(sums_ref)
    put_sums(sums_ref, totals)


def remote_sources(
    block, rel_ref, kron_ref, other_ref, left_ref, right_t_ref, before_ref,
    acc_ref,
    turned_ref, mixed_ref, *lists,
):
    dests = left_ref.shape[1]
    steps = list_pairs(rel_ref, dests + block, dests + block + 1, *lists)
    add_pairs(steps, lists, kron_ref, other_ref, left_ref, right_t_ref, acc_ref, turned_ref, mixed_ref)


def first_remote(
    rel_ref, kron_ref, other_ref, left_ref, right_t_ref, before_ref, local_sums_ref,
    acc_ref, sums_ref,
    turned_ref, mixed_ref, *lists,
):
    dests = left_ref.shape[1]
    sums_ref[...] = local_sums_ref[...]
    steps = list_pairs(rel_ref, dests, dests + 1, *lists)
    add_pairs(steps, lists, kron_ref, other_ref, left_ref, right_t_ref, acc_ref, turned_ref, mixed_ref)


def first_finish(
    turn, rel_ref, order_ref, kron_ref, other_ref, left_ref, right_t_ref, before_ref, x_ref,
    mine_ref, theirs_ref, *refs,
):
    dests, rows = x_ref.shape[:2]
    dest = order_ref[turn]
    last = turn == dests - 1
    if last:
        earlier_ref, acc_ref, head_ref, tail_ref, all_ref = refs[:5]
        all_ref[order_ref[0]] = earlier_ref[0]
    else:
        acc_ref, guess_ref = refs[:2]
    turned_ref, mixed_ref = refs[-6:-4]
    lists = refs[-4:]
    steps = list_pairs(rel_ref, dests + 1, 2 * dests, *lists, only=(dest,))
    add_pairs(steps, lists, kron_ref, other_ref, left_ref, right_t_ref, acc_ref, turned_ref, mixed_ref)
    shift = common_shift(mine_ref, theirs_ref)
    keep_state = jnp.tile(1.0 + STEP_SIZE * shift, (1, x_ref.shape[2] // LANES))

    def update(b, r, start, carry):
        x = x_ref[b, r, :].astype(F32)
        guess = (keep_state * x - STEP_SIZE * acc_ref[b, r, :]).astype(BF16)
        if last:
            all_ref[b, r, :] = guess
        else:
            guess_ref[0, r, :] = guess
        return carry

    row_loop(1, rows, update, 0, first=dest)
    if last:
        split = head_ref.shape[1]
        head_ref[0] = all_ref[dest, 0:split]
        tail_ref[0] = all_ref[dest, split:rows]


def second_local(
    rel_ref, rank_ref, kron_ref, guess_ref, left_ref, right_t_ref, x_ref, image_ref,
    acc_ref, sums_ref,
    turned_ref, mixed_ref, *lists,
):
    dests, rows, _ = x_ref.shape
    acc_ref[...] = jnp.zeros_like(acc_ref)
    steps = list_pairs(rel_ref, 0, dests, *lists)
    add_pairs(steps, lists, kron_ref, guess_ref, left_ref, right_t_ref, acc_ref, turned_ref, mixed_ref)

    def sums(b, r, start, carry):
        x = x_ref[b, r, :].astype(F32)
        guess = guess_ref[b, r, :].astype(F32)
        image = image_ref[b, r, :]
        keep = kept_rows(rank_ref[b], start)
        xx, xg, gg = fold(x * x), fold(x * guess), fold(guess * guess)
        new = (fold(x * image), xx, fold(guess * image), xg, gg, keep * gg, keep * xx, keep * xg)
        return tuple(total + value for total, value in zip(carry, new))

    put_sums(sums_ref, row_loop(dests, rows, sums, 8))


def second_finish(
    rel_ref, rank_ref, kron_ref, other_ref, left_ref, right_t_ref, before_ref, x_ref, guess_ref,
    mine_ref, theirs_ref, early_ref,
    kept_ref, sums_ref,
    turned_ref, mixed_ref, *lists,
):
    dests, rows, width = x_ref.shape
    steps = list_pairs(rel_ref, dests + 1, 2 * dests, *lists)
    add_pairs(
        steps, lists, kron_ref, other_ref, left_ref, right_t_ref, kept_ref, turned_ref, mixed_ref,
        rows - other_ref.shape[1],
    )
    shift = common_shift(mine_ref, theirs_ref)
    keep_guess = jnp.tile(1.0 + STEP_SIZE * shift, (1, width // LANES))

    def sums(b, r, start, carry):
        x = x_ref[b, r, :].astype(F32)
        guess = guess_ref[b, r, :].astype(F32)
        kept = keep_guess * guess - STEP_SIZE * kept_ref[b, r, :]
        kept_ref[b, r, :] = kept
        keep = kept_rows(rank_ref[b], start)
        kg, kx = fold(kept * guess), fold(kept * x)
        new = (kg, kx, keep * kg, keep * kx, keep * fold(kept * kept))
        return tuple(total + value for total, value in zip(carry, new))

    totals = row_loop(dests, rows, sums, 5)
    sums_ref[0:8, :] = early_ref[...]
    put_sums(sums_ref, totals, first=8)
    sums_ref[13:16, :] = jnp.zeros((3, LANES), F32)


def normalize(
    cells, rank_ref, kept_ref, guess_ref, x_ref, mine_ref, theirs_ref, my_sums_ref, their_sums_ref,
    both_ref,
):
    both = my_sums_ref[...] + their_sums_ref[...]
    xv, xx, gv, xg, gg, gg_kept, xx_kept, xg_kept, kg, kx, kg_kept, kx_kept, kk_kept = (
        both[n : n + 1] for n in range(13)
    )
    shift = common_shift(mine_ref, theirs_ref)
    delta = STEP_SIZE * (xv / xx - shift)
    scale = (1.0 + STEP_SIZE * shift) / STEP_SIZE
    gw, xw = scale * gg - kg / STEP_SIZE, scale * xg - kx / STEP_SIZE
    num = gw + delta * (xw + gv + delta * xv)
    den = gg + delta * (2.0 * xg + delta * xx)
    beta = STEP_SIZE * (num / den - shift)
    of_guess, of_state = beta + delta, beta * delta
    norm = (
        kk_kept
        + of_guess * (2.0 * kg_kept + of_guess * gg_kept)
        + of_state * (2.0 * kx_kept + of_state * xx_kept + 2.0 * of_guess * xg_kept)
    )
    gain = jnp.sqrt(cells / (jnp.maximum(norm, 0.0) + EPSILON))
    blocks, rows, width = kept_ref.shape
    group = 8 * LANES
    per = width // group
    row = lax.broadcasted_iota(jnp.int32, (rows, LANES), 0)

    def one(n, carry):
        b = n // per
        factor = jnp.where(row < rank_ref[b], gain, 0.0)
        for p in range(8):
            cols = pl.ds(pl.multiple_of(lax.rem(n, per) * group + p * LANES, LANES), LANES)
            kept = (
                kept_ref[b, :, cols]
                + of_guess * guess_ref[b, :, cols].astype(F32)
                + of_state * x_ref[b, :, cols].astype(F32)
            )
            state = (kept * factor).astype(BF16)
            both_ref[0, b, :, cols] = state
            both_ref[1, b, :, cols] = state.T
        return carry

    lax.fori_loop(0, blocks * per, one, 0)


def environments(
    first, counts, scale, use_left, env_ref, both_ref, out_ref, mid_ref
):
    _, dests, rows, width = both_ref.shape
    phys = width // LANES
    inner = jnp.where(use_left, 0, 1)

    def step(begin, pairs):
        for j in range(pairs):
            k = first + begin + 2 * j
            for b in range(dests):
                env = jnp.concatenate([env_ref[k, b], env_ref[k + 1, b]], axis=0)
                mid = dot(env, both_ref[inner, b]).astype(BF16)
                for p in range(phys):
                    for i in range(2):
                        mid_ref[
                            j * dests + b, p * rows : (p + 1) * rows, i * LANES : (i + 1) * LANES
                        ] = mid[i * rows : (i + 1) * rows, p * LANES : (p + 1) * LANES]
        for j in range(pairs):
            k = begin + 2 * j
            for b in range(dests):
                out = (dot(both_ref[1 - inner, b], mid_ref[j * dests + b]) * scale).astype(BF16)
                out_ref[k, b] = out[:, :LANES]
                out_ref[k + 1, b] = out[:, LANES:]

    begin = 0
    for pairs, passes in counts:

        def one(n, carry, begin=begin, pairs=pairs):
            step(begin + 2 * pairs * n, pairs)
            return carry

        lax.fori_loop(0, passes, one, 0)
        begin += 2 * pairs * passes


def normalize_and_cross(
    counts, scale, cells,
    odd_ref, rank_ref, kept_ref, guess_ref, x_ref, mine_ref, theirs_ref, my_sums_ref,
    their_sums_ref, env_ref,
    new_ref, both_ref, out_ref,
    mid_ref, sem,
):
    normalize(
        cells, rank_ref, kept_ref, guess_ref, x_ref, mine_ref, theirs_ref, my_sums_ref,
        their_sums_ref, both_ref,
    )
    copy = pltpu.make_async_copy(both_ref.at[0], new_ref, sem)
    copy.start()
    environments(0, counts, scale, odd_ref[0] == 1, env_ref, both_ref, out_ref, mid_ref)
    copy.wait()


def cross(first, counts, scale, odd_ref, env_ref, both_ref, out_ref, mid_ref):
    environments(first, counts, scale, odd_ref[0] == 1, env_ref, both_ref, out_ref, mid_ref)


def within(counts, scale, odd_ref, env_ref, both_ref, *refs):
    outs, all_ref, mid_ref = refs[:-2], refs[-2], refs[-1]
    environments(0, counts, scale, odd_ref[0] == 0, env_ref, both_ref, all_ref, mid_ref)
    begin = 0
    for out_ref in outs:
        count = out_ref.shape[0]
        out_ref[...] = all_ref[begin : begin + count]
        begin += count


def widen(begins, crossed, odd_ref, *refs):
    pieces, (outs, wide_ref, sems) = refs[: len(begins)], (refs[-4:-2], refs[-2], refs[-1])
    to_right = odd_ref[0] == (1 if crossed else 0)
    copies = []
    for piece, begin in zip(pieces, begins):
        for n in range(piece.shape[0]):
            place = begin + n
            wide_ref[place] = piece[n].astype(F32)
            pair = [
                pltpu.make_async_copy(wide_ref.at[place], out.at[place], sems.at[place])
                for out in outs
            ]
            pl.when(jnp.logical_not(to_right))(pair[0].start)
            pl.when(to_right)(pair[1].start)
            copies.append(pair)
    for pair in copies:
        pl.when(jnp.logical_not(to_right))(pair[0].wait)
        pl.when(to_right)(pair[1].wait)


def shards(state, left_env, right_env, site_ops, sector_map, ranks):
    dests, rows, width = state.shape[1:]
    chan, phys = site_ops.shape[1:3]
    groups = lax.axis_size("blk")
    total_blocks = groups * dests
    first_block = lax.axis_index("blk") * dests
    x, left, right, ops = state[0], left_env[0], right_env[0], site_ops[0]

    twice = jnp.concatenate([sector_map[0]] * 2, axis=1)
    turned_map = lax.dynamic_slice_in_dim(twice, first_block, total_blocks, 1)
    turned_map = lax.rem(turned_map - first_block + total_blocks, total_blocks)

    swap = [(g, groups - 1 - g) for g in range(groups)]

    def trade(value):
        return lax.ppermute(value, "blk", swap)

    def shape(dims, kind):
        return jax.ShapeDtypeStruct(dims, kind)

    wave = (dests, rows, width)
    wave_f32 = shape(wave, F32)
    wave_b16 = shape(wave, BF16)
    sums_kind = shape((8, LANES), F32)
    lists = [pltpu.SMEM((chan * dests + 2 * dests * dests + 1,), jnp.int32)] * 4
    pair_scratch = [
        pltpu.VMEM((2, rows // GROUP, phys * GROUP, LANES), BF16),
        pltpu.VMEM((2 * rows, width), BF16),
    ] + lists

    def call(body, specs, outs, scratch, *args, aliases={}, out_specs=None):
        return pl.pallas_call(
            body,
            in_specs=specs,
            out_specs=out_specs or jax.tree.map(lambda _: VMEM, outs),
            out_shape=outs,
            scratch_shapes=scratch,
            compiler_params=PARAMS,
            cost_estimate=COST,
            input_output_aliases=aliases,
        )(*args)

    block = shape((1, rows, width), BF16)
    own = [call(functools.partial(cut, b), [VMEM], block, [], x) for b in range(dests)]
    other = [trade(value) for value in own]
    kron = call(
        make_kron, [VMEM], shape((chan, phys * GROUP, phys * GROUP), BF16),
        [pltpu.VMEM((chan * phys, phys * GROUP), F32)], ops,
    )
    rel_kind = shape((chan, dests), jnp.int32)
    odd = jnp.full((1,), lax.rem(lax.axis_index("seg"), 2), jnp.int32)
    envs = shape(right.shape, BF16)
    right_t, image, mine, crossing, inner, rel, arrived, order = call(
        first_local, [SMEM] * 2 + [VMEM] * 4,
        (envs, wave_f32, sums_kind, envs, envs, rel_kind, rel_kind, shape((dests,), jnp.int32)),
        pair_scratch, turned_map, odd, kron, x, left, right,
        out_specs=(VMEM,) * 5 + (SMEM,) * 3,
    )
    image, mine = call(
        first_remote, [SMEM] + [VMEM] * 6, (wave_f32, sums_kind), pair_scratch,
        rel, kron, other[0], left, right_t, image, mine, aliases={5: 0},
    )
    theirs = trade(mine)
    image, first_guess = call(
        functools.partial(first_finish, 0), [SMEM] * 2 + [VMEM] * 8,
        (wave_f32, block), pair_scratch,
        rel, order, kron, other[1], left, right_t, image, x, mine, theirs, aliases={6: 0},
    )
    split = rows - rows // 4
    image, head, tail, guess = call(
        functools.partial(first_finish, 1), [SMEM] * 2 + [VMEM] * 9,
        (
            wave_f32, shape((1, split, width), BF16), shape((1, rows - split, width), BF16), wave_b16,
        ),
        pair_scratch,
        rel, order, kron, other[1], left, right_t, image, x, mine, theirs, first_guess,
        aliases={6: 0},
    )
    other = [trade(first_guess), trade(head), trade(tail)]
    acc, early_sums = call(
        second_local, [SMEM] * 2 + [VMEM] * 6, (wave_f32, sums_kind), pair_scratch,
        arrived, ranks[0], kron, guess, left, right_t, x, image,
    )
    for n in range(2):
        acc = call(
            functools.partial(remote_sources, n), [SMEM] + [VMEM] * 5, wave_f32, pair_scratch,
            arrived, kron, other[n], left, right_t, acc, aliases={5: 0},
        )
    kept, my_sums = call(
        second_finish, [SMEM] * 2 + [VMEM] * 10, (wave_f32, shape((16, LANES), F32)), pair_scratch,
        arrived, ranks[0], kron, other[2], left, right_t, acc, x, guess, mine, theirs, early_sums,
        aliases={6: 0},
    )
    their_sums = trade(my_sums)

    env_scale = 1.0 / math.sqrt(phys * rows)
    cells = float(total_blocks * rows * width)
    early = 8
    count = lax.axis_size("seg")

    def swapped(value, low):
        pairs = [(s, s + 1) for s in range(low, count - 1, 2)]
        return lax.ppermute(value, "seg", pairs + [(t, s) for s, t in pairs])

    def env_kind(number):
        return shape((number,) + left.shape[1:], BF16)

    def mid(pairs):
        return [pltpu.VMEM((pairs * dests, width, 2 * LANES), BF16)]

    new_state, both, piece = call(
        functools.partial(normalize_and_cross, ((2, 2),), env_scale, cells),
        [SMEM] * 2 + [VMEM] * 8, (wave_b16, shape((2,) + wave, BF16), env_kind(early)),
        mid(2) + [pltpu.SemaphoreType.DMA],
        odd, ranks[0], kept, guess, x, mine, theirs, my_sums, their_sums, crossing,
        out_specs=(HBM, VMEM, VMEM),
    )
    rest = call(
        functools.partial(cross, early, ((3, 1),), env_scale),
        [SMEM] + [VMEM] * 2, env_kind(chan - early), mid(3), odd, crossing, both,
    )
    sizes = (5, 5, 4)
    inside = call(
        functools.partial(within, ((2, 3), (1, 1)), env_scale),
        [SMEM] + [VMEM] * 2, tuple(env_kind(size) for size in sizes),
        [pltpu.VMEM(left.shape, BF16)] + mid(2), odd, inner, both,
    )
    piece, rest = swapped(piece, 1), swapped(rest, 1)
    inside = [swapped(value, 0) for value in inside]
    env_f32 = shape(left.shape, F32)

    def widened(begins, crossed, values, filled):
        number = 1 + len(values)
        return call(
            functools.partial(widen, begins, crossed),
            [SMEM] + [VMEM] * len(values) + [HBM] * len(filled), (env_f32, env_f32),
            [pltpu.VMEM(left.shape, F32), pltpu.SemaphoreType.DMA((chan,))],
            odd, *values, *filled,
            aliases={number + n: n for n in range(len(filled))}, out_specs=(HBM, HBM),
        )

    filled = widened((0,), True, [piece], ())
    filled = widened((0, sizes[0], sizes[0] + sizes[1]), False, inside, filled)
    received_left, received_right = widened((early,), True, [rest], filled)
    return (new_state[None], received_left[None], received_right[None])


def solution(mesh):
    placed = (
        P("seg", "blk", None, None),
        P("seg", None, "blk", None, None),
        P("seg", None, "blk", None, None),
        P("seg", None, None, None),
        P("seg", None, None),
        P("seg", "blk"),
    )
    return jax.shard_map(
        shards,
        mesh=mesh,
        in_specs=placed,
        out_specs=(
            P("seg", "blk", None, None),
            P("seg", None, "blk", None, None),
            P("seg", None, "blk", None, None),
        ),
        check_vma=False,
    )
```
